32 devices in a mesh: view: 4 (over y, core), ctx: 8 (over z, x).
Axes of the slice: x: 2, y: 2, z: 4, core: 2. Of those that a mesh axis runs over, the one named last changes fastest.
Arguments:
- q_self: bfloat16 [4, 896, 1024], P('view', 'ctx'), may hold values from -16 to 16
- k_self: bfloat16 [4, 896, 1024], P('view', 'ctx'), may hold values from -16 to 16
- v_self: bfloat16 [4, 896, 1024], P('view', 'ctx'), may hold values from -6 to 6
- q_cross: bfloat16 [4, 896, 1024], P('view', 'ctx'), may hold values from -16 to 16
- k_cross: bfloat16 [4, 896, 1024], P('view', 'ctx'), may hold values from -16 to 16
- v_cross: bfloat16 [4, 896, 1024], P('view', 'ctx'), may hold values from -6 to 6
Outputs:
- block_out: bfloat16 [4, 896, 1024], P('view', 'ctx')
The draws below stay inside these ranges and needn't reach their ends.
All inputs are finite; a program needn't handle non-finite values.
Results may differ from the reference program's by a relative error of at most 0.01.
Values may be sent and summed in bfloat16 or wider, within the bound.
No kernel may reach another device: no remote copies, remote signals or barrier semaphores. Data moves between devices by JAX's collectives and lax.ppermute only.
A program may use at most 128 MiB of HBM per device.

```python
import jax
import jax.numpy as jnp
from jax import lax

H = 8
HEAD = 128
VIEWS = 4
SEQ = 896
HD = 1024


def background(key, salt, factor):
    values = jnp.clip(jax.random.normal(jax.random.fold_in(key, salt), (VIEWS, SEQ, HD), jnp.float32), -6.0, 6.0)
    return factor * values


def draw_q_self(key, part):
    values = background(key, 11, 2.5)
    return values.astype(jnp.bfloat16)


def draw_k_self(key, part):
    values = background(key, 12, 1.0)
    return values.astype(jnp.bfloat16)


def draw_q_cross(key, part):
    values = background(key, 13, 1.5)
    return values.astype(jnp.bfloat16)


def draw_k_cross(key, part):
    values = background(key, 14, 1.0)
    return values.astype(jnp.bfloat16)


def block_levels(own_key, dims, pieces, low, largest):
    factor_of, own = 1.0, jax.random.fold_in(own_key, 6)
    for axis_at, blocks in pieces:
        steps = jnp.exp(jax.random.uniform(jax.random.fold_in(own, axis_at), (blocks,), jnp.float32, low / len(pieces), largest / len(pieces)))
        factor_of = factor_of * jnp.repeat(steps, dims[axis_at] // blocks).reshape([-1 if axis == axis_at else 1 for axis in range(len(dims))])
    return factor_of


def bell_draw(key, extent, scale, reach, pieces=(), kind=jnp.bfloat16):
    result = scale * jax.random.normal(key, extent, jnp.float32)
    if pieces:
        result = result * block_levels(key, extent, pieces, -0.22, 0.18)
    return jnp.clip(result, -reach, reach).astype(kind)


def setup_inputs(seed: int = 0) -> dict:
    key_of = jax.random.split(jax.random.key(seed), 7)
    return {
        "q_self": draw_q_self(jax.random.fold_in(key_of[6], 71), 0),
        "k_self": draw_k_self(jax.random.fold_in(key_of[6], 71), 0),
        "v_self": bell_draw(key_of[2], (VIEWS, SEQ, HD), 1.0, 6.0, ((0, 4), (1, 8))),
        "q_cross": draw_q_cross(jax.random.fold_in(key_of[6], 71), 0),
        "k_cross": draw_k_cross(jax.random.fold_in(key_of[6], 71), 0),
        "v_cross": bell_draw(key_of[5], (VIEWS, SEQ, HD), 1.0, 6.0, ((0, 4), (1, 8))),
    }


def one_view(arrays):
    queries, key_rows, value_rows = arrays
    score_scale = 1.0 / (HEAD ** 0.5)

    def one_head(head_arrays):
        query_head, key_head, value_head = head_arrays
        scores = jnp.dot(query_head, key_head.T, preferred_element_type=jnp.float32) * score_scale
        row_max = jnp.max(scores, axis=-1, keepdims=True)
        weights_full = jnp.exp(scores - row_max)
        total_weight = jnp.sum(weights_full, axis=-1, keepdims=True)
        weights_raw = weights_full.astype(jnp.bfloat16)
        return jnp.dot(weights_raw, value_head, preferred_element_type=jnp.float32) / total_weight

    split_q = jnp.transpose(queries.reshape(SEQ, H, HEAD), (1, 0, 2))
    split_k = jnp.transpose(key_rows.reshape(SEQ, H, HEAD), (1, 0, 2))
    split_v = jnp.transpose(value_rows.reshape(SEQ, H, HEAD), (1, 0, 2))
    attended = lax.map(one_head, (split_q, split_k, split_v))
    return jnp.transpose(attended, (1, 0, 2)).reshape(SEQ, HD).astype(jnp.bfloat16)


def reference(q_self, k_self, v_self, q_cross, k_cross, v_cross):
    o_self = lax.map(one_view, (q_self, k_self, v_self))
    cross_query = (q_cross.astype(jnp.float32) + o_self.astype(jnp.float32)).astype(jnp.bfloat16)
    score_scale = 1.0 / (HEAD ** 0.5)
    query_four = cross_query.reshape(VIEWS, SEQ, H, HEAD).astype(jnp.float32)
    key_four = k_cross.reshape(VIEWS, SEQ, H, HEAD).astype(jnp.float32)
    value_four = v_cross.reshape(VIEWS, SEQ, H, HEAD).astype(jnp.float32)
    cross_scores = jnp.einsum('atnd,btnd->tnab', query_four, key_four) * score_scale
    cross_scores = cross_scores - jnp.max(cross_scores, axis=-1, keepdims=True)
    weights_full = jnp.exp(cross_scores)
    cross_weights = (weights_full / jnp.sum(weights_full, axis=-1, keepdims=True)).astype(jnp.bfloat16)
    o_cross = jnp.einsum('tnab,btnd->atnd', cross_weights.astype(jnp.float32), value_four).astype(jnp.bfloat16)
    o_cross = o_cross.reshape(VIEWS, SEQ, HD)
    return (o_self.astype(jnp.float32) + o_cross.astype(jnp.float32)).astype(jnp.bfloat16)
```

```python
import functools
import math

import jax
import jax.numpy as jnp
from jax import lax
from jax.experimental import pallas as pl
from jax.experimental.pallas import tpu as pltpu
from jax.sharding import PartitionSpec as P

HEAD = 128
SCALE = 1.0 / math.sqrt(HEAD)
EXP2_SCALE = SCALE * math.log2(math.e)
VMEM_LIMIT = 48 * 1024 * 1024


def pack_kernel(head_count, q_ref, k_ref, v_ref, out_ref):
    rows = q_ref.shape[0]
    for head in range(head_count):
        lanes = slice(head * HEAD, (head + 1) * HEAD)
        out_ref[head, 0:rows, :] = q_ref[:, lanes]
        out_ref[head, rows : 2 * rows, :] = k_ref[:, lanes]
        out_ref[head, 2 * rows : 3 * rows, :] = v_ref[:, lanes]


def attend(query, keys, values):
    scores = lax.dot_general(
        query, keys, (((1,), (1,)), ((), ())), preferred_element_type=jnp.float32
    )
    row_max = jnp.max(scores, axis=-1, keepdims=True)
    weights_full = jnp.exp2((scores - row_max) * EXP2_SCALE)
    total = jnp.sum(weights_full, axis=-1, keepdims=True)
    mixed = jnp.dot(
        weights_full.astype(jnp.bfloat16), values, preferred_element_type=jnp.float32
    )
    return (mixed / total).astype(jnp.bfloat16)


def packed_attention_kernel(rows, data_ref, out_ref):
    blocks = data_ref.shape[0]
    keys = data_ref[:, rows : 2 * rows, :].reshape(blocks * rows, HEAD)
    values = data_ref[:, 2 * rows : 3 * rows, :].reshape(blocks * rows, HEAD)
    for block in range(blocks):
        out_ref[block] = attend(data_ref[block, 0:rows, :], keys, values)


def attention_kernel(q_ref, k_ref, v_ref, out_ref):
    out_ref[...] = attend(q_ref[...], k_ref[...], v_ref[...])


def cross_kernel(head_count, o_ref, q_ref, *refs):
    out_ref = refs[-1]
    views = (len(refs) - 1) // 2
    key_refs, value_refs = refs[:views], refs[views : 2 * views]
    for head in range(head_count):
        lanes = slice(head * HEAD, (head + 1) * HEAD)
        o_self = o_ref[head].astype(jnp.float32)
        query = (q_ref[:, lanes].astype(jnp.float32) + o_self).astype(jnp.bfloat16).astype(jnp.float32)
        scores = [
            jnp.sum(query * key_ref[:, lanes].astype(jnp.float32), axis=-1, keepdims=True)
            for key_ref in key_refs
        ]
        top = functools.reduce(jnp.maximum, scores)
        weights = [jnp.exp2((score - top) * EXP2_SCALE) for score in scores]
        total = sum(weights[1:], weights[0])
        mixed = None
        for weight, value_ref in zip(weights, value_refs):
            rounded = (weight / total).astype(jnp.bfloat16).astype(jnp.float32)
            term = rounded * value_ref[:, lanes].astype(jnp.float32)
            mixed = term if mixed is None else mixed + term
        o_cross = mixed.astype(jnp.bfloat16).astype(jnp.float32)
        out_ref[:, lanes] = (o_self + o_cross).astype(jnp.bfloat16)


def kernel_params():
    return pltpu.CompilerParams(vmem_limit_bytes=VMEM_LIMIT)


def self_attention(q, k, v, ctx_size):
    rows, width = q.shape
    heads = width // HEAD
    parts = ctx_size // heads
    vmem = pl.BlockSpec(memory_space=pltpu.VMEM)
    if parts == 1:
        packed = pl.pallas_call(
            functools.partial(pack_kernel, heads),
            out_shape=jax.ShapeDtypeStruct((heads, 3 * rows, HEAD), q.dtype),
            in_specs=[vmem] * 3,
            out_specs=vmem,
            compiler_params=kernel_params(),
            name="pack_qkv",
        )(q, k, v)
        moved = lax.all_to_all(packed, "ctx", split_axis=0, concat_axis=0, tiled=True)
        own = pl.pallas_call(
            functools.partial(packed_attention_kernel, rows),
            out_shape=jax.ShapeDtypeStruct((heads, rows, HEAD), q.dtype),
            in_specs=[vmem],
            out_specs=vmem,
            compiler_params=kernel_params(),
            cost_estimate=pl.CostEstimate(
                flops=4 * rows * rows * heads * heads * HEAD,
                bytes_accessed=8 * rows * heads * HEAD,
                transcendentals=rows * rows * heads * heads,
            ),
            name="self_attention",
        )(moved)
        return lax.all_to_all(own, "ctx", split_axis=0, concat_axis=0, tiled=True)

    piece = rows // parts
    query = jnp.transpose(q.reshape(parts, piece, heads, HEAD), (2, 0, 1, 3)).reshape(
        ctx_size, piece, HEAD
    )
    key = jnp.repeat(jnp.transpose(k.reshape(rows, heads, HEAD), (1, 0, 2)), parts, axis=0)
    value = jnp.repeat(jnp.transpose(v.reshape(rows, heads, HEAD), (1, 0, 2)), parts, axis=0)
    packed = jnp.concatenate([query, key, value], axis=1)
    moved = lax.all_to_all(packed, "ctx", split_axis=0, concat_axis=0, tiled=True)
    query = moved[:, :piece].reshape(ctx_size * piece, HEAD)
    key = moved[:, piece : piece + rows].reshape(ctx_size * rows, HEAD)
    value = moved[:, piece + rows :].reshape(ctx_size * rows, HEAD)
    own = pl.pallas_call(
        attention_kernel,
        out_shape=jax.ShapeDtypeStruct((ctx_size * piece, HEAD), q.dtype),
        grid=(ctx_size * piece // rows,),
        in_specs=[
            pl.BlockSpec((rows, HEAD), lambda i: (i, 0)),
            pl.BlockSpec((ctx_size * rows, HEAD), lambda i: (0, 0)),
            pl.BlockSpec((ctx_size * rows, HEAD), lambda i: (0, 0)),
        ],
        out_specs=pl.BlockSpec((rows, HEAD), lambda i: (i, 0)),
        compiler_params=kernel_params(),
        name="self_attention",
    )(query, key, value)
    back = lax.all_to_all(
        own.reshape(ctx_size, piece, HEAD), "ctx", split_axis=0, concat_axis=0, tiled=True
    )
    return back.reshape(heads, rows, HEAD)


def gather_views(array, view_count):
    gathered = [array]
    step = view_count // 2
    while step:
        swap = [(i, i ^ step) for i in range(view_count)]
        gathered += [lax.ppermute(block, "view", swap) for block in gathered]
        step //= 2
    return gathered


def body(view_count, ctx_size, q_self, k_self, v_self, q_cross, k_cross, v_cross):
    _, rows, width = q_self.shape
    heads = width // HEAD
    keys = gather_views(k_cross[0], view_count)
    values = gather_views(v_cross[0], view_count)
    o_self = self_attention(q_self[0], k_self[0], v_self[0], ctx_size)
    vmem = pl.BlockSpec(memory_space=pltpu.VMEM)
    out = pl.pallas_call(
        functools.partial(cross_kernel, heads),
        out_shape=jax.ShapeDtypeStruct((rows, width), q_self.dtype),
        in_specs=[vmem] * (2 + 2 * view_count),
        out_specs=vmem,
        compiler_params=kernel_params(),
        name="cross_view",
    )(o_self, q_cross[0], *keys, *values)
    return out[None]


def solution(mesh):
    spec = P("view", "ctx", None)
    return jax.shard_map(
        functools.partial(body, mesh.shape["view"], mesh.shape["ctx"]),
        mesh=mesh,
        in_specs=(spec,) * 6,
        out_specs=spec,
        check_vma=False,
    )
```

```python
import functools
import math

import jax
import jax.numpy as jnp
from jax import lax
from jax.experimental import pallas as pl
from jax.experimental.pallas import tpu as pltpu
from jax.sharding import PartitionSpec as P

HEAD = 128
SCALE = 1.0 / math.sqrt(HEAD)
EXP2_SCALE = SCALE * math.log2(math.e)
MIB = 1024 * 1024


def pack_kernel(partners, q_ref, k_ref, v_ref, kc_ref, vc_ref, *refs):
    block_refs, pair_ref, sems = refs[: len(partners)], refs[-2], refs[-1]
    rows = q_ref.shape[0]
    me = lax.axis_index("ctx")
    copies = []

    def start(source, target):
        copy = pltpu.make_async_copy(source, target, sems.at[len(copies)])
        copy.start()
        copies.append(copy)

    for partner, block_ref in zip(partners, block_refs):
        lanes = pl.ds(pl.multiple_of((me ^ partner) * HEAD, HEAD), HEAD)
        for part, source in enumerate((q_ref, k_ref, v_ref)):
            start(source.at[:, lanes], block_ref.at[pl.ds(part * rows, rows)])
    for part, source in enumerate((kc_ref, vc_ref)):
        start(source, pair_ref.at[pl.ds(part * rows, rows)])
    for copy in copies:
        copy.wait()


def attend(query, keys, values):
    scores = lax.dot_general(
        query, keys, (((1,), (1,)), ((), ())), preferred_element_type=jnp.float32
    )
    row_max = jnp.max(scores, axis=-1, keepdims=True)
    weights_full = jnp.exp2((scores - row_max) * EXP2_SCALE)
    total = jnp.sum(weights_full, axis=-1, keepdims=True)
    mixed = jnp.dot(
        weights_full.astype(jnp.bfloat16), values, preferred_element_type=jnp.float32
    )
    return (mixed / total).astype(jnp.bfloat16)


def packed_attention_kernel(rows, *refs):
    blocks = len(refs) // 2
    in_refs, out_refs = refs[:blocks], refs[blocks:]
    keys = jnp.concatenate([ref[rows : 2 * rows] for ref in in_refs], axis=0)
    values = jnp.concatenate([ref[2 * rows : 3 * rows] for ref in in_refs], axis=0)
    for in_ref, out_ref in zip(in_refs, out_refs):
        out_ref[...] = attend(in_ref[0:rows], keys, values)


def attention_kernel(q_ref, k_ref, v_ref, out_ref):
    out_ref[...] = attend(q_ref[...], k_ref[...], v_ref[...])


def cross_head(rows, o_self, lanes, q_ref, pair_refs, out_ref):
    o_self = o_self.astype(jnp.float32)
    query = (q_ref[:, lanes].astype(jnp.float32) + o_self).astype(jnp.bfloat16).astype(jnp.float32)
    scores = [
        jnp.sum(query * ref[0:rows, lanes].astype(jnp.float32), axis=-1, keepdims=True)
        for ref in pair_refs
    ]
    top = functools.reduce(jnp.maximum, scores)
    weights = [jnp.exp2((score - top) * EXP2_SCALE) for score in scores]
    total = sum(weights[1:], weights[0])
    mixed = None
    for weight, ref in zip(weights, pair_refs):
        rounded = (weight / total).astype(jnp.bfloat16).astype(jnp.float32)
        term = rounded * ref[rows : 2 * rows, lanes].astype(jnp.float32)
        mixed = term if mixed is None else mixed + term
    o_cross = mixed.astype(jnp.bfloat16).astype(jnp.float32)
    out_ref[:, lanes] = (o_self + o_cross).astype(jnp.bfloat16)


def cross_kernel(head_count, view_count, partners, *refs):
    out_ref, refs = refs[-1], refs[:-1]
    pair_refs, refs = refs[-view_count:], refs[:-view_count]
    q_ref, o_refs = refs[-1], refs[:-1]
    rows = q_ref.shape[0]
    if partners is None:
        for head in range(head_count):
            lanes = slice(head * HEAD, (head + 1) * HEAD)
            cross_head(rows, o_refs[0][head], lanes, q_ref, pair_refs, out_ref)
    else:
        me = lax.axis_index("ctx")
        for partner, o_ref in zip(partners, o_refs):
            lanes = pl.ds(pl.multiple_of((me ^ partner) * HEAD, HEAD), HEAD)
            cross_head(rows, o_ref[...], lanes, q_ref, pair_refs, out_ref)


def kernel_params(grant=32):
    return pltpu.CompilerParams(vmem_limit_bytes=grant * MIB)


def swap(array, axis_name, axis_size, partner):
    return lax.ppermute(array, axis_name, [(i, i ^ partner) for i in range(axis_size)])


def gather_views(array, view_count, *after):
    gathered = [array]
    step = view_count // 2
    for earlier in after:
        gathered, _ = lax.optimization_barrier((gathered, earlier))
        gathered += [swap(block, "view", view_count, step) for block in gathered]
        step //= 2
    return gathered


def split_attention(q, k, v, k_cross, v_cross, ctx_size):
    rows, width = q.shape
    heads = width // HEAD
    partners = tuple(range(1, ctx_size)) + (0,)
    vmem = pl.BlockSpec(memory_space=pltpu.VMEM)
    hbm = pl.BlockSpec(memory_space=pltpu.HBM)
    block = jax.ShapeDtypeStruct((3 * rows, HEAD), q.dtype)
    *blocks, pair = pl.pallas_call(
        functools.partial(pack_kernel, partners),
        out_shape=[block] * heads + [jax.ShapeDtypeStruct((2 * rows, width), q.dtype)],
        in_specs=[hbm] * 5,
        out_specs=[vmem] * (heads + 1),
        scratch_shapes=[pltpu.SemaphoreType.DMA((3 * heads + 2,))],
        compiler_params=kernel_params(60),
        name="pack_qkv",
    )(q, k, v, k_cross, v_cross)
    moved = [
        swap(data, "ctx", ctx_size, partner) if partner else data
        for partner, data in zip(partners, blocks)
    ]
    own = pl.pallas_call(
        functools.partial(packed_attention_kernel, rows),
        out_shape=[jax.ShapeDtypeStruct((rows, HEAD), q.dtype)] * heads,
        in_specs=[vmem] * heads,
        out_specs=[vmem] * heads,
        compiler_params=kernel_params(),
        cost_estimate=pl.CostEstimate(
            flops=4 * rows * rows * heads * heads * HEAD,
            bytes_accessed=8 * rows * heads * HEAD,
            transcendentals=rows * rows * heads * heads,
        ),
        name="self_attention",
    )(*moved)
    back = [
        swap(data, "ctx", ctx_size, partner) if partner else data
        for partner, data in zip(partners, own)
    ]
    return back, (pair, moved[:3], own[0]), partners


def shared_attention(q, k, v, ctx_size):
    rows, width = q.shape
    heads = width // HEAD
    parts = ctx_size // heads
    piece = rows // parts
    query = jnp.transpose(q.reshape(parts, piece, heads, HEAD), (2, 0, 1, 3)).reshape(
        ctx_size, piece, HEAD
    )
    key = jnp.repeat(jnp.transpose(k.reshape(rows, heads, HEAD), (1, 0, 2)), parts, axis=0)
    value = jnp.repeat(jnp.transpose(v.reshape(rows, heads, HEAD), (1, 0, 2)), parts, axis=0)
    packed = jnp.concatenate([query, key, value], axis=1)
    moved = lax.all_to_all(packed, "ctx", split_axis=0, concat_axis=0, tiled=True)
    query = moved[:, :piece].reshape(ctx_size * piece, HEAD)
    key = moved[:, piece : piece + rows].reshape(ctx_size * rows, HEAD)
    value = moved[:, piece + rows :].reshape(ctx_size * rows, HEAD)
    own = pl.pallas_call(
        attention_kernel,
        out_shape=jax.ShapeDtypeStruct((ctx_size * piece, HEAD), q.dtype),
        grid=(ctx_size * piece // rows,),
        in_specs=[
            pl.BlockSpec((rows, HEAD), lambda i: (i, 0)),
            pl.BlockSpec((ctx_size * rows, HEAD), lambda i: (0, 0)),
            pl.BlockSpec((ctx_size * rows, HEAD), lambda i: (0, 0)),
        ],
        out_specs=pl.BlockSpec((rows, HEAD), lambda i: (i, 0)),
        compiler_params=kernel_params(),
        name="self_attention",
    )(query, key, value)
    back = lax.all_to_all(
        own.reshape(ctx_size, piece, HEAD), "ctx", split_axis=0, concat_axis=0, tiled=True
    )
    return back.reshape(heads, rows, HEAD)


def body(view_count, ctx_size, q_self, k_self, v_self, q_cross, k_cross, v_cross):
    _, rows, width = q_self.shape
    heads = width // HEAD
    if ctx_size == heads:
        o_self, (pair, *after), partners = split_attention(
            q_self[0], k_self[0], v_self[0], k_cross[0], v_cross[0], ctx_size
        )
    else:
        o_self = [shared_attention(q_self[0], k_self[0], v_self[0], ctx_size)]
        pair, partners = jnp.concatenate([k_cross[0], v_cross[0]], axis=0), None
        after = [pair] * (view_count.bit_length() - 1)
    pairs = gather_views(pair, view_count, *after)
    vmem = pl.BlockSpec(memory_space=pltpu.VMEM)
    out = pl.pallas_call(
        functools.partial(cross_kernel, heads, view_count, partners),
        out_shape=jax.ShapeDtypeStruct((rows, width), q_self.dtype),
        in_specs=[vmem] * (len(o_self) + 1 + view_count),
        out_specs=vmem,
        compiler_params=kernel_params(),
        name="cross_view",
    )(*o_self, q_cross[0], *pairs)
    return out[None]


def solution(mesh):
    spec = P("view", "ctx", None)
    return jax.shard_map(
        functools.partial(body, mesh.shape["view"], mesh.shape["ctx"]),
        mesh=mesh,
        in_specs=(spec,) * 6,
        out_specs=spec,
        check_vma=False,
    )
```

```python
import functools
import math

import jax
import jax.numpy as jnp
from jax import lax
from jax.experimental import pallas as pl
from jax.experimental.pallas import tpu as pltpu
from jax.sharding import PartitionSpec as P

HEAD = 128
SCALE = 1.0 / math.sqrt(HEAD)
EXP2_SCALE = SCALE * math.log2(math.e)
MIB = 1024 * 1024


def pack_kernel(head_count, q_ref, k_ref, v_ref, out_ref, sems):
    rows = q_ref.shape[0]
    copies = []
    for head in range(head_count):
        lanes = pl.ds(head * HEAD, HEAD)
        for part, source in enumerate((q_ref, k_ref, v_ref)):
            target = out_ref.at[head, pl.ds(part * rows, rows)]
            copies.append(pltpu.make_async_copy(source.at[:, lanes], target, sems.at[len(copies)]))
            copies[-1].start()
    for copy in copies:
        copy.wait()


def attend(query, keys, values):
    scores = lax.dot_general(
        query, keys, (((1,), (1,)), ((), ())), preferred_element_type=jnp.float32
    )
    row_max = jnp.max(scores, axis=-1, keepdims=True)
    weights_raw = jnp.exp2((scores - row_max) * EXP2_SCALE).astype(jnp.bfloat16)
    values_ones = jnp.concatenate([values, jnp.ones_like(values)], axis=1)
    mixed = jnp.dot(weights_raw, values_ones, preferred_element_type=jnp.float32)
    return (mixed[:, :HEAD] / mixed[:, HEAD:]).astype(jnp.bfloat16)


def packed_attention_kernel(rows, group, data_ref, out_ref):
    blocks = data_ref.shape[0]
    keys = jnp.concatenate([data_ref[i, rows : 2 * rows] for i in range(blocks)], axis=0)
    values = jnp.concatenate([data_ref[i, 2 * rows : 3 * rows] for i in range(blocks)], axis=0)
    for first in range(0, blocks, group):
        query = jnp.concatenate(
            [data_ref[first + i, 0:rows] for i in range(group)], axis=0
        )
        mixed = attend(query, keys, values)
        for i in range(group):
            out_ref[first + i] = mixed[i * rows : (i + 1) * rows]


def attention_kernel(q_ref, k_ref, v_ref, out_ref):
    out_ref[...] = attend(q_ref[...], k_ref[...], v_ref[...])


def lane_sums(products):
    high = products.astype(jnp.bfloat16)
    low = (products - high.astype(jnp.float32)).astype(jnp.bfloat16)
    halves = jnp.concatenate([high, low], axis=1)
    ones = jnp.ones((2 * HEAD, HEAD), jnp.bfloat16)
    return jnp.dot(halves, ones, preferred_element_type=jnp.float32)


def cross_kernel(head_count, o_ref, q_ref, *refs):
    out_ref = refs[-1]
    views = (len(refs) - 1) // 2
    key_refs, value_refs = refs[:views], refs[views : 2 * views]
    for head in range(head_count):
        lanes = slice(head * HEAD, (head + 1) * HEAD)
        o_self = o_ref[head].astype(jnp.float32)
        query = (q_ref[:, lanes].astype(jnp.float32) + o_self).astype(jnp.bfloat16).astype(jnp.float32)
        scores = [
            lane_sums(query * key_ref[:, lanes].astype(jnp.float32)) for key_ref in key_refs
        ]
        top = functools.reduce(jnp.maximum, scores)
        weights = [jnp.exp2((score - top) * EXP2_SCALE) for score in scores]
        inverse = 1.0 / sum(weights[1:], weights[0])
        mixed = None
        for weight, value_ref in zip(weights, value_refs):
            rounded = (weight * inverse).astype(jnp.bfloat16).astype(jnp.float32)
            term = rounded * value_ref[:, lanes].astype(jnp.float32)
            mixed = term if mixed is None else mixed + term
        o_cross = mixed.astype(jnp.bfloat16).astype(jnp.float32)
        out_ref[:, lanes] = (o_self + o_cross).astype(jnp.bfloat16)


def kernel_params(grant=32):
    return pltpu.CompilerParams(vmem_limit_bytes=grant * MIB)


def self_attention(q, k, v, pairs, ctx_size):
    rows, width = q.shape
    heads = width // HEAD
    parts = ctx_size // heads
    vmem = pl.BlockSpec(memory_space=pltpu.VMEM)
    hbm = pl.BlockSpec(memory_space=pl.ANY)
    if parts == 1:
        packed = pl.pallas_call(
            functools.partial(pack_kernel, heads),
            out_shape=jax.ShapeDtypeStruct((heads, 3 * rows, HEAD), q.dtype),
            in_specs=[hbm] * 3,
            out_specs=hbm,
            scratch_shapes=[pltpu.SemaphoreType.DMA((3 * heads,))],
            compiler_params=kernel_params(60),
            name="pack_qkv",
        )(q, k, v)
        moved = lax.all_to_all(packed, "ctx", split_axis=0, concat_axis=0, tiled=True)
        moved, pairs = lax.optimization_barrier((moved, pairs))
        own = pl.pallas_call(
            functools.partial(packed_attention_kernel, rows, max(heads // 4, 1)),
            out_shape=jax.ShapeDtypeStruct((heads, rows, HEAD), q.dtype),
            in_specs=[vmem],
            out_specs=vmem,
            compiler_params=kernel_params(),
            cost_estimate=pl.CostEstimate(
                flops=4 * rows * rows * heads * heads * HEAD,
                bytes_accessed=8 * rows * heads * HEAD,
                transcendentals=rows * rows * heads * heads,
            ),
            name="self_attention",
        )(moved)
        back = lax.all_to_all(own, "ctx", split_axis=0, concat_axis=0, tiled=True)
        return back, pairs

    piece = rows // parts
    query = jnp.transpose(q.reshape(parts, piece, heads, HEAD), (2, 0, 1, 3)).reshape(
        ctx_size, piece, HEAD
    )
    key = jnp.repeat(jnp.transpose(k.reshape(rows, heads, HEAD), (1, 0, 2)), parts, axis=0)
    value = jnp.repeat(jnp.transpose(v.reshape(rows, heads, HEAD), (1, 0, 2)), parts, axis=0)
    packed = jnp.concatenate([query, key, value], axis=1)
    moved = lax.all_to_all(packed, "ctx", split_axis=0, concat_axis=0, tiled=True)
    query = moved[:, :piece].reshape(ctx_size * piece, HEAD)
    key = moved[:, piece : piece + rows].reshape(ctx_size * rows, HEAD)
    value = moved[:, piece + rows :].reshape(ctx_size * rows, HEAD)
    own = pl.pallas_call(
        attention_kernel,
        out_shape=jax.ShapeDtypeStruct((ctx_size * piece, HEAD), q.dtype),
        grid=(ctx_size * piece // rows,),
        in_specs=[
            pl.BlockSpec((rows, HEAD), lambda i: (i, 0)),
            pl.BlockSpec((ctx_size * rows, HEAD), lambda i: (0, 0)),
            pl.BlockSpec((ctx_size * rows, HEAD), lambda i: (0, 0)),
        ],
        out_specs=pl.BlockSpec((rows, HEAD), lambda i: (i, 0)),
        compiler_params=kernel_params(),
        name="self_attention",
    )(query, key, value)
    back = lax.all_to_all(
        own.reshape(ctx_size, piece, HEAD), "ctx", split_axis=0, concat_axis=0, tiled=True
    )
    return back.reshape(heads, rows, HEAD), pairs


def gather_views(array, view_count):
    gathered = [array]
    step = view_count // 2
    while step:
        swap = [(i, i ^ step) for i in range(view_count)]
        gathered += [lax.ppermute(block, "view", swap) for block in gathered]
        step //= 2
    return gathered


def body(view_count, ctx_size, q_self, k_self, v_self, q_cross, k_cross, v_cross):
    _, rows, width = q_self.shape
    heads = width // HEAD
    keys = gather_views(k_cross[0], view_count)
    values = gather_views(v_cross[0], view_count)
    o_self, (keys, values) = self_attention(
        q_self[0], k_self[0], v_self[0], (keys, values), ctx_size
    )
    vmem = pl.BlockSpec(memory_space=pltpu.VMEM)
    out = pl.pallas_call(
        functools.partial(cross_kernel, heads),
        out_shape=jax.ShapeDtypeStruct((rows, width), q_self.dtype),
        in_specs=[vmem] * (2 + 2 * view_count),
        out_specs=vmem,
        compiler_params=kernel_params(),
        name="cross_view",
    )(o_self, q_cross[0], *keys, *values)
    return out[None]


def solution(mesh):
    spec = P("view", "ctx", None)
    return jax.shard_map(
        functools.partial(body, mesh.shape["view"], mesh.shape["ctx"]),
        mesh=mesh,
        in_specs=(spec,) * 6,
        out_specs=spec,
        check_vma=False,
    )
```

```python
import functools
import math

import jax
import jax.numpy as jnp
from jax import lax
from jax.experimental import pallas as pl
from jax.experimental.pallas import tpu as pltpu
from jax.sharding import PartitionSpec as P

HEAD = 128
SCALE = 1.0 / math.sqrt(HEAD)
EXP2_SCALE = SCALE * math.log2(math.e)
MIB = 1024 * 1024


def pack_kernel(partners, q_ref, k_ref, v_ref, kc_ref, vc_ref, *refs):
    block_refs, pair_ref, sems = refs[: len(partners)], refs[-2], refs[-1]
    rows = q_ref.shape[0]
    me = lax.axis_index("ctx")
    copies = []

    def start(source, target):
        copy = pltpu.make_async_copy(source, target, sems.at[len(copies)])
        copy.start()
        copies.append(copy)

    for partner, block_ref in zip(partners, block_refs):
        lanes = pl.ds(pl.multiple_of((me ^ partner) * HEAD, HEAD), HEAD)
        for part, source in enumerate((q_ref, k_ref, v_ref)):
            start(source.at[:, lanes], block_ref.at[pl.ds(part * rows, rows)])
    for part, source in enumerate((kc_ref, vc_ref)):
        start(source, pair_ref.at[pl.ds(part * rows, rows)])
    for copy in copies:
        copy.wait()


def attend(query, keys, values):
    scores = lax.dot_general(
        query, keys, (((1,), (1,)), ((), ())), preferred_element_type=jnp.float32
    )
    row_max = jnp.max(scores, axis=-1, keepdims=True)
    weights_raw = jnp.exp2((scores - row_max) * EXP2_SCALE).astype(jnp.bfloat16)
    values_ones = jnp.concatenate([values, jnp.ones_like(values)], axis=1)
    mixed = jnp.dot(weights_raw, values_ones, preferred_element_type=jnp.float32)
    return (mixed[:, :HEAD] / mixed[:, HEAD:]).astype(jnp.bfloat16)


def packed_attention_kernel(partners, rows, group, *refs):
    *in_refs, out_ref = refs
    me = lax.axis_index("ctx")
    keys = jnp.concatenate([ref[rows : 2 * rows] for ref in in_refs], axis=0)
    values = jnp.concatenate([ref[2 * rows : 3 * rows] for ref in in_refs], axis=0)
    for first in range(0, len(in_refs), group):
        query = jnp.concatenate([ref[0:rows] for ref in in_refs[first : first + group]], axis=0)
        mixed = attend(query, keys, values)
        for i in range(group):
            out_ref[me ^ partners[first + i]] = mixed[i * rows : (i + 1) * rows]


def attention_kernel(q_ref, k_ref, v_ref, out_ref):
    out_ref[...] = attend(q_ref[...], k_ref[...], v_ref[...])


def cross_kernel(head_count, o_ref, q_ref, *refs):
    *pair_refs, out_ref = refs
    rows = q_ref.shape[0]
    for head in range(head_count):
        lanes = slice(head * HEAD, (head + 1) * HEAD)
        o_self = o_ref[head].astype(jnp.float32)
        query = (q_ref[:, lanes].astype(jnp.float32) + o_self).astype(jnp.bfloat16).astype(jnp.float32)
        scores = [
            jnp.sum(query * ref[0:rows, lanes].astype(jnp.float32), axis=-1, keepdims=True)
            for ref in pair_refs
        ]
        top = functools.reduce(jnp.maximum, scores)
        weights = [jnp.exp2((score - top) * EXP2_SCALE) for score in scores]
        total = sum(weights[1:], weights[0])
        mixed = None
        for weight, ref in zip(weights, pair_refs):
            rounded = (weight / total).astype(jnp.bfloat16).astype(jnp.float32)
            term = rounded * ref[rows : 2 * rows, lanes].astype(jnp.float32)
            mixed = term if mixed is None else mixed + term
        o_cross = mixed.astype(jnp.bfloat16).astype(jnp.float32)
        out_ref[:, lanes] = (o_self + o_cross).astype(jnp.bfloat16)


def kernel_params(grant=32):
    return pltpu.CompilerParams(vmem_limit_bytes=grant * MIB)


def swap(array, axis_name, axis_size, partner):
    return lax.ppermute(array, axis_name, [(i, i ^ partner) for i in range(axis_size)])


def gather_views(array, view_count, *after):
    gathered = [array]
    step = view_count // 2
    for earlier in after:
        gathered, _ = lax.optimization_barrier((gathered, earlier))
        gathered += [swap(block, "view", view_count, step) for block in gathered]
        step //= 2
    return gathered


def split_attention(q, k, v, k_cross, v_cross, ctx_size):
    rows, width = q.shape
    heads = width // HEAD
    partners = tuple(range(ctx_size - 1, -1, -1))
    vmem = pl.BlockSpec(memory_space=pltpu.VMEM)
    hbm = pl.BlockSpec(memory_space=pltpu.HBM)
    sources = [pltpu.with_memory_space_constraint(x, pltpu.HBM) for x in (q, k, v, k_cross, v_cross)]
    block = jax.ShapeDtypeStruct((3 * rows, HEAD), q.dtype)
    *blocks, pair = pl.pallas_call(
        functools.partial(pack_kernel, partners),
        out_shape=[block] * heads + [jax.ShapeDtypeStruct((2 * rows, width), q.dtype)],
        in_specs=[hbm] * 5,
        out_specs=[vmem] * (heads + 1),
        scratch_shapes=[pltpu.SemaphoreType.DMA((3 * heads + 2,))],
        compiler_params=kernel_params(),
        name="pack_qkv",
    )(*sources)
    moved = [
        swap(data, "ctx", ctx_size, partner) if partner else data
        for partner, data in zip(partners, blocks)
    ]
    own = pl.pallas_call(
        functools.partial(packed_attention_kernel, partners, rows, max(heads // 4, 1)),
        out_shape=jax.ShapeDtypeStruct((heads, rows, HEAD), q.dtype),
        in_specs=[vmem] * heads,
        out_specs=vmem,
        compiler_params=kernel_params(),
        cost_estimate=pl.CostEstimate(
            flops=4 * rows * rows * heads * heads * HEAD,
            bytes_accessed=8 * rows * heads * HEAD,
            transcendentals=rows * rows * heads * heads,
        ),
        name="self_attention",
    )(*moved)
    back = lax.all_to_all(own, "ctx", split_axis=0, concat_axis=0, tiled=True)
    return back, pair, (moved, own)


def shared_attention(q, k, v, ctx_size):
    rows, width = q.shape
    heads = width // HEAD
    parts = ctx_size // heads
    piece = rows // parts
    query = jnp.transpose(q.reshape(parts, piece, heads, HEAD), (2, 0, 1, 3)).reshape(
        ctx_size, piece, HEAD
    )
    key = jnp.repeat(jnp.transpose(k.reshape(rows, heads, HEAD), (1, 0, 2)), parts, axis=0)
    value = jnp.repeat(jnp.transpose(v.reshape(rows, heads, HEAD), (1, 0, 2)), parts, axis=0)
    packed = jnp.concatenate([query, key, value], axis=1)
    moved = lax.all_to_all(packed, "ctx", split_axis=0, concat_axis=0, tiled=True)
    query = moved[:, :piece].reshape(ctx_size * piece, HEAD)
    key = moved[:, piece : piece + rows].reshape(ctx_size * rows, HEAD)
    value = moved[:, piece + rows :].reshape(ctx_size * rows, HEAD)
    own = pl.pallas_call(
        attention_kernel,
        out_shape=jax.ShapeDtypeStruct((ctx_size * piece, HEAD), q.dtype),
        grid=(ctx_size * piece // rows,),
        in_specs=[
            pl.BlockSpec((rows, HEAD), lambda i: (i, 0)),
            pl.BlockSpec((ctx_size * rows, HEAD), lambda i: (0, 0)),
            pl.BlockSpec((ctx_size * rows, HEAD), lambda i: (0, 0)),
        ],
        out_specs=pl.BlockSpec((rows, HEAD), lambda i: (i, 0)),
        compiler_params=kernel_params(),
        name="self_attention",
    )(query, key, value)
    back = lax.all_to_all(
        own.reshape(ctx_size, piece, HEAD), "ctx", split_axis=0, concat_axis=0, tiled=True
    )
    return back.reshape(heads, rows, HEAD)


def body(view_count, ctx_size, q_self, k_self, v_self, q_cross, k_cross, v_cross):
    _, rows, width = q_self.shape
    heads = width // HEAD
    if ctx_size == heads:
        o_self, pair, after = split_attention(
            q_self[0], k_self[0], v_self[0], k_cross[0], v_cross[0], ctx_size
        )
    else:
        o_self = shared_attention(q_self[0], k_self[0], v_self[0], ctx_size)
        pair = jnp.concatenate([k_cross[0], v_cross[0]], axis=0)
        after = [pair] * (view_count.bit_length() - 1)
    pairs = gather_views(pair, view_count, *after)
    vmem = pl.BlockSpec(memory_space=pltpu.VMEM)
    out = pl.pallas_call(
        functools.partial(cross_kernel, heads),
        out_shape=jax.ShapeDtypeStruct((rows, width), q_self.dtype),
        in_specs=[vmem] * (2 + view_count),
        out_specs=vmem,
        compiler_params=kernel_params(),
        name="cross_view",
    )(o_self, q_cross[0], *pairs)
    return out[None]


def solution(mesh):
    spec = P("view", "ctx", None)
    return jax.shard_map(
        functools.partial(body, mesh.shape["view"], mesh.shape["ctx"]),
        mesh=mesh,
        in_specs=(spec,) * 6,
        out_specs=spec,
        check_vma=False,
    )
```

```python
import functools
import math

import jax
import jax.numpy as jnp
from jax import lax
from jax.experimental import pallas as pl
from jax.experimental.pallas import tpu as pltpu
from jax.sharding import PartitionSpec as P

HEAD = 128
SCALE = 1.0 / math.sqrt(HEAD)
EXP2_SCALE = SCALE * math.log2(math.e)
MIB = 1024 * 1024


def pack_kernel(partners, q_ref, k_ref, v_ref, kc_ref, vc_ref, *refs):
    block_refs, pair_ref, sems = refs[: len(partners)], refs[-2], refs[-1]
    rows = q_ref.shape[0]
    me = lax.axis_index("ctx")
    copies = []

    def start(source, target):
        copy = pltpu.make_async_copy(source, target, sems.at[len(copies)])
        copy.start()
        copies.append(copy)

    for partner, block_ref in zip(partners, block_refs):
        lanes = pl.ds(pl.multiple_of((me ^ partner) * HEAD, HEAD), HEAD)
        for part, source in enumerate((q_ref, k_ref, v_ref)):
            start(source.at[:, lanes], block_ref.at[pl.ds(part * rows, rows)])
    for part, source in enumerate((kc_ref, vc_ref)):
        start(source, pair_ref.at[pl.ds(part * rows, rows)])
    for copy in copies:
        copy.wait()


def attend(query, keys, values):
    scores = lax.dot_general(
        query, keys, (((1,), (1,)), ((), ())), preferred_element_type=jnp.float32
    )
    row_max = jnp.max(scores, axis=-1, keepdims=True)
    weights_raw = jnp.exp2((scores - row_max) * EXP2_SCALE).astype(jnp.bfloat16)
    values_ones = jnp.concatenate([values, jnp.ones_like(values)], axis=1)
    mixed = jnp.dot(weights_raw, values_ones, preferred_element_type=jnp.float32)
    return (mixed[:, :HEAD] / mixed[:, HEAD:]).astype(jnp.bfloat16)


def packed_attention_kernel(partners, rows, group, *refs):
    *in_refs, out_ref = refs
    me = lax.axis_index("ctx")
    keys = jnp.concatenate([ref[rows : 2 * rows] for ref in in_refs], axis=0)
    values = jnp.concatenate([ref[2 * rows : 3 * rows] for ref in in_refs], axis=0)
    for first in range(0, len(in_refs), group):
        query = jnp.concatenate([ref[0:rows] for ref in in_refs[first : first + group]], axis=0)
        mixed = attend(query, keys, values)
        for i in range(group):
            out_ref[me ^ partners[first + i]] = mixed[i * rows : (i + 1) * rows]


def attention_kernel(q_ref, k_ref, v_ref, out_ref):
    out_ref[...] = attend(q_ref[...], k_ref[...], v_ref[...])


def cross_kernel(head_count, o_ref, q_ref, *refs):
    *pair_refs, out_ref = refs
    rows = q_ref.shape[0]
    for head in range(head_count):
        lanes = slice(head * HEAD, (head + 1) * HEAD)
        o_self = o_ref[head].astype(jnp.float32)
        query = (q_ref[:, lanes].astype(jnp.float32) + o_self).astype(jnp.bfloat16).astype(jnp.float32)
        scores = [
            jnp.sum(query * ref[0:rows, lanes].astype(jnp.float32), axis=-1, keepdims=True)
            for ref in pair_refs
        ]
        top = functools.reduce(jnp.maximum, scores)
        weights = [jnp.exp2((score - top) * EXP2_SCALE) for score in scores]
        total = sum(weights[1:], weights[0])
        mixed = None
        for weight, ref in zip(weights, pair_refs):
            rounded = (weight / total).astype(jnp.bfloat16).astype(jnp.float32)
            term = rounded * ref[rows : 2 * rows, lanes].astype(jnp.float32)
            mixed = term if mixed is None else mixed + term
        o_cross = mixed.astype(jnp.bfloat16).astype(jnp.float32)
        out_ref[:, lanes] = (o_self + o_cross).astype(jnp.bfloat16)


def kernel_params(grant=32):
    return pltpu.CompilerParams(vmem_limit_bytes=grant * MIB)


def swap(array, axis_name, axis_size, partner):
    return lax.ppermute(array, axis_name, [(i, i ^ partner) for i in range(axis_size)])


def gather_views(array, view_count, *after):
    gathered = [array]
    step = view_count // 2
    for earlier in after:
        gathered, _ = lax.optimization_barrier((gathered, earlier))
        gathered += [swap(block, "view", view_count, step) for block in gathered]
        step //= 2
    return gathered


def split_attention(q, k, v, k_cross, v_cross, ctx_size):
    rows, width = q.shape
    heads = width // HEAD
    partners = tuple(range(ctx_size - 1, -1, -1))
    vmem = pl.BlockSpec(memory_space=pltpu.VMEM)
    hbm = pl.BlockSpec(memory_space=pltpu.HBM)
    sources = [pltpu.with_memory_space_constraint(x, pltpu.HBM) for x in (q, k, v, k_cross, v_cross)]
    block = jax.ShapeDtypeStruct((3 * rows, HEAD), q.dtype)
    *blocks, pair = pl.pallas_call(
        functools.partial(pack_kernel, partners),
        out_shape=[block] * heads + [jax.ShapeDtypeStruct((2 * rows, width), q.dtype)],
        in_specs=[hbm] * 5,
        out_specs=[vmem] * (heads + 1),
        scratch_shapes=[pltpu.SemaphoreType.DMA((3 * heads + 2,))],
        compiler_params=kernel_params(),
        name="pack_qkv",
    )(*sources)
    moved = [
        swap(data, "ctx", ctx_size, partner) if partner else data
        for partner, data in zip(partners, blocks)
    ]
    own = pl.pallas_call(
        functools.partial(packed_attention_kernel, partners, rows, max(heads // 4, 1)),
        out_shape=jax.ShapeDtypeStruct((heads, rows, HEAD), q.dtype),
        in_specs=[vmem] * heads,
        out_specs=vmem,
        compiler_params=kernel_params(),
        cost_estimate=pl.CostEstimate(
            flops=4 * rows * rows * heads * heads * HEAD,
            bytes_accessed=8 * rows * heads * HEAD,
            transcendentals=rows * rows * heads * heads,
        ),
        name="self_attention",
    )(*moved)
    back = lax.all_to_all(own, "ctx", split_axis=0, concat_axis=0, tiled=True)
    return back, pair, (pair, moved)


def shared_attention(q, k, v, ctx_size):
    rows, width = q.shape
    heads = width // HEAD
    parts = ctx_size // heads
    piece = rows // parts
    query = jnp.transpose(q.reshape(parts, piece, heads, HEAD), (2, 0, 1, 3)).reshape(
        ctx_size, piece, HEAD
    )
    key = jnp.repeat(jnp.transpose(k.reshape(rows, heads, HEAD), (1, 0, 2)), parts, axis=0)
    value = jnp.repeat(jnp.transpose(v.reshape(rows, heads, HEAD), (1, 0, 2)), parts, axis=0)
    packed = jnp.concatenate([query, key, value], axis=1)
    moved = lax.all_to_all(packed, "ctx", split_axis=0, concat_axis=0, tiled=True)
    query = moved[:, :piece].reshape(ctx_size * piece, HEAD)
    key = moved[:, piece : piece + rows].reshape(ctx_size * rows, HEAD)
    value = moved[:, piece + rows :].reshape(ctx_size * rows, HEAD)
    own = pl.pallas_call(
        attention_kernel,
        out_shape=jax.ShapeDtypeStruct((ctx_size * piece, HEAD), q.dtype),
        grid=(ctx_size * piece // rows,),
        in_specs=[
            pl.BlockSpec((rows, HEAD), lambda i: (i, 0)),
            pl.BlockSpec((ctx_size * rows, HEAD), lambda i: (0, 0)),
            pl.BlockSpec((ctx_size * rows, HEAD), lambda i: (0, 0)),
        ],
        out_specs=pl.BlockSpec((rows, HEAD), lambda i: (i, 0)),
        compiler_params=kernel_params(),
        name="self_attention",
    )(query, key, value)
    back = lax.all_to_all(
        own.reshape(ctx_size, piece, HEAD), "ctx", split_axis=0, concat_axis=0, tiled=True
    )
    return back.reshape(heads, rows, HEAD)


def body(view_count, ctx_size, q_self, k_self, v_self, q_cross, k_cross, v_cross):
    _, rows, width = q_self.shape
    heads = width // HEAD
    if ctx_size == heads:
        o_self, pair, after = split_attention(
            q_self[0], k_self[0], v_self[0], k_cross[0], v_cross[0], ctx_size
        )
    else:
        o_self = shared_attention(q_self[0], k_self[0], v_self[0], ctx_size)
        pair = jnp.concatenate([k_cross[0], v_cross[0]], axis=0)
        after = [pair] * (view_count.bit_length() - 1)
    pairs = gather_views(pair, view_count, *after)
    vmem = pl.BlockSpec(memory_space=pltpu.VMEM)
    out = pl.pallas_call(
        functools.partial(cross_kernel, heads),
        out_shape=jax.ShapeDtypeStruct((rows, width), q_self.dtype),
        in_specs=[vmem] * (2 + view_count),
        out_specs=vmem,
        compiler_params=kernel_params(),
        name="cross_view",
    )(o_self, q_cross[0], *pairs)
    return out[None]


def solution(mesh):
    spec = P("view", "ctx", None)
    return jax.shard_map(
        functools.partial(body, mesh.shape["view"], mesh.shape["ctx"]),
        mesh=mesh,
        in_specs=(spec,) * 6,
        out_specs=spec,
        check_vma=False,
    )
```

```python
import functools
import math

import jax
import jax.numpy as jnp
from jax import lax
from jax.experimental import pallas as pl
from jax.experimental.pallas import tpu as pltpu
from jax.sharding import PartitionSpec as P

HEAD = 128
SCALE = 1.0 / math.sqrt(HEAD)
EXP2_SCALE = SCALE * math.log2(math.e)
MIB = 1024 * 1024


def pack_kernel(head_count, q_ref, k_ref, v_ref, out_ref, sems):
    rows = q_ref.shape[0]
    copies = []
    for head in range(head_count):
        lanes = pl.ds(head * HEAD, HEAD)
        for part, source in enumerate((q_ref, k_ref, v_ref)):
            target = out_ref.at[head, pl.ds(part * rows, rows)]
            copies.append(pltpu.make_async_copy(source.at[:, lanes], target, sems.at[len(copies)]))
            copies[-1].start()
    for copy in copies:
        copy.wait()


def attend(query, keys, values):
    scores = lax.dot_general(
        query, keys, (((1,), (1,)), ((), ())), preferred_element_type=jnp.float32
    )
    row_max = jnp.max(scores, axis=-1, keepdims=True)
    weights_raw = jnp.exp2((scores - row_max) * EXP2_SCALE).astype(jnp.bfloat16)
    values_ones = jnp.concatenate([values, jnp.ones_like(values)], axis=1)
    mixed = jnp.dot(weights_raw, values_ones, preferred_element_type=jnp.float32)
    return (mixed[:, :HEAD] / mixed[:, HEAD:]).astype(jnp.bfloat16)


def packed_attention_kernel(rows, group, data_ref, out_ref):
    blocks = data_ref.shape[0]
    keys = jnp.concatenate([data_ref[i, rows : 2 * rows] for i in range(blocks)], axis=0)
    values = jnp.concatenate([data_ref[i, 2 * rows : 3 * rows] for i in range(blocks)], axis=0)
    for first in range(0, blocks, group):
        query = jnp.concatenate(
            [data_ref[first + i, 0:rows] for i in range(group)], axis=0
        )
        mixed = attend(query, keys, values)
        for i in range(group):
            out_ref[first + i] = mixed[i * rows : (i + 1) * rows]


def attention_kernel(q_ref, k_ref, v_ref, out_ref):
    out_ref[...] = attend(q_ref[...], k_ref[...], v_ref[...])


def cross_kernel(head_count, o_ref, q_ref, *refs):
    out_ref = refs[-1]
    views = (len(refs) - 1) // 2
    key_refs, value_refs = refs[:views], refs[views : 2 * views]
    for head in range(head_count):
        lanes = slice(head * HEAD, (head + 1) * HEAD)
        o_self = o_ref[head].astype(jnp.float32)
        query = (q_ref[:, lanes].astype(jnp.float32) + o_self).astype(jnp.bfloat16).astype(jnp.float32)
        scores = [
            jnp.sum(query * key_ref[:, lanes].astype(jnp.float32), axis=-1, keepdims=True)
            for key_ref in key_refs
        ]
        top = functools.reduce(jnp.maximum, scores)
        weights = [jnp.exp2((score - top) * EXP2_SCALE) for score in scores]
        total = sum(weights[1:], weights[0])
        mixed = None
        for weight, value_ref in zip(weights, value_refs):
            rounded = (weight / total).astype(jnp.bfloat16).astype(jnp.float32)
            term = rounded * value_ref[:, lanes].astype(jnp.float32)
            mixed = term if mixed is None else mixed + term
        o_cross = mixed.astype(jnp.bfloat16).astype(jnp.float32)
        out_ref[:, lanes] = (o_self + o_cross).astype(jnp.bfloat16)


def kernel_params(grant=32):
    return pltpu.CompilerParams(vmem_limit_bytes=grant * MIB)


def self_attention(q, k, v, pairs, ctx_size):
    rows, width = q.shape
    heads = width // HEAD
    parts = ctx_size // heads
    vmem = pl.BlockSpec(memory_space=pltpu.VMEM)
    hbm = pl.BlockSpec(memory_space=pltpu.HBM)
    if parts == 1:
        packed = pl.pallas_call(
            functools.partial(pack_kernel, heads),
            out_shape=jax.ShapeDtypeStruct((heads, 3 * rows, HEAD), q.dtype),
            in_specs=[hbm] * 3,
            out_specs=vmem,
            scratch_shapes=[pltpu.SemaphoreType.DMA((3 * heads,))],
            compiler_params=kernel_params(),
            name="pack_qkv",
        )(*[pltpu.with_memory_space_constraint(x, pltpu.HBM) for x in (q, k, v)])
        moved = lax.all_to_all(packed, "ctx", split_axis=0, concat_axis=0, tiled=True)
        moved, pairs = lax.optimization_barrier((moved, pairs))
        own = pl.pallas_call(
            functools.partial(packed_attention_kernel, rows, max(heads // 4, 1)),
            out_shape=jax.ShapeDtypeStruct((heads, rows, HEAD), q.dtype),
            in_specs=[vmem],
            out_specs=vmem,
            compiler_params=kernel_params(),
            cost_estimate=pl.CostEstimate(
                flops=4 * rows * rows * heads * heads * HEAD,
                bytes_accessed=8 * rows * heads * HEAD,
                transcendentals=rows * rows * heads * heads,
            ),
            name="self_attention",
        )(moved)
        back = lax.all_to_all(own, "ctx", split_axis=0, concat_axis=0, tiled=True)
        return back, pairs

    piece = rows // parts
    query = jnp.transpose(q.reshape(parts, piece, heads, HEAD), (2, 0, 1, 3)).reshape(
        ctx_size, piece, HEAD
    )
    key = jnp.repeat(jnp.transpose(k.reshape(rows, heads, HEAD), (1, 0, 2)), parts, axis=0)
    value = jnp.repeat(jnp.transpose(v.reshape(rows, heads, HEAD), (1, 0, 2)), parts, axis=0)
    packed = jnp.concatenate([query, key, value], axis=1)
    moved = lax.all_to_all(packed, "ctx", split_axis=0, concat_axis=0, tiled=True)
    query = moved[:, :piece].reshape(ctx_size * piece, HEAD)
    key = moved[:, piece : piece + rows].reshape(ctx_size * rows, HEAD)
    value = moved[:, piece + rows :].reshape(ctx_size * rows, HEAD)
    own = pl.pallas_call(
        attention_kernel,
        out_shape=jax.ShapeDtypeStruct((ctx_size * piece, HEAD), q.dtype),
        grid=(ctx_size * piece // rows,),
        in_specs=[
            pl.BlockSpec((rows, HEAD), lambda i: (i, 0)),
            pl.BlockSpec((ctx_size * rows, HEAD), lambda i: (0, 0)),
            pl.BlockSpec((ctx_size * rows, HEAD), lambda i: (0, 0)),
        ],
        out_specs=pl.BlockSpec((rows, HEAD), lambda i: (i, 0)),
        compiler_params=kernel_params(),
        name="self_attention",
    )(query, key, value)
    back = lax.all_to_all(
        own.reshape(ctx_size, piece, HEAD), "ctx", split_axis=0, concat_axis=0, tiled=True
    )
    return back.reshape(heads, rows, HEAD), pairs


def gather_views(array, view_count):
    gathered = [array]
    step = view_count // 2
    while step:
        swap = [(i, i ^ step) for i in range(view_count)]
        gathered += [lax.ppermute(block, "view", swap) for block in gathered]
        step //= 2
    return gathered


def body(view_count, ctx_size, q_self, k_self, v_self, q_cross, k_cross, v_cross):
    _, rows, width = q_self.shape
    heads = width // HEAD
    keys = gather_views(k_cross[0], view_count)
    values = gather_views(v_cross[0], view_count)
    o_self, (keys, values) = self_attention(
        q_self[0], k_self[0], v_self[0], (keys, values), ctx_size
    )
    vmem = pl.BlockSpec(memory_space=pltpu.VMEM)
    out = pl.pallas_call(
        functools.partial(cross_kernel, heads),
        out_shape=jax.ShapeDtypeStruct((rows, width), q_self.dtype),
        in_specs=[vmem] * (2 + 2 * view_count),
        out_specs=vmem,
        compiler_params=kernel_params(),
        name="cross_view",
    )(o_self, q_cross[0], *keys, *values)
    return out[None]


def solution(mesh):
    spec = P("view", "ctx", None)
    return jax.shard_map(
        functools.partial(body, mesh.shape["view"], mesh.shape["ctx"]),
        mesh=mesh,
        in_specs=(spec,) * 6,
        out_specs=spec,
        check_vma=False,
    )
```

```python
import functools
import math

import jax
import jax.numpy as jnp
from jax import lax
from jax.experimental import pallas as pl
from jax.experimental.pallas import tpu as pltpu
from jax.sharding import PartitionSpec as P

HEAD = 128
SCALE = 1.0 / math.sqrt(HEAD)
EXP2_SCALE = SCALE * math.log2(math.e)
MIB = 1024 * 1024


def pack_kernel(partners, q_ref, k_ref, v_ref, kc_ref, vc_ref, *refs):
    *far_refs, near_ref, pair_ref, sems = refs
    rows = q_ref.shape[0]
    group = near_ref.shape[0]
    me = lax.axis_index("ctx")
    copies = []

    def start(source, target):
        copy = pltpu.make_async_copy(source, target, sems.at[len(copies)])
        copy.start()
        copies.append(copy)

    def pack(head, target):
        lanes = pl.ds(pl.multiple_of(head * HEAD, HEAD), HEAD)
        for part, source in enumerate((q_ref, k_ref, v_ref)):
            start(source.at[:, lanes], target.at[pl.ds(part * rows, rows)])

    for partner, far_ref in zip(partners, far_refs):
        pack(me ^ partner, far_ref)
    for part, source in enumerate((kc_ref, vc_ref)):
        start(source, pair_ref.at[pl.ds(part * rows, rows)])
    for member in range(group):
        pack((me // group) * group + member, near_ref.at[member])
    for copy in copies:
        copy.wait()


def attend(query, keys, values):
    scores = lax.dot_general(
        query, keys, (((1,), (1,)), ((), ())), preferred_element_type=jnp.float32
    )
    row_max = jnp.max(scores, axis=-1, keepdims=True)
    weights_raw = jnp.exp2((scores - row_max) * EXP2_SCALE).astype(jnp.bfloat16)
    values_ones = jnp.concatenate([values, jnp.ones_like(values)], axis=1)
    mixed = jnp.dot(weights_raw, values_ones, preferred_element_type=jnp.float32)
    return (mixed[:, :HEAD] / mixed[:, HEAD:]).astype(jnp.bfloat16)


def packed_attention_kernel(partners, rows, *refs):
    *far_refs, near_ref, out_ref = refs
    group = near_ref.shape[0]
    me = lax.axis_index("ctx")
    blocks = [(me ^ partner, ref) for partner, ref in zip(partners, far_refs)]
    blocks += [((me // group) * group + i, near_ref.at[i]) for i in range(group)]
    keys = jnp.concatenate([ref[rows : 2 * rows] for _, ref in blocks], axis=0)
    values = jnp.concatenate([ref[2 * rows : 3 * rows] for _, ref in blocks], axis=0)
    for first in range(0, len(blocks), 2):
        chunk = blocks[first : first + 2]
        query = jnp.concatenate([ref[0:rows] for _, ref in chunk], axis=0)
        mixed = attend(query, keys, values)
        for i, (source, _) in enumerate(chunk):
            out_ref[source] = mixed[i * rows : (i + 1) * rows]


def attention_kernel(q_ref, k_ref, v_ref, out_ref):
    out_ref[...] = attend(q_ref[...], k_ref[...], v_ref[...])


def cross_kernel(head_count, o_ref, q_ref, *refs):
    *pair_refs, out_ref = refs
    rows = q_ref.shape[0]
    for head in range(head_count):
        lanes = slice(head * HEAD, (head + 1) * HEAD)
        o_self = o_ref[head].astype(jnp.float32)
        query = (q_ref[:, lanes].astype(jnp.float32) + o_self).astype(jnp.bfloat16).astype(jnp.float32)
        scores = [
            jnp.sum(query * ref[0:rows, lanes].astype(jnp.float32), axis=-1, keepdims=True)
            for ref in pair_refs
        ]
        top = functools.reduce(jnp.maximum, scores)
        weights = [jnp.exp2((score - top) * EXP2_SCALE) for score in scores]
        total = sum(weights[1:], weights[0])
        mixed = None
        for weight, ref in zip(weights, pair_refs):
            rounded = (weight / total).astype(jnp.bfloat16).astype(jnp.float32)
            term = rounded * ref[rows : 2 * rows, lanes].astype(jnp.float32)
            mixed = term if mixed is None else mixed + term
        o_cross = mixed.astype(jnp.bfloat16).astype(jnp.float32)
        out_ref[:, lanes] = (o_self + o_cross).astype(jnp.bfloat16)


def kernel_params(grant=32):
    return pltpu.CompilerParams(vmem_limit_bytes=grant * MIB)


def swap(array, axis_name, axis_size, partner):
    return lax.ppermute(array, axis_name, [(i, i ^ partner) for i in range(axis_size)])


def gather_views(array, view_count, *after):
    gathered = [array]
    step = view_count // 2
    for earlier in after:
        gathered, _ = lax.optimization_barrier((gathered, earlier))
        gathered += [swap(block, "view", view_count, step) for block in gathered]
        step //= 2
    return gathered


def split_attention(q, k, v, k_cross, v_cross, ctx_size):
    rows, width = q.shape
    heads = width // HEAD
    group = ctx_size // 2
    partners = tuple(range(ctx_size - 1, group - 1, -1))
    vmem = pl.BlockSpec(memory_space=pltpu.VMEM)
    hbm = pl.BlockSpec(memory_space=pltpu.HBM)
    sources = [pltpu.with_memory_space_constraint(x, pltpu.HBM) for x in (q, k, v, k_cross, v_cross)]
    *far, near, pair = pl.pallas_call(
        functools.partial(pack_kernel, partners),
        out_shape=[jax.ShapeDtypeStruct((3 * rows, HEAD), q.dtype)] * len(partners)
        + [
            jax.ShapeDtypeStruct((group, 3 * rows, HEAD), q.dtype),
            jax.ShapeDtypeStruct((2 * rows, width), q.dtype),
        ],
        in_specs=[hbm] * 5,
        out_specs=[vmem] * (len(partners) + 2),
        scratch_shapes=[pltpu.SemaphoreType.DMA((3 * heads + 2,))],
        compiler_params=kernel_params(),
        name="pack_qkv",
    )(*sources)
    far = [swap(data, "ctx", ctx_size, partner) for partner, data in zip(partners, far)]
    near = lax.all_to_all(
        near,
        "ctx",
        split_axis=0,
        concat_axis=0,
        tiled=True,
        axis_index_groups=[list(range(group)), list(range(group, ctx_size))],
    )
    own = pl.pallas_call(
        functools.partial(packed_attention_kernel, partners, rows),
        out_shape=jax.ShapeDtypeStruct((heads, rows, HEAD), q.dtype),
        in_specs=[vmem] * (len(partners) + 1),
        out_specs=vmem,
        compiler_params=kernel_params(),
        cost_estimate=pl.CostEstimate(
            flops=4 * rows * rows * heads * heads * HEAD,
            bytes_accessed=8 * rows * heads * HEAD,
            transcendentals=rows * rows * heads * heads,
        ),
        name="self_attention",
    )(*far, near)
    back = lax.all_to_all(own, "ctx", split_axis=0, concat_axis=0, tiled=True)
    return back, pair, (pair, near)


def shared_attention(q, k, v, ctx_size):
    rows, width = q.shape
    heads = width // HEAD
    parts = ctx_size // heads
    piece = rows // parts
    query = jnp.transpose(q.reshape(parts, piece, heads, HEAD), (2, 0, 1, 3)).reshape(
        ctx_size, piece, HEAD
    )
    key = jnp.repeat(jnp.transpose(k.reshape(rows, heads, HEAD), (1, 0, 2)), parts, axis=0)
    value = jnp.repeat(jnp.transpose(v.reshape(rows, heads, HEAD), (1, 0, 2)), parts, axis=0)
    packed = jnp.concatenate([query, key, value], axis=1)
    moved = lax.all_to_all(packed, "ctx", split_axis=0, concat_axis=0, tiled=True)
    query = moved[:, :piece].reshape(ctx_size * piece, HEAD)
    key = moved[:, piece : piece + rows].reshape(ctx_size * rows, HEAD)
    value = moved[:, piece + rows :].reshape(ctx_size * rows, HEAD)
    own = pl.pallas_call(
        attention_kernel,
        out_shape=jax.ShapeDtypeStruct((ctx_size * piece, HEAD), q.dtype),
        grid=(ctx_size * piece // rows,),
        in_specs=[
            pl.BlockSpec((rows, HEAD), lambda i: (i, 0)),
            pl.BlockSpec((ctx_size * rows, HEAD), lambda i: (0, 0)),
            pl.BlockSpec((ctx_size * rows, HEAD), lambda i: (0, 0)),
        ],
        out_specs=pl.BlockSpec((rows, HEAD), lambda i: (i, 0)),
        compiler_params=kernel_params(),
        name="self_attention",
    )(query, key, value)
    back = lax.all_to_all(
        own.reshape(ctx_size, piece, HEAD), "ctx", split_axis=0, concat_axis=0, tiled=True
    )
    return back.reshape(heads, rows, HEAD)


def body(view_count, ctx_size, q_self, k_self, v_self, q_cross, k_cross, v_cross):
    _, rows, width = q_self.shape
    heads = width // HEAD
    if ctx_size == heads:
        o_self, pair, after = split_attention(
            q_self[0], k_self[0], v_self[0], k_cross[0], v_cross[0], ctx_size
        )
    else:
        o_self = shared_attention(q_self[0], k_self[0], v_self[0], ctx_size)
        pair = jnp.concatenate([k_cross[0], v_cross[0]], axis=0)
        after = [pair] * (view_count.bit_length() - 1)
    pairs = gather_views(pair, view_count, *after)
    vmem = pl.BlockSpec(memory_space=pltpu.VMEM)
    out = pl.pallas_call(
        functools.partial(cross_kernel, heads),
        out_shape=jax.ShapeDtypeStruct((rows, width), q_self.dtype),
        in_specs=[vmem] * (2 + view_count),
        out_specs=vmem,
        compiler_params=kernel_params(),
        name="cross_view",
    )(o_self, q_cross[0], *pairs)
    return out[None]


def solution(mesh):
    spec = P("view", "ctx", None)
    return jax.shard_map(
        functools.partial(body, mesh.shape["view"], mesh.shape["ctx"]),
        mesh=mesh,
        in_specs=(spec,) * 6,
        out_specs=spec,
        check_vma=False,
    )
```

```python
import functools
import math

import jax
import jax.numpy as jnp
from jax import lax
from jax.experimental import pallas as pl
from jax.experimental.pallas import tpu as pltpu
from jax.sharding import PartitionSpec as P

HEAD = 128
SCALE = 1.0 / math.sqrt(HEAD)
EXP2_SCALE = SCALE * math.log2(math.e)
MIB = 1024 * 1024


def pack_kernel(partners, q_ref, k_ref, v_ref, kc_ref, vc_ref, *refs):
    block_refs, pair_ref, sems = refs[: len(partners)], refs[-2], refs[-1]
    rows = q_ref.shape[0]
    me = lax.axis_index("ctx")
    copies = []

    def start(source, target):
        copy = pltpu.make_async_copy(source, target, sems.at[len(copies)])
        copy.start()
        copies.append(copy)

    for partner, block_ref in zip(partners, block_refs):
        lanes = pl.ds(pl.multiple_of((me ^ partner) * HEAD, HEAD), HEAD)
        for part, source in enumerate((q_ref, k_ref, v_ref)):
            start(source.at[:, lanes], block_ref.at[pl.ds(part * rows, rows)])
    for part, source in enumerate((kc_ref, vc_ref)):
        start(source, pair_ref.at[pl.ds(part * rows, rows)])
    for copy in copies:
        copy.wait()


def attend(query, keys, values):
    scores = lax.dot_general(
        query, keys, (((1,), (1,)), ((), ())), preferred_element_type=jnp.float32
    )
    row_max = jnp.max(scores, axis=-1, keepdims=True)
    weights_raw = jnp.exp2((scores - row_max) * EXP2_SCALE).astype(jnp.bfloat16)
    values_ones = jnp.concatenate([values, jnp.ones_like(values)], axis=1)
    mixed = jnp.dot(weights_raw, values_ones, preferred_element_type=jnp.float32)
    return (mixed[:, :HEAD] / mixed[:, HEAD:]).astype(jnp.bfloat16)


def packed_attention_kernel(partners, rows, group, *refs):
    *in_refs, out_ref = refs
    me = lax.axis_index("ctx")
    keys = jnp.concatenate([ref[rows : 2 * rows] for ref in in_refs], axis=0)
    values = jnp.concatenate([ref[2 * rows : 3 * rows] for ref in in_refs], axis=0)
    for first in range(0, len(in_refs), group):
        query = jnp.concatenate([ref[0:rows] for ref in in_refs[first : first + group]], axis=0)
        mixed = attend(query, keys, values)
        for i in range(group):
            out_ref[me ^ partners[first + i]] = mixed[i * rows : (i + 1) * rows]


def attention_kernel(q_ref, k_ref, v_ref, out_ref):
    out_ref[...] = attend(q_ref[...], k_ref[...], v_ref[...])


def cross_kernel(head_count, o_ref, q_ref, *refs):
    *pair_refs, out_ref = refs
    rows = q_ref.shape[0]
    for head in range(head_count):
        lanes = slice(head * HEAD, (head + 1) * HEAD)
        o_self = o_ref[head].astype(jnp.float32)
        query = (q_ref[:, lanes].astype(jnp.float32) + o_self).astype(jnp.bfloat16).astype(jnp.float32)
        scores = [
            jnp.sum(query * ref[0:rows, lanes].astype(jnp.float32), axis=-1, keepdims=True)
            for ref in pair_refs
        ]
        top = functools.reduce(jnp.maximum, scores)
        weights = [jnp.exp2((score - top) * EXP2_SCALE) for score in scores]
        total = sum(weights[1:], weights[0])
        mixed = None
        for weight, ref in zip(weights, pair_refs):
            rounded = (weight / total).astype(jnp.bfloat16).astype(jnp.float32)
            term = rounded * ref[rows : 2 * rows, lanes].astype(jnp.float32)
            mixed = term if mixed is None else mixed + term
        o_cross = mixed.astype(jnp.bfloat16).astype(jnp.float32)
        out_ref[:, lanes] = (o_self + o_cross).astype(jnp.bfloat16)


def kernel_params(grant=32):
    return pltpu.CompilerParams(vmem_limit_bytes=grant * MIB)


def swap(array, axis_name, axis_size, partner):
    return lax.ppermute(array, axis_name, [(i, i ^ partner) for i in range(axis_size)])


def gather_views(array, view_count, *after):
    gathered = [array]
    step = view_count // 2
    for earlier in after:
        gathered, _ = lax.optimization_barrier((gathered, earlier))
        gathered += [swap(block, "view", view_count, step) for block in gathered]
        step //= 2
    return gathered


def split_attention(q, k, v, k_cross, v_cross, ctx_size):
    rows, width = q.shape
    heads = width // HEAD
    far = list(range(ctx_size - 1, ctx_size // 2 - 1, -1))
    near = list(range(ctx_size // 2 - 1, -1, -1))
    partners = tuple(far[:3] + near[:1] + far[3:] + near[1:])
    vmem = pl.BlockSpec(memory_space=pltpu.VMEM)
    hbm = pl.BlockSpec(memory_space=pltpu.HBM)
    sources = [pltpu.with_memory_space_constraint(x, pltpu.HBM) for x in (q, k, v, k_cross, v_cross)]
    block = jax.ShapeDtypeStruct((3 * rows, HEAD), q.dtype)
    *blocks, pair = pl.pallas_call(
        functools.partial(pack_kernel, partners),
        out_shape=[block] * heads + [jax.ShapeDtypeStruct((2 * rows, width), q.dtype)],
        in_specs=[hbm] * 5,
        out_specs=[vmem] * (heads + 1),
        scratch_shapes=[pltpu.SemaphoreType.DMA((3 * heads + 2,))],
        compiler_params=kernel_params(),
        name="pack_qkv",
    )(*sources)
    moved = [
        swap(data, "ctx", ctx_size, partner) if partner else data
        for partner, data in zip(partners, blocks)
    ]
    own = pl.pallas_call(
        functools.partial(packed_attention_kernel, partners, rows, max(heads // 4, 1)),
        out_shape=jax.ShapeDtypeStruct((heads, rows, HEAD), q.dtype),
        in_specs=[vmem] * heads,
        out_specs=vmem,
        compiler_params=kernel_params(),
        cost_estimate=pl.CostEstimate(
            flops=4 * rows * rows * heads * heads * HEAD,
            bytes_accessed=8 * rows * heads * HEAD,
            transcendentals=rows * rows * heads * heads,
        ),
        name="self_attention",
    )(*moved)
    back = lax.all_to_all(own, "ctx", split_axis=0, concat_axis=0, tiled=True)
    return back, pair, (pair, moved)


def shared_attention(q, k, v, ctx_size):
    rows, width = q.shape
    heads = width // HEAD
    parts = ctx_size // heads
    piece = rows // parts
    query = jnp.transpose(q.reshape(parts, piece, heads, HEAD), (2, 0, 1, 3)).reshape(
        ctx_size, piece, HEAD
    )
    key = jnp.repeat(jnp.transpose(k.reshape(rows, heads, HEAD), (1, 0, 2)), parts, axis=0)
    value = jnp.repeat(jnp.transpose(v.reshape(rows, heads, HEAD), (1, 0, 2)), parts, axis=0)
    packed = jnp.concatenate([query, key, value], axis=1)
    moved = lax.all_to_all(packed, "ctx", split_axis=0, concat_axis=0, tiled=True)
    query = moved[:, :piece].reshape(ctx_size * piece, HEAD)
    key = moved[:, piece : piece + rows].reshape(ctx_size * rows, HEAD)
    value = moved[:, piece + rows :].reshape(ctx_size * rows, HEAD)
    own = pl.pallas_call(
        attention_kernel,
        out_shape=jax.ShapeDtypeStruct((ctx_size * piece, HEAD), q.dtype),
        grid=(ctx_size * piece // rows,),
        in_specs=[
            pl.BlockSpec((rows, HEAD), lambda i: (i, 0)),
            pl.BlockSpec((ctx_size * rows, HEAD), lambda i: (0, 0)),
            pl.BlockSpec((ctx_size * rows, HEAD), lambda i: (0, 0)),
        ],
        out_specs=pl.BlockSpec((rows, HEAD), lambda i: (i, 0)),
        compiler_params=kernel_params(),
        name="self_attention",
    )(query, key, value)
    back = lax.all_to_all(
        own.reshape(ctx_size, piece, HEAD), "ctx", split_axis=0, concat_axis=0, tiled=True
    )
    return back.reshape(heads, rows, HEAD)


def body(view_count, ctx_size, q_self, k_self, v_self, q_cross, k_cross, v_cross):
    _, rows, width = q_self.shape
    heads = width // HEAD
    if ctx_size == heads:
        o_self, pair, after = split_attention(
            q_self[0], k_self[0], v_self[0], k_cross[0], v_cross[0], ctx_size
        )
    else:
        o_self = shared_attention(q_self[0], k_self[0], v_self[0], ctx_size)
        pair = jnp.concatenate([k_cross[0], v_cross[0]], axis=0)
        after = [pair] * (view_count.bit_length() - 1)
    pairs = gather_views(pair, view_count, *after)
    vmem = pl.BlockSpec(memory_space=pltpu.VMEM)
    out = pl.pallas_call(
        functools.partial(cross_kernel, heads),
        out_shape=jax.ShapeDtypeStruct((rows, width), q_self.dtype),
        in_specs=[vmem] * (2 + view_count),
        out_specs=vmem,
        compiler_params=kernel_params(),
        name="cross_view",
    )(o_self, q_cross[0], *pairs)
    return out[None]


def solution(mesh):
    spec = P("view", "ctx", None)
    return jax.shard_map(
        functools.partial(body, mesh.shape["view"], mesh.shape["ctx"]),
        mesh=mesh,
        in_specs=(spec,) * 6,
        out_specs=spec,
        check_vma=False,
    )
```

```python
import functools
import math

import jax
import jax.numpy as jnp
from jax import lax
from jax.experimental import pallas as pl
from jax.experimental.pallas import tpu as pltpu
from jax.sharding import PartitionSpec as P

HEAD = 128
SCALE = 1.0 / math.sqrt(HEAD)
EXP2_SCALE = SCALE * math.log2(math.e)
MIB = 1024 * 1024


def pack_kernel(far, q_ref, k_ref, v_ref, kc_ref, vc_ref, *refs):
    *far_refs, across_ref, along_ref, own_ref, pair_ref, sems = refs
    rows = q_ref.shape[0]
    me = lax.axis_index("ctx")
    copies = []

    def start(source, target):
        copy = pltpu.make_async_copy(source, target, sems.at[len(copies)])
        copy.start()
        copies.append(copy)

    blocks = list(zip(far, far_refs))
    blocks += [(1, across_ref.at[0]), (3, across_ref.at[1]), (2, along_ref), (0, own_ref)]
    for partner, target in blocks:
        lanes = pl.ds(pl.multiple_of((me ^ partner) * HEAD, HEAD), HEAD)
        for part, source in enumerate((q_ref, k_ref, v_ref)):
            start(source.at[:, lanes], target.at[pl.ds(part * rows, rows)])
    for part, source in enumerate((kc_ref, vc_ref)):
        start(source, pair_ref.at[pl.ds(part * rows, rows)])
    for copy in copies:
        copy.wait()


def attend(query, keys, values):
    scores = lax.dot_general(
        query, keys, (((1,), (1,)), ((), ())), preferred_element_type=jnp.float32
    )
    row_max = jnp.max(scores, axis=-1, keepdims=True)
    weights_raw = jnp.exp2((scores - row_max) * EXP2_SCALE).astype(jnp.bfloat16)
    values_ones = jnp.concatenate([values, jnp.ones_like(values)], axis=1)
    mixed = jnp.dot(weights_raw, values_ones, preferred_element_type=jnp.float32)
    return (mixed[:, :HEAD] / mixed[:, HEAD:]).astype(jnp.bfloat16)


def packed_attention_kernel(far, rows, *refs):
    *far_refs, across_ref, along_ref, own_ref, out_ref = refs
    me = lax.axis_index("ctx")
    blocks = list(zip(far, far_refs))
    blocks += [(0, own_ref), (1, across_ref.at[0]), (2, along_ref.at[0]), (3, along_ref.at[1])]
    keys = jnp.concatenate([ref[rows : 2 * rows] for _, ref in blocks], axis=0)
    values = jnp.concatenate([ref[2 * rows : 3 * rows] for _, ref in blocks], axis=0)
    for first in range(0, len(blocks), 2):
        chunk = blocks[first : first + 2]
        query = jnp.concatenate([ref[0:rows] for _, ref in chunk], axis=0)
        mixed = attend(query, keys, values)
        for i, (partner, _) in enumerate(chunk):
            out_ref[me ^ partner] = mixed[i * rows : (i + 1) * rows]


def attention_kernel(q_ref, k_ref, v_ref, out_ref):
    out_ref[...] = attend(q_ref[...], k_ref[...], v_ref[...])


def cross_kernel(head_count, o_ref, q_ref, *refs):
    *pair_refs, out_ref = refs
    rows = q_ref.shape[0]
    for head in range(head_count):
        lanes = slice(head * HEAD, (head + 1) * HEAD)
        o_self = o_ref[head].astype(jnp.float32)
        query = (q_ref[:, lanes].astype(jnp.float32) + o_self).astype(jnp.bfloat16).astype(jnp.float32)
        scores = [
            jnp.sum(query * ref[0:rows, lanes].astype(jnp.float32), axis=-1, keepdims=True)
            for ref in pair_refs
        ]
        top = functools.reduce(jnp.maximum, scores)
        weights = [jnp.exp2((score - top) * EXP2_SCALE) for score in scores]
        total = sum(weights[1:], weights[0])
        mixed = None
        for weight, ref in zip(weights, pair_refs):
            rounded = (weight / total).astype(jnp.bfloat16).astype(jnp.float32)
            term = rounded * ref[rows : 2 * rows, lanes].astype(jnp.float32)
            mixed = term if mixed is None else mixed + term
        o_cross = mixed.astype(jnp.bfloat16).astype(jnp.float32)
        out_ref[:, lanes] = (o_self + o_cross).astype(jnp.bfloat16)


def kernel_params(grant=32):
    return pltpu.CompilerParams(vmem_limit_bytes=grant * MIB)


def swap(array, axis_name, axis_size, partner):
    return lax.ppermute(array, axis_name, [(i, i ^ partner) for i in range(axis_size)])


def gather_views(array, view_count, *after):
    gathered = [array]
    step = view_count // 2
    for earlier in after:
        gathered, _ = lax.optimization_barrier((gathered, earlier))
        gathered += [swap(block, "view", view_count, step) for block in gathered]
        step //= 2
    return gathered


def split_attention(q, k, v, k_cross, v_cross, ctx_size):
    rows, width = q.shape
    heads = width // HEAD
    far = (7, 6, 5, 4)
    vmem = pl.BlockSpec(memory_space=pltpu.VMEM)
    hbm = pl.BlockSpec(memory_space=pltpu.HBM)
    sources = [pltpu.with_memory_space_constraint(x, pltpu.HBM) for x in (q, k, v, k_cross, v_cross)]
    block = jax.ShapeDtypeStruct((3 * rows, HEAD), q.dtype)
    two_blocks = jax.ShapeDtypeStruct((2, 3 * rows, HEAD), q.dtype)
    *far_blocks, across, along, own, pair = pl.pallas_call(
        functools.partial(pack_kernel, far),
        out_shape=[block] * len(far)
        + [two_blocks, block, block, jax.ShapeDtypeStruct((2 * rows, width), q.dtype)],
        in_specs=[hbm] * 5,
        out_specs=[vmem] * (len(far) + 4),
        scratch_shapes=[pltpu.SemaphoreType.DMA((3 * heads + 2,))],
        compiler_params=kernel_params(),
        name="pack_qkv",
    )(*sources)
    across = swap(across, "ctx", ctx_size, 1)
    moved = [swap(data, "ctx", ctx_size, partner) for partner, data in zip(far, far_blocks)]
    along = swap(jnp.stack([along, across[1]]), "ctx", ctx_size, 2)
    moved += [across, along, own]
    own_heads = pl.pallas_call(
        functools.partial(packed_attention_kernel, far, rows),
        out_shape=jax.ShapeDtypeStruct((heads, rows, HEAD), q.dtype),
        in_specs=[vmem] * len(moved),
        out_specs=vmem,
        compiler_params=kernel_params(),
        cost_estimate=pl.CostEstimate(
            flops=4 * rows * rows * heads * heads * HEAD,
            bytes_accessed=8 * rows * heads * HEAD,
            transcendentals=rows * rows * heads * heads,
        ),
        name="self_attention",
    )(*moved)
    back = lax.all_to_all(own_heads, "ctx", split_axis=0, concat_axis=0, tiled=True)
    return back, pair, (pair, moved)


def shared_attention(q, k, v, ctx_size):
    rows, width = q.shape
    heads = width // HEAD
    parts = ctx_size // heads
    piece = rows // parts
    query = jnp.transpose(q.reshape(parts, piece, heads, HEAD), (2, 0, 1, 3)).reshape(
        ctx_size, piece, HEAD
    )
    key = jnp.repeat(jnp.transpose(k.reshape(rows, heads, HEAD), (1, 0, 2)), parts, axis=0)
    value = jnp.repeat(jnp.transpose(v.reshape(rows, heads, HEAD), (1, 0, 2)), parts, axis=0)
    packed = jnp.concatenate([query, key, value], axis=1)
    moved = lax.all_to_all(packed, "ctx", split_axis=0, concat_axis=0, tiled=True)
    query = moved[:, :piece].reshape(ctx_size * piece, HEAD)
    key = moved[:, piece : piece + rows].reshape(ctx_size * rows, HEAD)
    value = moved[:, piece + rows :].reshape(ctx_size * rows, HEAD)
    own = pl.pallas_call(
        attention_kernel,
        out_shape=jax.ShapeDtypeStruct((ctx_size * piece, HEAD), q.dtype),
        grid=(ctx_size * piece // rows,),
        in_specs=[
            pl.BlockSpec((rows, HEAD), lambda i: (i, 0)),
            pl.BlockSpec((ctx_size * rows, HEAD), lambda i: (0, 0)),
            pl.BlockSpec((ctx_size * rows, HEAD), lambda i: (0, 0)),
        ],
        out_specs=pl.BlockSpec((rows, HEAD), lambda i: (i, 0)),
        compiler_params=kernel_params(),
        name="self_attention",
    )(query, key, value)
    back = lax.all_to_all(
        own.reshape(ctx_size, piece, HEAD), "ctx", split_axis=0, concat_axis=0, tiled=True
    )
    return back.reshape(heads, rows, HEAD)


def body(view_count, ctx_size, q_self, k_self, v_self, q_cross, k_cross, v_cross):
    _, rows, width = q_self.shape
    heads = width // HEAD
    if ctx_size == heads == 8:
        o_self, pair, after = split_attention(
            q_self[0], k_self[0], v_self[0], k_cross[0], v_cross[0], ctx_size
        )
    else:
        o_self = shared_attention(q_self[0], k_self[0], v_self[0], ctx_size)
        pair = jnp.concatenate([k_cross[0], v_cross[0]], axis=0)
        after = [pair] * (view_count.bit_length() - 1)
    pairs = gather_views(pair, view_count, *after)
    vmem = pl.BlockSpec(memory_space=pltpu.VMEM)
    out = pl.pallas_call(
        functools.partial(cross_kernel, heads),
        out_shape=jax.ShapeDtypeStruct((rows, width), q_self.dtype),
        in_specs=[vmem] * (2 + view_count),
        out_specs=vmem,
        compiler_params=kernel_params(),
        name="cross_view",
    )(o_self, q_cross[0], *pairs)
    return out[None]


def solution(mesh):
    spec = P("view", "ctx", None)
    return jax.shard_map(
        functools.partial(body, mesh.shape["view"], mesh.shape["ctx"]),
        mesh=mesh,
        in_specs=(spec,) * 6,
        out_specs=spec,
        check_vma=False,
    )
```

```python
import functools
import math

import jax
import jax.numpy as jnp
from jax import lax
from jax.experimental import pallas as pl
from jax.experimental.pallas import tpu as pltpu
from jax.sharding import PartitionSpec as P

HEAD = 128
SCALE = 1.0 / math.sqrt(HEAD)
EXP2_SCALE = SCALE * math.log2(math.e)
MIB = 1024 * 1024


def pack_kernel(partners, q_ref, k_ref, v_ref, kc_ref, vc_ref, *refs):
    block_refs, pair_ref, sems = refs[: len(partners)], refs[-2], refs[-1]
    rows = q_ref.shape[0]
    me = lax.axis_index("ctx")
    copies = []

    def start(source, target):
        copy = pltpu.make_async_copy(source, target, sems.at[len(copies)])
        copy.start()
        copies.append(copy)

    for partner, block_ref in zip(partners, block_refs):
        lanes = pl.ds(pl.multiple_of((me ^ partner) * HEAD, HEAD), HEAD)
        for part, source in enumerate((q_ref, k_ref, v_ref)):
            start(source.at[:, lanes], block_ref.at[pl.ds(part * rows, rows)])
    for part, source in enumerate((kc_ref, vc_ref)):
        start(source, pair_ref.at[pl.ds(part * rows, rows)])
    for copy in copies:
        copy.wait()


def attend(query, keys, values):
    scores = lax.dot_general(
        query, keys, (((1,), (1,)), ((), ())), preferred_element_type=jnp.float32
    )
    row_max = jnp.max(scores, axis=-1, keepdims=True)
    weights_raw = jnp.exp2((scores - row_max) * EXP2_SCALE).astype(jnp.bfloat16)
    values_ones = jnp.concatenate([values, jnp.ones_like(values)], axis=1)
    mixed = jnp.dot(weights_raw, values_ones, preferred_element_type=jnp.float32)
    return (mixed[:, :HEAD] / mixed[:, HEAD:]).astype(jnp.bfloat16)


def packed_attention_kernel(partners, rows, group, *refs):
    *in_refs, out_ref = refs
    me = lax.axis_index("ctx")
    keys = jnp.concatenate([ref[rows : 2 * rows] for ref in in_refs], axis=0)
    values = jnp.concatenate([ref[2 * rows : 3 * rows] for ref in in_refs], axis=0)
    for first in range(0, len(in_refs), group):
        query = jnp.concatenate([ref[0:rows] for ref in in_refs[first : first + group]], axis=0)
        mixed = attend(query, keys, values)
        for i in range(group):
            out_ref[me ^ partners[first + i]] = mixed[i * rows : (i + 1) * rows]


def attention_kernel(q_ref, k_ref, v_ref, out_ref):
    out_ref[...] = attend(q_ref[...], k_ref[...], v_ref[...])


def cross_kernel(head_count, o_ref, q_ref, *refs):
    *pair_refs, out_ref = refs
    rows = q_ref.shape[0]
    for head in range(head_count):
        lanes = slice(head * HEAD, (head + 1) * HEAD)
        o_self = o_ref[head].astype(jnp.float32)
        query = (q_ref[:, lanes].astype(jnp.float32) + o_self).astype(jnp.bfloat16).astype(jnp.float32)
        scores = [
            jnp.sum(query * ref[0:rows, lanes].astype(jnp.float32), axis=-1, keepdims=True)
            for ref in pair_refs
        ]
        top = functools.reduce(jnp.maximum, scores)
        weights = [jnp.exp2((score - top) * EXP2_SCALE) for score in scores]
        inverse = 1.0 / sum(weights[1:], weights[0])
        mixed = None
        for weight, ref in zip(weights, pair_refs):
            rounded = (weight * inverse).astype(jnp.bfloat16).astype(jnp.float32)
            term = rounded * ref[rows : 2 * rows, lanes].astype(jnp.float32)
            mixed = term if mixed is None else mixed + term
        o_cross = mixed.astype(jnp.bfloat16).astype(jnp.float32)
        out_ref[:, lanes] = (o_self + o_cross).astype(jnp.bfloat16)


def kernel_params(grant=32):
    return pltpu.CompilerParams(vmem_limit_bytes=grant * MIB)


def swap(array, axis_name, axis_size, partner):
    return lax.ppermute(array, axis_name, [(i, i ^ partner) for i in range(axis_size)])


def gather_views(array, view_count, *after):
    gathered = [array]
    step = view_count // 2
    for earlier in after:
        gathered, _ = lax.optimization_barrier((gathered, earlier))
        gathered += [swap(block, "view", view_count, step) for block in gathered]
        step //= 2
    return gathered


def split_attention(q, k, v, k_cross, v_cross, ctx_size):
    rows, width = q.shape
    heads = width // HEAD
    partners = (3, 7, 6, 2, 5, 4, 1, 0)
    vmem = pl.BlockSpec(memory_space=pltpu.VMEM)
    hbm = pl.BlockSpec(memory_space=pltpu.HBM)
    sources = [pltpu.with_memory_space_constraint(x, pltpu.HBM) for x in (q, k, v, k_cross, v_cross)]
    block = jax.ShapeDtypeStruct((3 * rows, HEAD), q.dtype)
    *blocks, pair = pl.pallas_call(
        functools.partial(pack_kernel, partners),
        out_shape=[block] * heads + [jax.ShapeDtypeStruct((2 * rows, width), q.dtype)],
        in_specs=[hbm] * 5,
        out_specs=[vmem] * (heads + 1),
        scratch_shapes=[pltpu.SemaphoreType.DMA((3 * heads + 2,))],
        compiler_params=kernel_params(),
        name="pack_qkv",
    )(*sources)
    moved = [
        swap(data, "ctx", ctx_size, partner) if partner else data
        for partner, data in zip(partners, blocks)
    ]
    own = pl.pallas_call(
        functools.partial(packed_attention_kernel, partners, rows, max(heads // 4, 1)),
        out_shape=jax.ShapeDtypeStruct((heads, rows, HEAD), q.dtype),
        in_specs=[vmem] * heads,
        out_specs=vmem,
        compiler_params=kernel_params(),
        cost_estimate=pl.CostEstimate(
            flops=4 * rows * rows * heads * heads * HEAD,
            bytes_accessed=8 * rows * heads * HEAD,
            transcendentals=rows * rows * heads * heads,
        ),
        name="self_attention",
    )(*moved)
    back = lax.all_to_all(own, "ctx", split_axis=0, concat_axis=0, tiled=True)
    return back, pair, (pair, moved[:4])


def shared_attention(q, k, v, ctx_size):
    rows, width = q.shape
    heads = width // HEAD
    parts = ctx_size // heads
    piece = rows // parts
    query = jnp.transpose(q.reshape(parts, piece, heads, HEAD), (2, 0, 1, 3)).reshape(
        ctx_size, piece, HEAD
    )
    key = jnp.repeat(jnp.transpose(k.reshape(rows, heads, HEAD), (1, 0, 2)), parts, axis=0)
    value = jnp.repeat(jnp.transpose(v.reshape(rows, heads, HEAD), (1, 0, 2)), parts, axis=0)
    packed = jnp.concatenate([query, key, value], axis=1)
    moved = lax.all_to_all(packed, "ctx", split_axis=0, concat_axis=0, tiled=True)
    query = moved[:, :piece].reshape(ctx_size * piece, HEAD)
    key = moved[:, piece : piece + rows].reshape(ctx_size * rows, HEAD)
    value = moved[:, piece + rows :].reshape(ctx_size * rows, HEAD)
    own = pl.pallas_call(
        attention_kernel,
        out_shape=jax.ShapeDtypeStruct((ctx_size * piece, HEAD), q.dtype),
        grid=(ctx_size * piece // rows,),
        in_specs=[
            pl.BlockSpec((rows, HEAD), lambda i: (i, 0)),
            pl.BlockSpec((ctx_size * rows, HEAD), lambda i: (0, 0)),
            pl.BlockSpec((ctx_size * rows, HEAD), lambda i: (0, 0)),
        ],
        out_specs=pl.BlockSpec((rows, HEAD), lambda i: (i, 0)),
        compiler_params=kernel_params(),
        name="self_attention",
    )(query, key, value)
    back = lax.all_to_all(
        own.reshape(ctx_size, piece, HEAD), "ctx", split_axis=0, concat_axis=0, tiled=True
    )
    return back.reshape(heads, rows, HEAD)


def body(view_count, ctx_size, q_self, k_self, v_self, q_cross, k_cross, v_cross):
    _, rows, width = q_self.shape
    heads = width // HEAD
    if ctx_size == heads == 8:
        o_self, pair, after = split_attention(
            q_self[0], k_self[0], v_self[0], k_cross[0], v_cross[0], ctx_size
        )
    else:
        o_self = shared_attention(q_self[0], k_self[0], v_self[0], ctx_size)
        pair = jnp.concatenate([k_cross[0], v_cross[0]], axis=0)
        after = [pair] * (view_count.bit_length() - 1)
    pairs = gather_views(pair, view_count, *after)
    vmem = pl.BlockSpec(memory_space=pltpu.VMEM)
    out = pl.pallas_call(
        functools.partial(cross_kernel, heads),
        out_shape=jax.ShapeDtypeStruct((rows, width), q_self.dtype),
        in_specs=[vmem] * (2 + view_count),
        out_specs=vmem,
        compiler_params=kernel_params(),
        name="cross_view",
    )(o_self, q_cross[0], *pairs)
    return out[None]


def solution(mesh):
    spec = P("view", "ctx", None)
    return jax.shard_map(
        functools.partial(body, mesh.shape["view"], mesh.shape["ctx"]),
        mesh=mesh,
        in_specs=(spec,) * 6,
        out_specs=spec,
        check_vma=False,
    )
```

```python
import functools
import math

import jax
import jax.numpy as jnp
from jax import lax
from jax.experimental import pallas as pl
from jax.experimental.pallas import tpu as pltpu
from jax.sharding import PartitionSpec as P

HEAD = 128
SCALE = 1.0 / math.sqrt(HEAD)
EXP2_SCALE = SCALE * math.log2(math.e)
MIB = 1024 * 1024


def pack_kernel(partners, q_ref, k_ref, v_ref, kc_ref, vc_ref, *refs):
    *far_refs, near_ref, pair_ref, sems = refs
    rows = q_ref.shape[0]
    group = near_ref.shape[0]
    me = lax.axis_index("ctx")
    copies = []

    def start(source, target):
        copy = pltpu.make_async_copy(source, target, sems.at[len(copies)])
        copy.start()
        copies.append(copy)

    def pack(head, target):
        lanes = pl.ds(pl.multiple_of(head * HEAD, HEAD), HEAD)
        for part, source in enumerate((q_ref, k_ref, v_ref)):
            start(source.at[:, lanes], target.at[pl.ds(part * rows, rows)])

    for partner, far_ref in zip(partners, far_refs):
        pack(me ^ partner, far_ref)
    for part, source in enumerate((kc_ref, vc_ref)):
        start(source, pair_ref.at[pl.ds(part * rows, rows)])
    for member in range(group):
        pack((me // group) * group + member, near_ref.at[member])
    for copy in copies:
        copy.wait()


def attend(query, keys, values):
    scores = lax.dot_general(
        query, keys, (((1,), (1,)), ((), ())), preferred_element_type=jnp.float32
    )
    row_max = jnp.max(scores, axis=-1, keepdims=True)
    weights_raw = jnp.exp2((scores - row_max) * EXP2_SCALE).astype(jnp.bfloat16)
    values_ones = jnp.concatenate([values, jnp.ones_like(values)], axis=1)
    mixed = jnp.dot(weights_raw, values_ones, preferred_element_type=jnp.float32)
    return (mixed[:, :HEAD] / mixed[:, HEAD:]).astype(jnp.bfloat16)


def packed_attention_kernel(partners, rows, *refs):
    *far_refs, near_ref, out_ref = refs
    group = near_ref.shape[0]
    me = lax.axis_index("ctx")
    blocks = [(me ^ partner, ref) for partner, ref in zip(partners, far_refs)]
    blocks += [((me // group) * group + i, near_ref.at[i]) for i in range(group)]
    keys = jnp.concatenate([ref[rows : 2 * rows] for _, ref in blocks], axis=0)
    values = jnp.concatenate([ref[2 * rows : 3 * rows] for _, ref in blocks], axis=0)
    for first in range(0, len(blocks), 2):
        chunk = blocks[first : first + 2]
        query = jnp.concatenate([ref[0:rows] for _, ref in chunk], axis=0)
        mixed = attend(query, keys, values)
        for i, (source, _) in enumerate(chunk):
            out_ref[source] = mixed[i * rows : (i + 1) * rows]


def attention_kernel(q_ref, k_ref, v_ref, out_ref):
    out_ref[...] = attend(q_ref[...], k_ref[...], v_ref[...])


def cross_kernel(head_count, o_ref, q_ref, *refs):
    *pair_refs, out_ref = refs
    rows = q_ref.shape[0]
    for head in range(head_count):
        lanes = slice(head * HEAD, (head + 1) * HEAD)
        o_self = o_ref[head].astype(jnp.float32)
        query = (q_ref[:, lanes].astype(jnp.float32) + o_self).astype(jnp.bfloat16).astype(jnp.float32)
        scores = [
            jnp.sum(query * ref[0:rows, lanes].astype(jnp.float32), axis=-1, keepdims=True)
            for ref in pair_refs
        ]
        top = functools.reduce(jnp.maximum, scores)
        weights = [jnp.exp2((score - top) * EXP2_SCALE) for score in scores]
        inverse = 1.0 / sum(weights[1:], weights[0])
        mixed = None
        for weight, ref in zip(weights, pair_refs):
            rounded = (weight * inverse).astype(jnp.bfloat16).astype(jnp.float32)
            term = rounded * ref[rows : 2 * rows, lanes].astype(jnp.float32)
            mixed = term if mixed is None else mixed + term
        o_cross = mixed.astype(jnp.bfloat16).astype(jnp.float32)
        out_ref[:, lanes] = (o_self + o_cross).astype(jnp.bfloat16)


def kernel_params(grant=32):
    return pltpu.CompilerParams(vmem_limit_bytes=grant * MIB)


def swap(array, axis_name, axis_size, partner):
    return lax.ppermute(array, axis_name, [(i, i ^ partner) for i in range(axis_size)])


def split_attention(q, k, v, k_cross, v_cross, ctx_size, view_count):
    rows, width = q.shape
    heads = width // HEAD
    group = ctx_size // 2
    partners = tuple(range(ctx_size - 1, group - 1, -1))
    vmem = pl.BlockSpec(memory_space=pltpu.VMEM)
    hbm = pl.BlockSpec(memory_space=pltpu.HBM)
    sources = [pltpu.with_memory_space_constraint(x, pltpu.HBM) for x in (q, k, v, k_cross, v_cross)]
    *far, near, pair = pl.pallas_call(
        functools.partial(pack_kernel, partners),
        out_shape=[jax.ShapeDtypeStruct((3 * rows, HEAD), q.dtype)] * len(partners)
        + [
            jax.ShapeDtypeStruct((group, 3 * rows, HEAD), q.dtype),
            jax.ShapeDtypeStruct((2 * rows, width), q.dtype),
        ],
        in_specs=[hbm] * 5,
        out_specs=[vmem] * (len(partners) + 2),
        scratch_shapes=[pltpu.SemaphoreType.DMA((3 * heads + 2,))],
        compiler_params=kernel_params(),
        name="pack_qkv",
    )(*sources)
    far = [swap(data, "ctx", ctx_size, partner) for partner, data in zip(partners, far)]
    mate = swap(pair, "view", view_count, 1)
    near, _ = lax.optimization_barrier((near, mate))
    near = lax.all_to_all(
        near,
        "ctx",
        split_axis=0,
        concat_axis=0,
        tiled=True,
        axis_index_groups=[list(range(group)), list(range(group, ctx_size))],
    )
    own = pl.pallas_call(
        functools.partial(packed_attention_kernel, partners, rows),
        out_shape=jax.ShapeDtypeStruct((heads, rows, HEAD), q.dtype),
        in_specs=[vmem] * (len(partners) + 1),
        out_specs=vmem,
        compiler_params=kernel_params(),
        cost_estimate=pl.CostEstimate(
            flops=4 * rows * rows * heads * heads * HEAD,
            bytes_accessed=8 * rows * heads * HEAD,
            transcendentals=rows * rows * heads * heads,
        ),
        name="self_attention",
    )(*far, near)
    back = lax.all_to_all(own, "ctx", split_axis=0, concat_axis=0, tiled=True)
    return back, [pair, mate], [near, far[0]]


def shared_attention(q, k, v, ctx_size):
    rows, width = q.shape
    heads = width // HEAD
    parts = ctx_size // heads
    piece = rows // parts
    query = jnp.transpose(q.reshape(parts, piece, heads, HEAD), (2, 0, 1, 3)).reshape(
        ctx_size, piece, HEAD
    )
    key = jnp.repeat(jnp.transpose(k.reshape(rows, heads, HEAD), (1, 0, 2)), parts, axis=0)
    value = jnp.repeat(jnp.transpose(v.reshape(rows, heads, HEAD), (1, 0, 2)), parts, axis=0)
    packed = jnp.concatenate([query, key, value], axis=1)
    moved = lax.all_to_all(packed, "ctx", split_axis=0, concat_axis=0, tiled=True)
    query = moved[:, :piece].reshape(ctx_size * piece, HEAD)
    key = moved[:, piece : piece + rows].reshape(ctx_size * rows, HEAD)
    value = moved[:, piece + rows :].reshape(ctx_size * rows, HEAD)
    own = pl.pallas_call(
        attention_kernel,
        out_shape=jax.ShapeDtypeStruct((ctx_size * piece, HEAD), q.dtype),
        grid=(ctx_size * piece // rows,),
        in_specs=[
            pl.BlockSpec((rows, HEAD), lambda i: (i, 0)),
            pl.BlockSpec((ctx_size * rows, HEAD), lambda i: (0, 0)),
            pl.BlockSpec((ctx_size * rows, HEAD), lambda i: (0, 0)),
        ],
        out_specs=pl.BlockSpec((rows, HEAD), lambda i: (i, 0)),
        compiler_params=kernel_params(),
        name="self_attention",
    )(query, key, value)
    back = lax.all_to_all(
        own.reshape(ctx_size, piece, HEAD), "ctx", split_axis=0, concat_axis=0, tiled=True
    )
    return back.reshape(heads, rows, HEAD)


def body(view_count, ctx_size, q_self, k_self, v_self, q_cross, k_cross, v_cross):
    _, rows, width = q_self.shape
    heads = width // HEAD
    if ctx_size == heads == 8:
        o_self, (pair, mate), after = split_attention(
            q_self[0], k_self[0], v_self[0], k_cross[0], v_cross[0], ctx_size, view_count
        )
    else:
        o_self = shared_attention(q_self[0], k_self[0], v_self[0], ctx_size)
        pair = after = jnp.concatenate([k_cross[0], v_cross[0]], axis=0)
        mate = swap(pair, "view", view_count, 1)
    far = swap(pair, "view", view_count, 2)
    far, _ = lax.optimization_barrier((far, after))
    pairs = [pair, mate, far, swap(far, "view", view_count, 1)]
    vmem = pl.BlockSpec(memory_space=pltpu.VMEM)
    out = pl.pallas_call(
        functools.partial(cross_kernel, heads),
        out_shape=jax.ShapeDtypeStruct((rows, width), q_self.dtype),
        in_specs=[vmem] * (2 + view_count),
        out_specs=vmem,
        compiler_params=kernel_params(),
        name="cross_view",
    )(o_self, q_cross[0], *pairs)
    return out[None]


def solution(mesh):
    spec = P("view", "ctx", None)
    return jax.shard_map(
        functools.partial(body, mesh.shape["view"], mesh.shape["ctx"]),
        mesh=mesh,
        in_specs=(spec,) * 6,
        out_specs=spec,
        check_vma=False,
    )
```

```python
import functools
import math

import jax
import jax.numpy as jnp
from jax import lax
from jax.experimental import pallas as pl
from jax.experimental.pallas import tpu as pltpu
from jax.sharding import PartitionSpec as P

HEAD = 128
SCALE = 1.0 / math.sqrt(HEAD)
EXP2_SCALE = SCALE * math.log2(math.e)
MIB = 1024 * 1024


def pack_kernel(partners, q_ref, k_ref, v_ref, kc_ref, vc_ref, *refs):
    block_refs, pair_ref, sems = refs[: len(partners)], refs[-2], refs[-1]
    rows = q_ref.shape[0]
    me = lax.axis_index("ctx")
    copies = []

    def start(source, target):
        copy = pltpu.make_async_copy(source, target, sems.at[len(copies)])
        copy.start()
        copies.append(copy)

    for partner, block_ref in zip(partners, block_refs):
        lanes = pl.ds(pl.multiple_of((me ^ partner) * HEAD, HEAD), HEAD)
        for part, source in enumerate((q_ref, k_ref, v_ref)):
            start(source.at[:, lanes], block_ref.at[pl.ds(part * rows, rows)])
    for part, source in enumerate((kc_ref, vc_ref)):
        start(source, pair_ref.at[pl.ds(part * rows, rows)])
    for copy in copies:
        copy.wait()


def attend(query, keys, values):
    scores = lax.dot_general(
        query, keys, (((1,), (1,)), ((), ())), preferred_element_type=jnp.float32
    )
    row_max = jnp.max(scores, axis=-1, keepdims=True)
    weights_raw = jnp.exp2((scores - row_max) * EXP2_SCALE).astype(jnp.bfloat16)
    values_ones = jnp.concatenate([values, jnp.ones_like(values)], axis=1)
    mixed = jnp.dot(weights_raw, values_ones, preferred_element_type=jnp.float32)
    return (mixed[:, :HEAD] / mixed[:, HEAD:]).astype(jnp.bfloat16)


def packed_attention_kernel(partners, rows, group, *refs):
    *in_refs, out_ref = refs
    me = lax.axis_index("ctx")
    keys = jnp.concatenate([ref[rows : 2 * rows] for ref in in_refs], axis=0)
    values = jnp.concatenate([ref[2 * rows : 3 * rows] for ref in in_refs], axis=0)
    for first in range(0, len(in_refs), group):
        query = jnp.concatenate([ref[0:rows] for ref in in_refs[first : first + group]], axis=0)
        mixed = attend(query, keys, values)
        for i in range(group):
            out_ref[me ^ partners[first + i]] = mixed[i * rows : (i + 1) * rows]


def attention_kernel(q_ref, k_ref, v_ref, out_ref):
    out_ref[...] = attend(q_ref[...], k_ref[...], v_ref[...])


def cross_kernel(head_count, o_ref, q_ref, *refs):
    *pair_refs, out_ref = refs
    rows = q_ref.shape[0]
    for head in range(head_count):
        lanes = slice(head * HEAD, (head + 1) * HEAD)
        o_self = o_ref[head].astype(jnp.float32)
        query = (q_ref[:, lanes].astype(jnp.float32) + o_self).astype(jnp.bfloat16).astype(jnp.float32)
        scores = [
            jnp.sum(query * ref[0:rows, lanes].astype(jnp.float32), axis=-1, keepdims=True)
            for ref in pair_refs
        ]
        top = functools.reduce(jnp.maximum, scores)
        weights = [jnp.exp2((score - top) * EXP2_SCALE) for score in scores]
        inverse = 1.0 / sum(weights[1:], weights[0])
        mixed = None
        for weight, ref in zip(weights, pair_refs):
            rounded = (weight * inverse).astype(jnp.bfloat16).astype(jnp.float32)
            term = rounded * ref[rows : 2 * rows, lanes].astype(jnp.float32)
            mixed = term if mixed is None else mixed + term
        o_cross = mixed.astype(jnp.bfloat16).astype(jnp.float32)
        out_ref[:, lanes] = (o_self + o_cross).astype(jnp.bfloat16)


def kernel_params(grant=32):
    return pltpu.CompilerParams(vmem_limit_bytes=grant * MIB)


def swap(array, axis_name, axis_size, partner):
    return lax.ppermute(array, axis_name, [(i, i ^ partner) for i in range(axis_size)])


def gather_views(array, view_count, *after):
    gathered = [array]
    step = view_count // 2
    for earlier in after:
        gathered, _ = lax.optimization_barrier((gathered, earlier))
        gathered += [swap(block, "view", view_count, step) for block in gathered]
        step //= 2
    return gathered


def split_attention(q, k, v, k_cross, v_cross, ctx_size):
    rows, width = q.shape
    heads = width // HEAD
    partners = (3, 2, 7, 6, 5, 4, 1, 0)
    vmem = pl.BlockSpec(memory_space=pltpu.VMEM)
    hbm = pl.BlockSpec(memory_space=pltpu.HBM)
    sources = [pltpu.with_memory_space_constraint(x, pltpu.HBM) for x in (q, k, v, k_cross, v_cross)]
    block = jax.ShapeDtypeStruct((3 * rows, HEAD), q.dtype)
    *blocks, pair = pl.pallas_call(
        functools.partial(pack_kernel, partners),
        out_shape=[block] * heads + [jax.ShapeDtypeStruct((2 * rows, width), q.dtype)],
        in_specs=[hbm] * 5,
        out_specs=[vmem] * (heads + 1),
        scratch_shapes=[pltpu.SemaphoreType.DMA((3 * heads + 2,))],
        compiler_params=kernel_params(),
        name="pack_qkv",
    )(*sources)
    moved = [
        swap(data, "ctx", ctx_size, partner) if partner else data
        for partner, data in zip(partners, blocks)
    ]
    own = pl.pallas_call(
        functools.partial(packed_attention_kernel, partners, rows, max(heads // 4, 1)),
        out_shape=jax.ShapeDtypeStruct((heads, rows, HEAD), q.dtype),
        in_specs=[vmem] * heads,
        out_specs=vmem,
        compiler_params=kernel_params(),
        cost_estimate=pl.CostEstimate(
            flops=4 * rows * rows * heads * heads * HEAD,
            bytes_accessed=8 * rows * heads * HEAD,
            transcendentals=rows * rows * heads * heads,
        ),
        name="self_attention",
    )(*moved)
    back = lax.all_to_all(own, "ctx", split_axis=0, concat_axis=0, tiled=True)
    return back, pair, (pair, moved[:4])


def shared_attention(q, k, v, ctx_size):
    rows, width = q.shape
    heads = width // HEAD
    parts = ctx_size // heads
    piece = rows // parts
    query = jnp.transpose(q.reshape(parts, piece, heads, HEAD), (2, 0, 1, 3)).reshape(
        ctx_size, piece, HEAD
    )
    key = jnp.repeat(jnp.transpose(k.reshape(rows, heads, HEAD), (1, 0, 2)), parts, axis=0)
    value = jnp.repeat(jnp.transpose(v.reshape(rows, heads, HEAD), (1, 0, 2)), parts, axis=0)
    packed = jnp.concatenate([query, key, value], axis=1)
    moved = lax.all_to_all(packed, "ctx", split_axis=0, concat_axis=0, tiled=True)
    query = moved[:, :piece].reshape(ctx_size * piece, HEAD)
    key = moved[:, piece : piece + rows].reshape(ctx_size * rows, HEAD)
    value = moved[:, piece + rows :].reshape(ctx_size * rows, HEAD)
    own = pl.pallas_call(
        attention_kernel,
        out_shape=jax.ShapeDtypeStruct((ctx_size * piece, HEAD), q.dtype),
        grid=(ctx_size * piece // rows,),
        in_specs=[
            pl.BlockSpec((rows, HEAD), lambda i: (i, 0)),
            pl.BlockSpec((ctx_size * rows, HEAD), lambda i: (0, 0)),
            pl.BlockSpec((ctx_size * rows, HEAD), lambda i: (0, 0)),
        ],
        out_specs=pl.BlockSpec((rows, HEAD), lambda i: (i, 0)),
        compiler_params=kernel_params(),
        name="self_attention",
    )(query, key, value)
    back = lax.all_to_all(
        own.reshape(ctx_size, piece, HEAD), "ctx", split_axis=0, concat_axis=0, tiled=True
    )
    return back.reshape(heads, rows, HEAD)


def body(view_count, ctx_size, q_self, k_self, v_self, q_cross, k_cross, v_cross):
    _, rows, width = q_self.shape
    heads = width // HEAD
    if ctx_size == heads == 8:
        o_self, pair, after = split_attention(
            q_self[0], k_self[0], v_self[0], k_cross[0], v_cross[0], ctx_size
        )
    else:
        o_self = shared_attention(q_self[0], k_self[0], v_self[0], ctx_size)
        pair = jnp.concatenate([k_cross[0], v_cross[0]], axis=0)
        after = [pair] * (view_count.bit_length() - 1)
    pairs = gather_views(pair, view_count, *after)
    vmem = pl.BlockSpec(memory_space=pltpu.VMEM)
    out = pl.pallas_call(
        functools.partial(cross_kernel, heads),
        out_shape=jax.ShapeDtypeStruct((rows, width), q_self.dtype),
        in_specs=[vmem] * (2 + view_count),
        out_specs=vmem,
        compiler_params=kernel_params(),
        name="cross_view",
    )(o_self, q_cross[0], *pairs)
    return out[None]


def solution(mesh):
    spec = P("view", "ctx", None)
    return jax.shard_map(
        functools.partial(body, mesh.shape["view"], mesh.shape["ctx"]),
        mesh=mesh,
        in_specs=(spec,) * 6,
        out_specs=spec,
        check_vma=False,
    )
```

```python
import functools
import math

import jax
import jax.numpy as jnp
from jax import lax
from jax.experimental import pallas as pl
from jax.experimental.pallas import tpu as pltpu
from jax.sharding import PartitionSpec as P

HEAD = 128
SCALE = 1.0 / math.sqrt(HEAD)
EXP2_SCALE = SCALE * math.log2(math.e)
MIB = 1024 * 1024


def pack_kernel(far, q_ref, k_ref, v_ref, kc_ref, vc_ref, *refs):
    *far_refs, across_ref, along_ref, own_ref, pair_ref, sems = refs
    rows = q_ref.shape[0]
    me = lax.axis_index("ctx")
    copies = []

    def start(source, target):
        copy = pltpu.make_async_copy(source, target, sems.at[len(copies)])
        copy.start()
        copies.append(copy)

    blocks = list(zip(far, far_refs))
    blocks += [(1, across_ref.at[0]), (3, across_ref.at[1]), (2, along_ref), (0, own_ref)]
    for partner, target in blocks:
        lanes = pl.ds(pl.multiple_of((me ^ partner) * HEAD, HEAD), HEAD)
        for part, source in enumerate((q_ref, k_ref, v_ref)):
            start(source.at[:, lanes], target.at[pl.ds(part * rows, rows)])
    for part, source in enumerate((kc_ref, vc_ref)):
        start(source, pair_ref.at[pl.ds(part * rows, rows)])
    for copy in copies:
        copy.wait()


def attend(query, keys, values):
    scores = lax.dot_general(
        query, keys, (((1,), (1,)), ((), ())), preferred_element_type=jnp.float32
    )
    row_max = jnp.max(scores, axis=-1, keepdims=True)
    weights_raw = jnp.exp2((scores - row_max) * EXP2_SCALE).astype(jnp.bfloat16)
    values_ones = jnp.concatenate([values, jnp.ones_like(values)], axis=1)
    mixed = jnp.dot(weights_raw, values_ones, preferred_element_type=jnp.float32)
    return (mixed[:, :HEAD] / mixed[:, HEAD:]).astype(jnp.bfloat16)


def packed_attention_kernel(far, rows, *refs):
    *far_refs, across_ref, along_ref, own_ref, out_ref = refs
    me = lax.axis_index("ctx")
    blocks = list(zip(far, far_refs))
    blocks += [(0, own_ref), (1, across_ref.at[0]), (2, along_ref.at[0]), (3, along_ref.at[1])]
    keys = jnp.concatenate([ref[rows : 2 * rows] for _, ref in blocks], axis=0)
    values = jnp.concatenate([ref[2 * rows : 3 * rows] for _, ref in blocks], axis=0)
    for first in range(0, len(blocks), 2):
        chunk = blocks[first : first + 2]
        query = jnp.concatenate([ref[0:rows] for _, ref in chunk], axis=0)
        mixed = attend(query, keys, values)
        for i, (partner, _) in enumerate(chunk):
            out_ref[me ^ partner] = mixed[i * rows : (i + 1) * rows]


def attention_kernel(q_ref, k_ref, v_ref, out_ref):
    out_ref[...] = attend(q_ref[...], k_ref[...], v_ref[...])


def cross_kernel(head_count, o_ref, q_ref, *refs):
    *pair_refs, out_ref = refs
    rows = q_ref.shape[0]
    for head in range(head_count):
        lanes = slice(head * HEAD, (head + 1) * HEAD)
        o_self = o_ref[head].astype(jnp.float32)
        query = (q_ref[:, lanes].astype(jnp.float32) + o_self).astype(jnp.bfloat16).astype(jnp.float32)
        scores = [
            jnp.sum(query * ref[0:rows, lanes].astype(jnp.float32), axis=-1, keepdims=True)
            for ref in pair_refs
        ]
        top = functools.reduce(jnp.maximum, scores)
        weights = [jnp.exp2((score - top) * EXP2_SCALE) for score in scores]
        inverse = 1.0 / sum(weights[1:], weights[0])
        mixed = None
        for weight, ref in zip(weights, pair_refs):
            rounded = (weight * inverse).astype(jnp.bfloat16).astype(jnp.float32)
            term = rounded * ref[rows : 2 * rows, lanes].astype(jnp.float32)
            mixed = term if mixed is None else mixed + term
        o_cross = mixed.astype(jnp.bfloat16).astype(jnp.float32)
        out_ref[:, lanes] = (o_self + o_cross).astype(jnp.bfloat16)


def kernel_params(grant=32):
    return pltpu.CompilerParams(vmem_limit_bytes=grant * MIB)


def swap(array, axis_name, axis_size, partner):
    return lax.ppermute(array, axis_name, [(i, i ^ partner) for i in range(axis_size)])


def gather_views(array, view_count, *after):
    gathered = [array]
    step = view_count // 2
    for earlier in after:
        gathered, _ = lax.optimization_barrier((gathered, earlier))
        gathered += [swap(block, "view", view_count, step) for block in gathered]
        step //= 2
    return gathered


def split_attention(q, k, v, k_cross, v_cross, ctx_size):
    rows, width = q.shape
    heads = width // HEAD
    far = (7, 6, 5, 4)
    vmem = pl.BlockSpec(memory_space=pltpu.VMEM)
    hbm = pl.BlockSpec(memory_space=pltpu.HBM)
    sources = [pltpu.with_memory_space_constraint(x, pltpu.HBM) for x in (q, k, v, k_cross, v_cross)]
    block = jax.ShapeDtypeStruct((3 * rows, HEAD), q.dtype)
    two_blocks = jax.ShapeDtypeStruct((2, 3 * rows, HEAD), q.dtype)
    *far_blocks, across, along, own, pair = pl.pallas_call(
        functools.partial(pack_kernel, far),
        out_shape=[block] * len(far)
        + [two_blocks, block, block, jax.ShapeDtypeStruct((2 * rows, width), q.dtype)],
        in_specs=[hbm] * 5,
        out_specs=[vmem] * (len(far) + 4),
        scratch_shapes=[pltpu.SemaphoreType.DMA((3 * heads + 2,))],
        compiler_params=kernel_params(),
        name="pack_qkv",
    )(*sources)
    across = swap(across, "ctx", ctx_size, 1)
    moved = [swap(data, "ctx", ctx_size, partner) for partner, data in zip(far, far_blocks)]
    along = swap(jnp.stack([along, across[1]]), "ctx", ctx_size, 2)
    moved += [across, along, own]
    own_heads = pl.pallas_call(
        functools.partial(packed_attention_kernel, far, rows),
        out_shape=jax.ShapeDtypeStruct((heads, rows, HEAD), q.dtype),
        in_specs=[vmem] * len(moved),
        out_specs=vmem,
        compiler_params=kernel_params(),
        cost_estimate=pl.CostEstimate(
            flops=4 * rows * rows * heads * heads * HEAD,
            bytes_accessed=8 * rows * heads * HEAD,
            transcendentals=rows * rows * heads * heads,
        ),
        name="self_attention",
    )(*moved)
    back = lax.all_to_all(own_heads, "ctx", split_axis=0, concat_axis=0, tiled=True)
    return back, pair, (pair, moved[:2])


def shared_attention(q, k, v, ctx_size):
    rows, width = q.shape
    heads = width // HEAD
    parts = ctx_size // heads
    piece = rows // parts
    query = jnp.transpose(q.reshape(parts, piece, heads, HEAD), (2, 0, 1, 3)).reshape(
        ctx_size, piece, HEAD
    )
    key = jnp.repeat(jnp.transpose(k.reshape(rows, heads, HEAD), (1, 0, 2)), parts, axis=0)
    value = jnp.repeat(jnp.transpose(v.reshape(rows, heads, HEAD), (1, 0, 2)), parts, axis=0)
    packed = jnp.concatenate([query, key, value], axis=1)
    moved = lax.all_to_all(packed, "ctx", split_axis=0, concat_axis=0, tiled=True)
    query = moved[:, :piece].reshape(ctx_size * piece, HEAD)
    key = moved[:, piece : piece + rows].reshape(ctx_size * rows, HEAD)
    value = moved[:, piece + rows :].reshape(ctx_size * rows, HEAD)
    own = pl.pallas_call(
        attention_kernel,
        out_shape=jax.ShapeDtypeStruct((ctx_size * piece, HEAD), q.dtype),
        grid=(ctx_size * piece // rows,),
        in_specs=[
            pl.BlockSpec((rows, HEAD), lambda i: (i, 0)),
            pl.BlockSpec((ctx_size * rows, HEAD), lambda i: (0, 0)),
            pl.BlockSpec((ctx_size * rows, HEAD), lambda i: (0, 0)),
        ],
        out_specs=pl.BlockSpec((rows, HEAD), lambda i: (i, 0)),
        compiler_params=kernel_params(),
        name="self_attention",
    )(query, key, value)
    back = lax.all_to_all(
        own.reshape(ctx_size, piece, HEAD), "ctx", split_axis=0, concat_axis=0, tiled=True
    )
    return back.reshape(heads, rows, HEAD)


def body(view_count, ctx_size, q_self, k_self, v_self, q_cross, k_cross, v_cross):
    _, rows, width = q_self.shape
    heads = width // HEAD
    if ctx_size == heads == 8:
        o_self, pair, after = split_attention(
            q_self[0], k_self[0], v_self[0], k_cross[0], v_cross[0], ctx_size
        )
    else:
        o_self = shared_attention(q_self[0], k_self[0], v_self[0], ctx_size)
        pair = jnp.concatenate([k_cross[0], v_cross[0]], axis=0)
        after = [pair] * (view_count.bit_length() - 1)
    pairs = gather_views(pair, view_count, *after)
    vmem = pl.BlockSpec(memory_space=pltpu.VMEM)
    out = pl.pallas_call(
        functools.partial(cross_kernel, heads),
        out_shape=jax.ShapeDtypeStruct((rows, width), q_self.dtype),
        in_specs=[vmem] * (2 + view_count),
        out_specs=vmem,
        compiler_params=kernel_params(),
        name="cross_view",
    )(o_self, q_cross[0], *pairs)
    return out[None]


def solution(mesh):
    spec = P("view", "ctx", None)
    return jax.shard_map(
        functools.partial(body, mesh.shape["view"], mesh.shape["ctx"]),
        mesh=mesh,
        in_specs=(spec,) * 6,
        out_specs=spec,
        check_vma=False,
    )
```

```python
import functools
import math

import jax
import jax.numpy as jnp
from jax import lax
from jax.experimental import pallas as pl
from jax.experimental.pallas import tpu as pltpu
from jax.sharding import PartitionSpec as P

HEAD = 128
SCALE = 1.0 / math.sqrt(HEAD)
EXP2_SCALE = SCALE * math.log2(math.e)
MIB = 1024 * 1024


def pack_kernel(partners, q_ref, k_ref, v_ref, kc_ref, vc_ref, *refs):
    block_refs, pair_ref, sems = refs[: len(partners)], refs[-2], refs[-1]
    rows = q_ref.shape[0]
    me = lax.axis_index("ctx")
    copies = []

    def start(source, target):
        copy = pltpu.make_async_copy(source, target, sems.at[len(copies)])
        copy.start()
        copies.append(copy)

    for partner, block_ref in zip(partners, block_refs):
        lanes = pl.ds(pl.multiple_of((me ^ partner) * HEAD, HEAD), HEAD)
        for part, source in enumerate((q_ref, k_ref, v_ref)):
            start(source.at[:, lanes], block_ref.at[pl.ds(part * rows, rows)])
    for part, source in enumerate((kc_ref, vc_ref)):
        start(source, pair_ref.at[pl.ds(part * rows, rows)])
    for copy in copies:
        copy.wait()


def attend(query, keys, values):
    scores = lax.dot_general(
        query, keys, (((1,), (1,)), ((), ())), preferred_element_type=jnp.float32
    )
    row_max = jnp.max(scores, axis=-1, keepdims=True)
    weights_raw = jnp.exp2((scores - row_max) * EXP2_SCALE).astype(jnp.bfloat16)
    values_ones = jnp.concatenate([values, jnp.ones_like(values)], axis=1)
    mixed = jnp.dot(weights_raw, values_ones, preferred_element_type=jnp.float32)
    return (mixed[:, :HEAD] / mixed[:, HEAD:]).astype(jnp.bfloat16)


def packed_attention_kernel(partners, rows, group, *refs):
    *in_refs, out_ref = refs
    me = lax.axis_index("ctx")
    keys = jnp.concatenate([ref[rows : 2 * rows] for ref in in_refs], axis=0)
    values = jnp.concatenate([ref[2 * rows : 3 * rows] for ref in in_refs], axis=0)
    for first in range(0, len(in_refs), group):
        query = jnp.concatenate([ref[0:rows] for ref in in_refs[first : first + group]], axis=0)
        mixed = attend(query, keys, values)
        for i in range(group):
            out_ref[me ^ partners[first + i]] = mixed[i * rows : (i + 1) * rows]


def attention_kernel(q_ref, k_ref, v_ref, out_ref):
    out_ref[...] = attend(q_ref[...], k_ref[...], v_ref[...])


def cross_kernel(head_count, o_ref, q_ref, *refs):
    *pair_refs, out_ref = refs
    rows = q_ref.shape[0]
    for head in range(head_count):
        lanes = slice(head * HEAD, (head + 1) * HEAD)
        o_self = o_ref[head].astype(jnp.float32)
        query = (q_ref[:, lanes].astype(jnp.float32) + o_self).astype(jnp.bfloat16).astype(jnp.float32)
        scores = [
            jnp.sum(query * ref[0:rows, lanes].astype(jnp.float32), axis=-1, keepdims=True)
            for ref in pair_refs
        ]
        top = functools.reduce(jnp.maximum, scores)
        weights = [jnp.exp2((score - top) * EXP2_SCALE) for score in scores]
        inverse = 1.0 / sum(weights[1:], weights[0])
        mixed = None
        for weight, ref in zip(weights, pair_refs):
            rounded = (weight * inverse).astype(jnp.bfloat16).astype(jnp.float32)
            term = rounded * ref[rows : 2 * rows, lanes].astype(jnp.float32)
            mixed = term if mixed is None else mixed + term
        o_cross = mixed.astype(jnp.bfloat16).astype(jnp.float32)
        out_ref[:, lanes] = (o_self + o_cross).astype(jnp.bfloat16)


def kernel_params(grant=32):
    return pltpu.CompilerParams(vmem_limit_bytes=grant * MIB)


def swap(array, axis_name, axis_size, partner):
    return lax.ppermute(array, axis_name, [(i, i ^ partner) for i in range(axis_size)])


def gather_views(array, view_count, *after):
    gathered = [array]
    step = view_count // 2
    for earlier in after:
        gathered, _ = lax.optimization_barrier((gathered, earlier))
        gathered += [swap(block, "view", view_count, step) for block in gathered]
        step //= 2
    return gathered


def split_attention(q, k, v, k_cross, v_cross, ctx_size):
    rows, width = q.shape
    heads = width // HEAD
    partners = (3, 2, 1, 7, 6, 5, 4, 0)
    vmem = pl.BlockSpec(memory_space=pltpu.VMEM)
    hbm = pl.BlockSpec(memory_space=pltpu.HBM)
    sources = [pltpu.with_memory_space_constraint(x, pltpu.HBM) for x in (q, k, v, k_cross, v_cross)]
    block = jax.ShapeDtypeStruct((3 * rows, HEAD), q.dtype)
    *blocks, pair = pl.pallas_call(
        functools.partial(pack_kernel, partners),
        out_shape=[block] * heads + [jax.ShapeDtypeStruct((2 * rows, width), q.dtype)],
        in_specs=[hbm] * 5,
        out_specs=[vmem] * (heads + 1),
        scratch_shapes=[pltpu.SemaphoreType.DMA((3 * heads + 2,))],
        compiler_params=kernel_params(),
        name="pack_qkv",
    )(*sources)
    moved = [
        swap(data, "ctx", ctx_size, partner) if partner else data
        for partner, data in zip(partners, blocks)
    ]
    own = pl.pallas_call(
        functools.partial(packed_attention_kernel, partners, rows, max(heads // 4, 1)),
        out_shape=jax.ShapeDtypeStruct((heads, rows, HEAD), q.dtype),
        in_specs=[vmem] * heads,
        out_specs=vmem,
        compiler_params=kernel_params(),
        cost_estimate=pl.CostEstimate(
            flops=4 * rows * rows * heads * heads * HEAD,
            bytes_accessed=8 * rows * heads * HEAD,
            transcendentals=rows * rows * heads * heads,
        ),
        name="self_attention",
    )(*moved)
    back = lax.all_to_all(own, "ctx", split_axis=0, concat_axis=0, tiled=True)
    return back, pair, (pair, moved[:4])


def shared_attention(q, k, v, ctx_size):
    rows, width = q.shape
    heads = width // HEAD
    parts = ctx_size // heads
    piece = rows // parts
    query = jnp.transpose(q.reshape(parts, piece, heads, HEAD), (2, 0, 1, 3)).reshape(
        ctx_size, piece, HEAD
    )
    key = jnp.repeat(jnp.transpose(k.reshape(rows, heads, HEAD), (1, 0, 2)), parts, axis=0)
    value = jnp.repeat(jnp.transpose(v.reshape(rows, heads, HEAD), (1, 0, 2)), parts, axis=0)
    packed = jnp.concatenate([query, key, value], axis=1)
    moved = lax.all_to_all(packed, "ctx", split_axis=0, concat_axis=0, tiled=True)
    query = moved[:, :piece].reshape(ctx_size * piece, HEAD)
    key = moved[:, piece : piece + rows].reshape(ctx_size * rows, HEAD)
    value = moved[:, piece + rows :].reshape(ctx_size * rows, HEAD)
    own = pl.pallas_call(
        attention_kernel,
        out_shape=jax.ShapeDtypeStruct((ctx_size * piece, HEAD), q.dtype),
        grid=(ctx_size * piece // rows,),
        in_specs=[
            pl.BlockSpec((rows, HEAD), lambda i: (i, 0)),
            pl.BlockSpec((ctx_size * rows, HEAD), lambda i: (0, 0)),
            pl.BlockSpec((ctx_size * rows, HEAD), lambda i: (0, 0)),
        ],
        out_specs=pl.BlockSpec((rows, HEAD), lambda i: (i, 0)),
        compiler_params=kernel_params(),
        name="self_attention",
    )(query, key, value)
    back = lax.all_to_all(
        own.reshape(ctx_size, piece, HEAD), "ctx", split_axis=0, concat_axis=0, tiled=True
    )
    return back.reshape(heads, rows, HEAD)


def body(view_count, ctx_size, q_self, k_self, v_self, q_cross, k_cross, v_cross):
    _, rows, width = q_self.shape
    heads = width // HEAD
    if ctx_size == heads == 8:
        o_self, pair, after = split_attention(
            q_self[0], k_self[0], v_self[0], k_cross[0], v_cross[0], ctx_size
        )
    else:
        o_self = shared_attention(q_self[0], k_self[0], v_self[0], ctx_size)
        pair = jnp.concatenate([k_cross[0], v_cross[0]], axis=0)
        after = [pair] * (view_count.bit_length() - 1)
    pairs = gather_views(pair, view_count, *after)
    vmem = pl.BlockSpec(memory_space=pltpu.VMEM)
    out = pl.pallas_call(
        functools.partial(cross_kernel, heads),
        out_shape=jax.ShapeDtypeStruct((rows, width), q_self.dtype),
        in_specs=[vmem] * (2 + view_count),
        out_specs=vmem,
        compiler_params=kernel_params(),
        name="cross_view",
    )(o_self, q_cross[0], *pairs)
    return out[None]


def solution(mesh):
    spec = P("view", "ctx", None)
    return jax.shard_map(
        functools.partial(body, mesh.shape["view"], mesh.shape["ctx"]),
        mesh=mesh,
        in_specs=(spec,) * 6,
        out_specs=spec,
        check_vma=False,
    )
```

```python
import functools
import math

import jax
import jax.numpy as jnp
from jax import lax
from jax.experimental import pallas as pl
from jax.experimental.pallas import tpu as pltpu
from jax.sharding import PartitionSpec as P

HEAD = 128
SCALE = 1.0 / math.sqrt(HEAD)
EXP2_SCALE = SCALE * math.log2(math.e)
MIB = 1024 * 1024
PARTNERS = tuple(zip((7, 6, 5, 3, 4, 2, 1, 0), (3, 2, 1, 7, 6, 5, 4, 0)))


def partner_of(orders):
    core = lax.rem(lax.axis_index("view"), 2)
    first, second = orders
    return lax.axis_index("ctx") ^ (first + core * (second - first))


def pack_kernel(partners, q_ref, k_ref, v_ref, kc_ref, vc_ref, *refs):
    block_refs, pair_ref, sems = refs[: len(partners)], refs[-2], refs[-1]
    rows = q_ref.shape[0]
    copies = []

    def start(source, target):
        copy = pltpu.make_async_copy(source, target, sems.at[len(copies)])
        copy.start()
        copies.append(copy)

    for partner, block_ref in zip(partners, block_refs):
        lanes = pl.ds(pl.multiple_of(partner_of(partner) * HEAD, HEAD), HEAD)
        for part, source in enumerate((q_ref, k_ref, v_ref)):
            start(source.at[:, lanes], block_ref.at[pl.ds(part * rows, rows)])
    for part, source in enumerate((kc_ref, vc_ref)):
        start(source, pair_ref.at[pl.ds(part * rows, rows)])
    for copy in copies:
        copy.wait()


def attend(query, keys, values):
    scores = lax.dot_general(
        query, keys, (((1,), (1,)), ((), ())), preferred_element_type=jnp.float32
    )
    row_max = jnp.max(scores, axis=-1, keepdims=True)
    weights_raw = jnp.exp2((scores - row_max) * EXP2_SCALE).astype(jnp.bfloat16)
    values_ones = jnp.concatenate([values, jnp.ones_like(values)], axis=1)
    mixed = jnp.dot(weights_raw, values_ones, preferred_element_type=jnp.float32)
    return (mixed[:, :HEAD] / mixed[:, HEAD:]).astype(jnp.bfloat16)


def packed_attention_kernel(partners, rows, group, *refs):
    *in_refs, out_ref = refs
    keys = jnp.concatenate([ref[rows : 2 * rows] for ref in in_refs], axis=0)
    values = jnp.concatenate([ref[2 * rows : 3 * rows] for ref in in_refs], axis=0)
    for first in range(0, len(in_refs), group):
        query = jnp.concatenate([ref[0:rows] for ref in in_refs[first : first + group]], axis=0)
        mixed = attend(query, keys, values)
        for i in range(group):
            out_ref[partner_of(partners[first + i])] = mixed[i * rows : (i + 1) * rows]


def attention_kernel(q_ref, k_ref, v_ref, out_ref):
    out_ref[...] = attend(q_ref[...], k_ref[...], v_ref[...])


def cross_kernel(head_count, o_ref, q_ref, *refs):
    *pair_refs, out_ref = refs
    rows = q_ref.shape[0]
    for head in range(head_count):
        lanes = slice(head * HEAD, (head + 1) * HEAD)
        o_self = o_ref[head].astype(jnp.float32)
        query = (q_ref[:, lanes].astype(jnp.float32) + o_self).astype(jnp.bfloat16).astype(jnp.float32)
        scores = [
            jnp.sum(query * ref[0:rows, lanes].astype(jnp.float32), axis=-1, keepdims=True)
            for ref in pair_refs
        ]
        top = functools.reduce(jnp.maximum, scores)
        weights = [jnp.exp2((score - top) * EXP2_SCALE) for score in scores]
        inverse = 1.0 / sum(weights[1:], weights[0])
        mixed = None
        for weight, ref in zip(weights, pair_refs):
            rounded = (weight * inverse).astype(jnp.bfloat16).astype(jnp.float32)
            term = rounded * ref[rows : 2 * rows, lanes].astype(jnp.float32)
            mixed = term if mixed is None else mixed + term
        o_cross = mixed.astype(jnp.bfloat16).astype(jnp.float32)
        out_ref[:, lanes] = (o_self + o_cross).astype(jnp.bfloat16)


def kernel_params(grant=32):
    return pltpu.CompilerParams(vmem_limit_bytes=grant * MIB)


def swap(array, axis_name, axis_size, partner):
    return lax.ppermute(array, axis_name, [(i, i ^ partner) for i in range(axis_size)])


def exchange(array, view_count, ctx_size, orders):
    pairs = [
        (view * ctx_size + i, view * ctx_size + (i ^ orders[view % 2]))
        for view in range(view_count)
        for i in range(ctx_size)
    ]
    return lax.ppermute(array, ("view", "ctx"), pairs)


def gather_views(array, view_count, *after):
    gathered = [array]
    step = view_count // 2
    for earlier in after:
        gathered, _ = lax.optimization_barrier((gathered, earlier))
        gathered += [swap(block, "view", view_count, step) for block in gathered]
        step //= 2
    return gathered


def split_attention(q, k, v, k_cross, v_cross, view_count, ctx_size):
    rows, width = q.shape
    heads = width // HEAD
    partners = PARTNERS
    vmem = pl.BlockSpec(memory_space=pltpu.VMEM)
    hbm = pl.BlockSpec(memory_space=pltpu.HBM)
    sources = [pltpu.with_memory_space_constraint(x, pltpu.HBM) for x in (q, k, v, k_cross, v_cross)]
    block = jax.ShapeDtypeStruct((3 * rows, HEAD), q.dtype)
    *blocks, pair = pl.pallas_call(
        functools.partial(pack_kernel, partners),
        out_shape=[block] * heads + [jax.ShapeDtypeStruct((2 * rows, width), q.dtype)],
        in_specs=[hbm] * 5,
        out_specs=[vmem] * (heads + 1),
        scratch_shapes=[pltpu.SemaphoreType.DMA((3 * heads + 2,))],
        compiler_params=kernel_params(),
        name="pack_qkv",
    )(*sources)
    moved = [
        exchange(data, view_count, ctx_size, partner) if any(partner) else data
        for partner, data in zip(partners, blocks)
    ]
    own = pl.pallas_call(
        functools.partial(packed_attention_kernel, partners, rows, max(heads // 4, 1)),
        out_shape=jax.ShapeDtypeStruct((heads, rows, HEAD), q.dtype),
        in_specs=[vmem] * heads,
        out_specs=vmem,
        compiler_params=kernel_params(),
        cost_estimate=pl.CostEstimate(
            flops=4 * rows * rows * heads * heads * HEAD,
            bytes_accessed=8 * rows * heads * HEAD,
            transcendentals=rows * rows * heads * heads,
        ),
        name="self_attention",
    )(*moved)
    back = lax.all_to_all(own, "ctx", split_axis=0, concat_axis=0, tiled=True)
    return back, pair, (pair, moved[:4])


def shared_attention(q, k, v, ctx_size):
    rows, width = q.shape
    heads = width // HEAD
    parts = ctx_size // heads
    piece = rows // parts
    query = jnp.transpose(q.reshape(parts, piece, heads, HEAD), (2, 0, 1, 3)).reshape(
        ctx_size, piece, HEAD
    )
    key = jnp.repeat(jnp.transpose(k.reshape(rows, heads, HEAD), (1, 0, 2)), parts, axis=0)
    value = jnp.repeat(jnp.transpose(v.reshape(rows, heads, HEAD), (1, 0, 2)), parts, axis=0)
    packed = jnp.concatenate([query, key, value], axis=1)
    moved = lax.all_to_all(packed, "ctx", split_axis=0, concat_axis=0, tiled=True)
    query = moved[:, :piece].reshape(ctx_size * piece, HEAD)
    key = moved[:, piece : piece + rows].reshape(ctx_size * rows, HEAD)
    value = moved[:, piece + rows :].reshape(ctx_size * rows, HEAD)
    own = pl.pallas_call(
        attention_kernel,
        out_shape=jax.ShapeDtypeStruct((ctx_size * piece, HEAD), q.dtype),
        grid=(ctx_size * piece // rows,),
        in_specs=[
            pl.BlockSpec((rows, HEAD), lambda i: (i, 0)),
            pl.BlockSpec((ctx_size * rows, HEAD), lambda i: (0, 0)),
            pl.BlockSpec((ctx_size * rows, HEAD), lambda i: (0, 0)),
        ],
        out_specs=pl.BlockSpec((rows, HEAD), lambda i: (i, 0)),
        compiler_params=kernel_params(),
        name="self_attention",
    )(query, key, value)
    back = lax.all_to_all(
        own.reshape(ctx_size, piece, HEAD), "ctx", split_axis=0, concat_axis=0, tiled=True
    )
    return back.reshape(heads, rows, HEAD)


def body(view_count, ctx_size, q_self, k_self, v_self, q_cross, k_cross, v_cross):
    _, rows, width = q_self.shape
    heads = width // HEAD
    if ctx_size == heads == 8:
        o_self, pair, after = split_attention(
            q_self[0], k_self[0], v_self[0], k_cross[0], v_cross[0], view_count, ctx_size
        )
    else:
        o_self = shared_attention(q_self[0], k_self[0], v_self[0], ctx_size)
        pair = jnp.concatenate([k_cross[0], v_cross[0]], axis=0)
        after = [pair] * (view_count.bit_length() - 1)
    pairs = gather_views(pair, view_count, *after)
    vmem = pl.BlockSpec(memory_space=pltpu.VMEM)
    out = pl.pallas_call(
        functools.partial(cross_kernel, heads),
        out_shape=jax.ShapeDtypeStruct((rows, width), q_self.dtype),
        in_specs=[vmem] * (2 + view_count),
        out_specs=vmem,
        compiler_params=kernel_params(),
        name="cross_view",
    )(o_self, q_cross[0], *pairs)
    return out[None]


def solution(mesh):
    spec = P("view", "ctx", None)
    return jax.shard_map(
        functools.partial(body, mesh.shape["view"], mesh.shape["ctx"]),
        mesh=mesh,
        in_specs=(spec,) * 6,
        out_specs=spec,
        check_vma=False,
    )
```

```python
import functools
import math

import jax
import jax.numpy as jnp
from jax import lax
from jax.experimental import pallas as pl
from jax.experimental.pallas import tpu as pltpu
from jax.sharding import PartitionSpec as P

HEAD = 128
SCALE = 1.0 / math.sqrt(HEAD)
EXP2_SCALE = SCALE * math.log2(math.e)
MIB = 1024 * 1024


def pack_kernel(partners, q_ref, k_ref, v_ref, kc_ref, vc_ref, *refs):
    block_refs, pair_ref, sems = refs[: len(partners)], refs[-2], refs[-1]
    rows = q_ref.shape[0]
    me = lax.axis_index("ctx")
    copies = []

    def start(source, target):
        copy = pltpu.make_async_copy(source, target, sems.at[len(copies)])
        copy.start()
        copies.append(copy)

    for partner, block_ref in zip(partners, block_refs):
        lanes = pl.ds(pl.multiple_of((me ^ partner) * HEAD, HEAD), HEAD)
        for part, source in enumerate((q_ref, k_ref, v_ref)):
            start(source.at[:, lanes], block_ref.at[pl.ds(part * rows, rows)])
    for part, source in enumerate((kc_ref, vc_ref)):
        start(source, pair_ref.at[pl.ds(part * rows, rows)])
    for copy in copies:
        copy.wait()


def attend(query, keys, values):
    scores = lax.dot_general(
        query, keys, (((1,), (1,)), ((), ())), preferred_element_type=jnp.float32
    )
    row_max = jnp.max(scores, axis=-1, keepdims=True)
    weights_raw = jnp.exp2((scores - row_max) * EXP2_SCALE).astype(jnp.bfloat16)
    values_ones = jnp.concatenate([values, jnp.ones_like(values)], axis=1)
    mixed = jnp.dot(weights_raw, values_ones, preferred_element_type=jnp.float32)
    return (mixed[:, :HEAD] / mixed[:, HEAD:]).astype(jnp.bfloat16)


def packed_attention_kernel(partners, rows, group, *refs):
    *in_refs, out_ref = refs
    me = lax.axis_index("ctx")
    keys = jnp.concatenate([ref[rows : 2 * rows] for ref in in_refs], axis=0)
    values = jnp.concatenate([ref[2 * rows : 3 * rows] for ref in in_refs], axis=0)
    for first in range(0, len(in_refs), group):
        query = jnp.concatenate([ref[0:rows] for ref in in_refs[first : first + group]], axis=0)
        mixed = attend(query, keys, values)
        for i in range(group):
            out_ref[me ^ partners[first + i]] = mixed[i * rows : (i + 1) * rows]


def attention_kernel(q_ref, k_ref, v_ref, out_ref):
    out_ref[...] = attend(q_ref[...], k_ref[...], v_ref[...])


def cross_kernel(head_count, o_ref, q_ref, *refs):
    *pair_refs, out_hbm_ref, out_ref, sems = refs
    copies = []
    rows = q_ref.shape[0]
    for head in range(head_count):
        lanes = slice(head * HEAD, (head + 1) * HEAD)
        o_self = o_ref[head].astype(jnp.float32)
        query = (q_ref[:, lanes].astype(jnp.float32) + o_self).astype(jnp.bfloat16).astype(jnp.float32)
        scores = [
            jnp.sum(query * ref[0:rows, lanes].astype(jnp.float32), axis=-1, keepdims=True)
            for ref in pair_refs
        ]
        top = functools.reduce(jnp.maximum, scores)
        weights = [jnp.exp2((score - top) * EXP2_SCALE) for score in scores]
        inverse = 1.0 / sum(weights[1:], weights[0])
        mixed = None
        for weight, ref in zip(weights, pair_refs):
            rounded = (weight * inverse).astype(jnp.bfloat16).astype(jnp.float32)
            term = rounded * ref[rows : 2 * rows, lanes].astype(jnp.float32)
            mixed = term if mixed is None else mixed + term
        o_cross = mixed.astype(jnp.bfloat16).astype(jnp.float32)
        out_ref[:, lanes] = (o_self + o_cross).astype(jnp.bfloat16)
        if head % 2:
            done = pl.ds((head - 1) * HEAD, 2 * HEAD)
            copies.append(
                pltpu.make_async_copy(out_ref.at[:, done], out_hbm_ref.at[:, done], sems.at[head // 2])
            )
            copies[-1].start()
    for copy in copies:
        copy.wait()


def kernel_params(grant=32):
    return pltpu.CompilerParams(vmem_limit_bytes=grant * MIB)


def swap(array, axis_name, axis_size, partner):
    return lax.ppermute(array, axis_name, [(i, i ^ partner) for i in range(axis_size)])


def gather_views(array, view_count, *after):
    gathered = [array]
    step = view_count // 2
    for earlier in after:
        gathered, _ = lax.optimization_barrier((gathered, earlier))
        gathered += [swap(block, "view", view_count, step) for block in gathered]
        step //= 2
    return gathered


def split_attention(q, k, v, k_cross, v_cross, ctx_size):
    rows, width = q.shape
    heads = width // HEAD
    partners = (3, 2, 1, 5, 4, 7, 6, 0)
    vmem = pl.BlockSpec(memory_space=pltpu.VMEM)
    hbm = pl.BlockSpec(memory_space=pltpu.HBM)
    sources = [pltpu.with_memory_space_constraint(x, pltpu.HBM) for x in (q, k, v, k_cross, v_cross)]
    block = jax.ShapeDtypeStruct((3 * rows, HEAD), q.dtype)
    *blocks, pair = pl.pallas_call(
        functools.partial(pack_kernel, partners),
        out_shape=[block] * heads + [jax.ShapeDtypeStruct((2 * rows, width), q.dtype)],
        in_specs=[hbm] * 5,
        out_specs=[vmem] * (heads + 1),
        scratch_shapes=[pltpu.SemaphoreType.DMA((3 * heads + 2,))],
        compiler_params=kernel_params(),
        name="pack_qkv",
    )(*sources)
    moved = [
        swap(data, "ctx", ctx_size, partner) if partner else data
        for partner, data in zip(partners, blocks)
    ]
    own = pl.pallas_call(
        functools.partial(packed_attention_kernel, partners, rows, max(heads // 4, 1)),
        out_shape=jax.ShapeDtypeStruct((heads, rows, HEAD), q.dtype),
        in_specs=[vmem] * heads,
        out_specs=vmem,
        compiler_params=kernel_params(),
        cost_estimate=pl.CostEstimate(
            flops=4 * rows * rows * heads * heads * HEAD,
            bytes_accessed=8 * rows * heads * HEAD,
            transcendentals=rows * rows * heads * heads,
        ),
        name="self_attention",
    )(*moved)
    back = lax.all_to_all(own, "ctx", split_axis=0, concat_axis=0, tiled=True)
    return back, pair, (pair, moved[:4])


def shared_attention(q, k, v, ctx_size):
    rows, width = q.shape
    heads = width // HEAD
    parts = ctx_size // heads
    piece = rows // parts
    query = jnp.transpose(q.reshape(parts, piece, heads, HEAD), (2, 0, 1, 3)).reshape(
        ctx_size, piece, HEAD
    )
    key = jnp.repeat(jnp.transpose(k.reshape(rows, heads, HEAD), (1, 0, 2)), parts, axis=0)
    value = jnp.repeat(jnp.transpose(v.reshape(rows, heads, HEAD), (1, 0, 2)), parts, axis=0)
    packed = jnp.concatenate([query, key, value], axis=1)
    moved = lax.all_to_all(packed, "ctx", split_axis=0, concat_axis=0, tiled=True)
    query = moved[:, :piece].reshape(ctx_size * piece, HEAD)
    key = moved[:, piece : piece + rows].reshape(ctx_size * rows, HEAD)
    value = moved[:, piece + rows :].reshape(ctx_size * rows, HEAD)
    own = pl.pallas_call(
        attention_kernel,
        out_shape=jax.ShapeDtypeStruct((ctx_size * piece, HEAD), q.dtype),
        grid=(ctx_size * piece // rows,),
        in_specs=[
            pl.BlockSpec((rows, HEAD), lambda i: (i, 0)),
            pl.BlockSpec((ctx_size * rows, HEAD), lambda i: (0, 0)),
            pl.BlockSpec((ctx_size * rows, HEAD), lambda i: (0, 0)),
        ],
        out_specs=pl.BlockSpec((rows, HEAD), lambda i: (i, 0)),
        compiler_params=kernel_params(),
        name="self_attention",
    )(query, key, value)
    back = lax.all_to_all(
        own.reshape(ctx_size, piece, HEAD), "ctx", split_axis=0, concat_axis=0, tiled=True
    )
    return back.reshape(heads, rows, HEAD)


def body(view_count, ctx_size, q_self, k_self, v_self, q_cross, k_cross, v_cross):
    _, rows, width = q_self.shape
    heads = width // HEAD
    if ctx_size == heads == 8:
        o_self, pair, after = split_attention(
            q_self[0], k_self[0], v_self[0], k_cross[0], v_cross[0], ctx_size
        )
    else:
        o_self = shared_attention(q_self[0], k_self[0], v_self[0], ctx_size)
        pair = jnp.concatenate([k_cross[0], v_cross[0]], axis=0)
        after = [pair] * (view_count.bit_length() - 1)
    pairs = gather_views(pair, view_count, *after)
    vmem = pl.BlockSpec(memory_space=pltpu.VMEM)
    out = pl.pallas_call(
        functools.partial(cross_kernel, heads),
        out_shape=jax.ShapeDtypeStruct((rows, width), q_self.dtype),
        in_specs=[vmem] * (2 + view_count),
        out_specs=pl.BlockSpec(memory_space=pl.ANY),
        scratch_shapes=[
            pltpu.VMEM((rows, width), q_self.dtype),
            pltpu.SemaphoreType.DMA((heads // 2,)),
        ],
        compiler_params=kernel_params(),
        name="cross_view",
    )(o_self, q_cross[0], *pairs)
    return out[None]


def solution(mesh):
    spec = P("view", "ctx", None)
    return jax.shard_map(
        functools.partial(body, mesh.shape["view"], mesh.shape["ctx"]),
        mesh=mesh,
        in_specs=(spec,) * 6,
        out_specs=spec,
        check_vma=False,
    )
```

```python
import functools
import math

import jax
import jax.numpy as jnp
from jax import lax
from jax.experimental import pallas as pl
from jax.experimental.pallas import tpu as pltpu
from jax.sharding import PartitionSpec as P

HEAD = 128
SCALE = 1.0 / math.sqrt(HEAD)
EXP2_SCALE = SCALE * math.log2(math.e)
MIB = 1024 * 1024
PARTNERS = tuple(zip((5, 4, 3, 2, 7, 6, 1, 0), (3, 2, 1, 5, 4, 7, 6, 0)))


def partner_of(orders):
    core = lax.rem(lax.axis_index("view"), 2)
    first, second = orders
    return lax.axis_index("ctx") ^ (first + core * (second - first))


def pack_kernel(partners, q_ref, k_ref, v_ref, kc_ref, vc_ref, *refs):
    block_refs, pair_ref, sems = refs[: len(partners)], refs[-2], refs[-1]
    rows = q_ref.shape[0]
    copies = []

    def start(source, target):
        copy = pltpu.make_async_copy(source, target, sems.at[len(copies)])
        copy.start()
        copies.append(copy)

    for partner, block_ref in zip(partners, block_refs):
        lanes = pl.ds(pl.multiple_of(partner_of(partner) * HEAD, HEAD), HEAD)
        for part, source in enumerate((q_ref, k_ref, v_ref)):
            start(source.at[:, lanes], block_ref.at[pl.ds(part * rows, rows)])
    for part, source in enumerate((kc_ref, vc_ref)):
        start(source, pair_ref.at[pl.ds(part * rows, rows)])
    for copy in copies:
        copy.wait()


def attend(query, keys, values):
    scores = lax.dot_general(
        query, keys, (((1,), (1,)), ((), ())), preferred_element_type=jnp.float32
    )
    row_max = jnp.max(scores, axis=-1, keepdims=True)
    weights_raw = jnp.exp2((scores - row_max) * EXP2_SCALE).astype(jnp.bfloat16)
    values_ones = jnp.concatenate([values, jnp.ones_like(values)], axis=1)
    mixed = jnp.dot(weights_raw, values_ones, preferred_element_type=jnp.float32)
    return (mixed[:, :HEAD] / mixed[:, HEAD:]).astype(jnp.bfloat16)


def packed_attention_kernel(partners, rows, group, *refs):
    *in_refs, out_ref = refs
    keys = jnp.concatenate([ref[rows : 2 * rows] for ref in in_refs], axis=0)
    values = jnp.concatenate([ref[2 * rows : 3 * rows] for ref in in_refs], axis=0)
    for first in range(0, len(in_refs), group):
        query = jnp.concatenate([ref[0:rows] for ref in in_refs[first : first + group]], axis=0)
        mixed = attend(query, keys, values)
        for i in range(group):
            out_ref[partner_of(partners[first + i])] = mixed[i * rows : (i + 1) * rows]


def attention_kernel(q_ref, k_ref, v_ref, out_ref):
    out_ref[...] = attend(q_ref[...], k_ref[...], v_ref[...])


def cross_kernel(head_count, o_ref, q_ref, *refs):
    *pair_refs, out_ref = refs
    rows = q_ref.shape[0]
    for head in range(head_count):
        lanes = slice(head * HEAD, (head + 1) * HEAD)
        o_self = o_ref[head].astype(jnp.float32)
        query = (q_ref[:, lanes].astype(jnp.float32) + o_self).astype(jnp.bfloat16).astype(jnp.float32)
        scores = [
            jnp.sum(query * ref[0:rows, lanes].astype(jnp.float32), axis=-1, keepdims=True)
            for ref in pair_refs
        ]
        top = functools.reduce(jnp.maximum, scores)
        weights = [jnp.exp2((score - top) * EXP2_SCALE) for score in scores]
        inverse = 1.0 / sum(weights[1:], weights[0])
        mixed = None
        for weight, ref in zip(weights, pair_refs):
            rounded = (weight * inverse).astype(jnp.bfloat16).astype(jnp.float32)
            term = rounded * ref[rows : 2 * rows, lanes].astype(jnp.float32)
            mixed = term if mixed is None else mixed + term
        o_cross = mixed.astype(jnp.bfloat16).astype(jnp.float32)
        out_ref[:, lanes] = (o_self + o_cross).astype(jnp.bfloat16)


def kernel_params(grant=32):
    return pltpu.CompilerParams(vmem_limit_bytes=grant * MIB)


def swap(array, axis_name, axis_size, partner):
    return lax.ppermute(array, axis_name, [(i, i ^ partner) for i in range(axis_size)])


def exchange(array, view_count, ctx_size, orders):
    pairs = [
        (view * ctx_size + i, view * ctx_size + (i ^ orders[view % 2]))
        for view in range(view_count)
        for i in range(ctx_size)
    ]
    return lax.ppermute(array, ("view", "ctx"), pairs)


def gather_views(array, view_count, *after):
    gathered = [array]
    step = view_count // 2
    for earlier in after:
        gathered, _ = lax.optimization_barrier((gathered, earlier))
        gathered += [swap(block, "view", view_count, step) for block in gathered]
        step //= 2
    return gathered


def split_attention(q, k, v, k_cross, v_cross, view_count, ctx_size):
    rows, width = q.shape
    heads = width // HEAD
    partners = PARTNERS
    vmem = pl.BlockSpec(memory_space=pltpu.VMEM)
    hbm = pl.BlockSpec(memory_space=pltpu.HBM)
    sources = [pltpu.with_memory_space_constraint(x, pltpu.HBM) for x in (q, k, v, k_cross, v_cross)]
    block = jax.ShapeDtypeStruct((3 * rows, HEAD), q.dtype)
    *blocks, pair = pl.pallas_call(
        functools.partial(pack_kernel, partners),
        out_shape=[block] * heads + [jax.ShapeDtypeStruct((2 * rows, width), q.dtype)],
        in_specs=[hbm] * 5,
        out_specs=[vmem] * (heads + 1),
        scratch_shapes=[pltpu.SemaphoreType.DMA((3 * heads + 2,))],
        compiler_params=kernel_params(),
        name="pack_qkv",
    )(*sources)
    moved = [
        exchange(data, view_count, ctx_size, partner) if any(partner) else data
        for partner, data in zip(partners, blocks)
    ]
    own = pl.pallas_call(
        functools.partial(packed_attention_kernel, partners, rows, max(heads // 4, 1)),
        out_shape=jax.ShapeDtypeStruct((heads, rows, HEAD), q.dtype),
        in_specs=[vmem] * heads,
        out_specs=vmem,
        compiler_params=kernel_params(),
        cost_estimate=pl.CostEstimate(
            flops=4 * rows * rows * heads * heads * HEAD,
            bytes_accessed=8 * rows * heads * HEAD,
            transcendentals=rows * rows * heads * heads,
        ),
        name="self_attention",
    )(*moved)
    back = lax.all_to_all(own, "ctx", split_axis=0, concat_axis=0, tiled=True)
    return back, pair, (pair, moved[:4])


def shared_attention(q, k, v, ctx_size):
    rows, width = q.shape
    heads = width // HEAD
    parts = ctx_size // heads
    piece = rows // parts
    query = jnp.transpose(q.reshape(parts, piece, heads, HEAD), (2, 0, 1, 3)).reshape(
        ctx_size, piece, HEAD
    )
    key = jnp.repeat(jnp.transpose(k.reshape(rows, heads, HEAD), (1, 0, 2)), parts, axis=0)
    value = jnp.repeat(jnp.transpose(v.reshape(rows, heads, HEAD), (1, 0, 2)), parts, axis=0)
    packed = jnp.concatenate([query, key, value], axis=1)
    moved = lax.all_to_all(packed, "ctx", split_axis=0, concat_axis=0, tiled=True)
    query = moved[:, :piece].reshape(ctx_size * piece, HEAD)
    key = moved[:, piece : piece + rows].reshape(ctx_size * rows, HEAD)
    value = moved[:, piece + rows :].reshape(ctx_size * rows, HEAD)
    own = pl.pallas_call(
        attention_kernel,
        out_shape=jax.ShapeDtypeStruct((ctx_size * piece, HEAD), q.dtype),
        grid=(ctx_size * piece // rows,),
        in_specs=[
            pl.BlockSpec((rows, HEAD), lambda i: (i, 0)),
            pl.BlockSpec((ctx_size * rows, HEAD), lambda i: (0, 0)),
            pl.BlockSpec((ctx_size * rows, HEAD), lambda i: (0, 0)),
        ],
        out_specs=pl.BlockSpec((rows, HEAD), lambda i: (i, 0)),
        compiler_params=kernel_params(),
        name="self_attention",
    )(query, key, value)
    back = lax.all_to_all(
        own.reshape(ctx_size, piece, HEAD), "ctx", split_axis=0, concat_axis=0, tiled=True
    )
    return back.reshape(heads, rows, HEAD)


def body(view_count, ctx_size, q_self, k_self, v_self, q_cross, k_cross, v_cross):
    _, rows, width = q_self.shape
    heads = width // HEAD
    if ctx_size == heads == 8:
        o_self, pair, after = split_attention(
            q_self[0], k_self[0], v_self[0], k_cross[0], v_cross[0], view_count, ctx_size
        )
    else:
        o_self = shared_attention(q_self[0], k_self[0], v_self[0], ctx_size)
        pair = jnp.concatenate([k_cross[0], v_cross[0]], axis=0)
        after = [pair] * (view_count.bit_length() - 1)
    pairs = gather_views(pair, view_count, *after)
    vmem = pl.BlockSpec(memory_space=pltpu.VMEM)
    out = pl.pallas_call(
        functools.partial(cross_kernel, heads),
        out_shape=jax.ShapeDtypeStruct((rows, width), q_self.dtype),
        in_specs=[vmem] * (2 + view_count),
        out_specs=vmem,
        compiler_params=kernel_params(),
        name="cross_view",
    )(o_self, q_cross[0], *pairs)
    return out[None]


def solution(mesh):
    spec = P("view", "ctx", None)
    return jax.shard_map(
        functools.partial(body, mesh.shape["view"], mesh.shape["ctx"]),
        mesh=mesh,
        in_specs=(spec,) * 6,
        out_specs=spec,
        check_vma=False,
    )
```

```python
import functools
import math

import jax
import jax.numpy as jnp
from jax import lax
from jax.experimental import pallas as pl
from jax.experimental.pallas import tpu as pltpu
from jax.sharding import PartitionSpec as P

HEAD = 128
SCALE = 1.0 / math.sqrt(HEAD)
EXP2_SCALE = SCALE * math.log2(math.e)
MIB = 1024 * 1024


def pack_kernel(far, q_ref, k_ref, v_ref, kc_ref, vc_ref, *refs):
    *far_refs, across_ref, along_ref, own_ref, pair_ref, sems = refs
    rows = q_ref.shape[0]
    me = lax.axis_index("ctx")
    copies = []

    def start(source, target):
        copy = pltpu.make_async_copy(source, target, sems.at[len(copies)])
        copy.start()
        copies.append(copy)

    blocks = list(zip(far, far_refs))
    blocks += [(1, across_ref.at[0]), (3, across_ref.at[1]), (2, along_ref), (0, own_ref)]
    for partner, target in blocks:
        lanes = pl.ds(pl.multiple_of((me ^ partner) * HEAD, HEAD), HEAD)
        for part, source in enumerate((q_ref, k_ref, v_ref)):
            start(source.at[:, lanes], target.at[pl.ds(part * rows, rows)])
    for part, source in enumerate((kc_ref, vc_ref)):
        start(source, pair_ref.at[pl.ds(part * rows, rows)])
    for copy in copies:
        copy.wait()


def attend(query, keys, values):
    scores = lax.dot_general(
        query, keys, (((1,), (1,)), ((), ())), preferred_element_type=jnp.float32
    )
    row_max = jnp.max(scores, axis=-1, keepdims=True)
    weights_raw = jnp.exp2((scores - row_max) * EXP2_SCALE).astype(jnp.bfloat16)
    values_ones = jnp.concatenate([values, jnp.ones_like(values)], axis=1)
    mixed = jnp.dot(weights_raw, values_ones, preferred_element_type=jnp.float32)
    return (mixed[:, :HEAD] / mixed[:, HEAD:]).astype(jnp.bfloat16)


def packed_attention_kernel(far, rows, *refs):
    *far_refs, across_ref, along_ref, own_ref, out_ref = refs
    me = lax.axis_index("ctx")
    blocks = list(zip(far, far_refs))
    blocks += [(0, own_ref), (1, across_ref.at[0]), (2, along_ref.at[0]), (3, along_ref.at[1])]
    keys = jnp.concatenate([ref[rows : 2 * rows] for _, ref in blocks], axis=0)
    values = jnp.concatenate([ref[2 * rows : 3 * rows] for _, ref in blocks], axis=0)
    for first in range(0, len(blocks), 2):
        chunk = blocks[first : first + 2]
        query = jnp.concatenate([ref[0:rows] for _, ref in chunk], axis=0)
        mixed = attend(query, keys, values)
        for i, (partner, _) in enumerate(chunk):
            out_ref[me ^ partner] = mixed[i * rows : (i + 1) * rows]


def attention_kernel(q_ref, k_ref, v_ref, out_ref):
    out_ref[...] = attend(q_ref[...], k_ref[...], v_ref[...])


def cross_kernel(head_count, o_ref, q_ref, *refs):
    *pair_refs, out_ref = refs
    rows = q_ref.shape[0]
    for head in range(head_count):
        lanes = slice(head * HEAD, (head + 1) * HEAD)
        o_self = o_ref[head].astype(jnp.float32)
        query = (q_ref[:, lanes].astype(jnp.float32) + o_self).astype(jnp.bfloat16).astype(jnp.float32)
        scores = [
            jnp.sum(query * ref[0:rows, lanes].astype(jnp.float32), axis=-1, keepdims=True)
            for ref in pair_refs
        ]
        top = functools.reduce(jnp.maximum, scores)
        weights = [jnp.exp2((score - top) * EXP2_SCALE) for score in scores]
        inverse = 1.0 / sum(weights[1:], weights[0])
        mixed = None
        for weight, ref in zip(weights, pair_refs):
            rounded = (weight * inverse).astype(jnp.bfloat16).astype(jnp.float32)
            term = rounded * ref[rows : 2 * rows, lanes].astype(jnp.float32)
            mixed = term if mixed is None else mixed + term
        o_cross = mixed.astype(jnp.bfloat16).astype(jnp.float32)
        out_ref[:, lanes] = (o_self + o_cross).astype(jnp.bfloat16)


def kernel_params(grant=32):
    return pltpu.CompilerParams(vmem_limit_bytes=grant * MIB)


def swap(array, axis_name, axis_size, partner):
    return lax.ppermute(array, axis_name, [(i, i ^ partner) for i in range(axis_size)])


def gather_views(array, view_count, *after):
    gathered = [array]
    step = view_count // 2
    for earlier in after:
        gathered, _ = lax.optimization_barrier((gathered, earlier))
        gathered += [swap(block, "view", view_count, step) for block in gathered]
        step //= 2
    return gathered


def split_attention(q, k, v, k_cross, v_cross, ctx_size):
    rows, width = q.shape
    heads = width // HEAD
    far = (5, 7, 4, 6)
    vmem = pl.BlockSpec(memory_space=pltpu.VMEM)
    hbm = pl.BlockSpec(memory_space=pltpu.HBM)
    sources = [pltpu.with_memory_space_constraint(x, pltpu.HBM) for x in (q, k, v, k_cross, v_cross)]
    block = jax.ShapeDtypeStruct((3 * rows, HEAD), q.dtype)
    two_blocks = jax.ShapeDtypeStruct((2, 3 * rows, HEAD), q.dtype)
    *far_blocks, across, along, own, pair = pl.pallas_call(
        functools.partial(pack_kernel, far),
        out_shape=[block] * len(far)
        + [two_blocks, block, block, jax.ShapeDtypeStruct((2 * rows, width), q.dtype)],
        in_specs=[hbm] * 5,
        out_specs=[vmem] * (len(far) + 4),
        scratch_shapes=[pltpu.SemaphoreType.DMA((3 * heads + 2,))],
        compiler_params=kernel_params(),
        name="pack_qkv",
    )(*sources)
    across = swap(across, "ctx", ctx_size, 1)
    moved = [swap(data, "ctx", ctx_size, partner) for partner, data in zip(far, far_blocks)]
    along = swap(jnp.stack([along, across[1]]), "ctx", ctx_size, 2)
    moved += [across, along, own]
    own_heads = pl.pallas_call(
        functools.partial(packed_attention_kernel, far, rows),
        out_shape=jax.ShapeDtypeStruct((heads, rows, HEAD), q.dtype),
        in_specs=[vmem] * len(moved),
        out_specs=vmem,
        compiler_params=kernel_params(),
        cost_estimate=pl.CostEstimate(
            flops=4 * rows * rows * heads * heads * HEAD,
            bytes_accessed=8 * rows * heads * HEAD,
            transcendentals=rows * rows * heads * heads,
        ),
        name="self_attention",
    )(*moved)
    back = lax.all_to_all(own_heads, "ctx", split_axis=0, concat_axis=0, tiled=True)
    return back, pair, (pair, moved)


def shared_attention(q, k, v, ctx_size):
    rows, width = q.shape
    heads = width // HEAD
    parts = ctx_size // heads
    piece = rows // parts
    query = jnp.transpose(q.reshape(parts, piece, heads, HEAD), (2, 0, 1, 3)).reshape(
        ctx_size, piece, HEAD
    )
    key = jnp.repeat(jnp.transpose(k.reshape(rows, heads, HEAD), (1, 0, 2)), parts, axis=0)
    value = jnp.repeat(jnp.transpose(v.reshape(rows, heads, HEAD), (1, 0, 2)), parts, axis=0)
    packed = jnp.concatenate([query, key, value], axis=1)
    moved = lax.all_to_all(packed, "ctx", split_axis=0, concat_axis=0, tiled=True)
    query = moved[:, :piece].reshape(ctx_size * piece, HEAD)
    key = moved[:, piece : piece + rows].reshape(ctx_size * rows, HEAD)
    value = moved[:, piece + rows :].reshape(ctx_size * rows, HEAD)
    own = pl.pallas_call(
        attention_kernel,
        out_shape=jax.ShapeDtypeStruct((ctx_size * piece, HEAD), q.dtype),
        grid=(ctx_size * piece // rows,),
        in_specs=[
            pl.BlockSpec((rows, HEAD), lambda i: (i, 0)),
            pl.BlockSpec((ctx_size * rows, HEAD), lambda i: (0, 0)),
            pl.BlockSpec((ctx_size * rows, HEAD), lambda i: (0, 0)),
        ],
        out_specs=pl.BlockSpec((rows, HEAD), lambda i: (i, 0)),
        compiler_params=kernel_params(),
        name="self_attention",
    )(query, key, value)
    back = lax.all_to_all(
        own.reshape(ctx_size, piece, HEAD), "ctx", split_axis=0, concat_axis=0, tiled=True
    )
    return back.reshape(heads, rows, HEAD)


def body(view_count, ctx_size, q_self, k_self, v_self, q_cross, k_cross, v_cross):
    _, rows, width = q_self.shape
    heads = width // HEAD
    if ctx_size == heads == 8:
        o_self, pair, after = split_attention(
            q_self[0], k_self[0], v_self[0], k_cross[0], v_cross[0], ctx_size
        )
    else:
        o_self = shared_attention(q_self[0], k_self[0], v_self[0], ctx_size)
        pair = jnp.concatenate([k_cross[0], v_cross[0]], axis=0)
        after = [pair] * (view_count.bit_length() - 1)
    pairs = gather_views(pair, view_count, *after)
    vmem = pl.BlockSpec(memory_space=pltpu.VMEM)
    out = pl.pallas_call(
        functools.partial(cross_kernel, heads),
        out_shape=jax.ShapeDtypeStruct((rows, width), q_self.dtype),
        in_specs=[vmem] * (2 + view_count),
        out_specs=vmem,
        compiler_params=kernel_params(),
        name="cross_view",
    )(o_self, q_cross[0], *pairs)
    return out[None]


def solution(mesh):
    spec = P("view", "ctx", None)
    return jax.shard_map(
        functools.partial(body, mesh.shape["view"], mesh.shape["ctx"]),
        mesh=mesh,
        in_specs=(spec,) * 6,
        out_specs=spec,
        check_vma=False,
    )
```

```python
import functools
import math

import jax
import jax.numpy as jnp
from jax import lax
from jax.experimental import pallas as pl
from jax.experimental.pallas import tpu as pltpu
from jax.sharding import PartitionSpec as P

HEAD = 128
SCALE = 1.0 / math.sqrt(HEAD)
EXP2_SCALE = SCALE * math.log2(math.e)
MIB = 1024 * 1024


def pack_kernel(partners, q_ref, k_ref, v_ref, kc_ref, vc_ref, *refs):
    block_refs, pair_ref, sems = refs[: len(partners)], refs[-2], refs[-1]
    rows = q_ref.shape[0]
    me = lax.axis_index("ctx")
    copies = []

    def start(source, target):
        copy = pltpu.make_async_copy(source, target, sems.at[len(copies)])
        copy.start()
        copies.append(copy)

    for partner, block_ref in zip(partners, block_refs):
        lanes = pl.ds(pl.multiple_of((me ^ partner) * HEAD, HEAD), HEAD)
        for part, source in enumerate((q_ref, k_ref, v_ref)):
            start(source.at[:, lanes], block_ref.at[pl.ds(part * rows, rows)])
    for part, source in enumerate((kc_ref, vc_ref)):
        start(source, pair_ref.at[pl.ds(part * rows, rows)])
    for copy in copies:
        copy.wait()


def attend(query, keys, values):
    scores = lax.dot_general(
        query, keys, (((1,), (1,)), ((), ())), preferred_element_type=jnp.float32
    )
    row_max = jnp.max(scores, axis=-1, keepdims=True)
    weights_raw = jnp.exp2((scores - row_max) * EXP2_SCALE).astype(jnp.bfloat16)
    values_ones = jnp.concatenate([values, jnp.ones_like(values)], axis=1)
    mixed = jnp.dot(weights_raw, values_ones, preferred_element_type=jnp.float32)
    return (mixed[:, :HEAD] / mixed[:, HEAD:]).astype(jnp.bfloat16)


def packed_attention_kernel(partners, rows, group, *refs):
    *in_refs, out_ref = refs
    me = lax.axis_index("ctx")
    keys = jnp.concatenate([ref[rows : 2 * rows] for ref in in_refs], axis=0)
    values = jnp.concatenate([ref[2 * rows : 3 * rows] for ref in in_refs], axis=0)
    for first in range(0, len(in_refs), group):
        query = jnp.concatenate([ref[0:rows] for ref in in_refs[first : first + group]], axis=0)
        mixed = attend(query, keys, values)
        for i in range(group):
            out_ref[me ^ partners[first + i]] = mixed[i * rows : (i + 1) * rows]


def attention_kernel(q_ref, k_ref, v_ref, out_ref):
    out_ref[...] = attend(q_ref[...], k_ref[...], v_ref[...])


def matrix_sums(products):
    high = products.astype(jnp.bfloat16)
    low = (products - high.astype(jnp.float32)).astype(jnp.bfloat16)
    halves = jnp.concatenate([high, low], axis=1)
    ones = jnp.ones((2 * HEAD, HEAD), jnp.bfloat16)
    return jnp.dot(halves, ones, preferred_element_type=jnp.float32)


def cross_kernel(head_count, o_ref, q_ref, *refs):
    *pair_refs, out_ref = refs
    rows = q_ref.shape[0]
    for head in range(head_count):
        lanes = slice(head * HEAD, (head + 1) * HEAD)
        o_self = o_ref[head].astype(jnp.float32)
        query = (q_ref[:, lanes].astype(jnp.float32) + o_self).astype(jnp.bfloat16).astype(jnp.float32)
        products = [query * ref[0:rows, lanes].astype(jnp.float32) for ref in pair_refs]
        scores = [
            matrix_sums(product) if view % 2 else jnp.sum(product, axis=-1, keepdims=True)
            for view, product in enumerate(products)
        ]
        top = functools.reduce(jnp.maximum, scores)
        weights = [jnp.exp2((score - top) * EXP2_SCALE) for score in scores]
        inverse = 1.0 / sum(weights[1:], weights[0])
        mixed = None
        for weight, ref in zip(weights, pair_refs):
            rounded = (weight * inverse).astype(jnp.bfloat16).astype(jnp.float32)
            term = rounded * ref[rows : 2 * rows, lanes].astype(jnp.float32)
            mixed = term if mixed is None else mixed + term
        o_cross = mixed.astype(jnp.bfloat16).astype(jnp.float32)
        out_ref[:, lanes] = (o_self + o_cross).astype(jnp.bfloat16)


def kernel_params(grant=32):
    return pltpu.CompilerParams(vmem_limit_bytes=grant * MIB)


def swap(array, axis_name, axis_size, partner):
    return lax.ppermute(array, axis_name, [(i, i ^ partner) for i in range(axis_size)])


def gather_views(array, view_count, *after):
    gathered = [array]
    step = view_count // 2
    for earlier in after:
        gathered, _ = lax.optimization_barrier((gathered, earlier))
        gathered += [swap(block, "view", view_count, step) for block in gathered]
        step //= 2
    return gathered


def split_attention(q, k, v, k_cross, v_cross, ctx_size):
    rows, width = q.shape
    heads = width // HEAD
    partners = (3, 2, 1, 5, 7, 4, 6, 0)
    vmem = pl.BlockSpec(memory_space=pltpu.VMEM)
    hbm = pl.BlockSpec(memory_space=pltpu.HBM)
    sources = [pltpu.with_memory_space_constraint(x, pltpu.HBM) for x in (q, k, v, k_cross, v_cross)]
    block = jax.ShapeDtypeStruct((3 * rows, HEAD), q.dtype)
    *blocks, pair = pl.pallas_call(
        functools.partial(pack_kernel, partners),
        out_shape=[block] * heads + [jax.ShapeDtypeStruct((2 * rows, width), q.dtype)],
        in_specs=[hbm] * 5,
        out_specs=[vmem] * (heads + 1),
        scratch_shapes=[pltpu.SemaphoreType.DMA((3 * heads + 2,))],
        compiler_params=kernel_params(),
        name="pack_qkv",
    )(*sources)
    moved = [
        swap(data, "ctx", ctx_size, partner) if partner else data
        for partner, data in zip(partners, blocks)
    ]
    own = pl.pallas_call(
        functools.partial(packed_attention_kernel, partners, rows, max(heads // 4, 1)),
        out_shape=jax.ShapeDtypeStruct((heads, rows, HEAD), q.dtype),
        in_specs=[vmem] * heads,
        out_specs=vmem,
        compiler_params=kernel_params(),
        cost_estimate=pl.CostEstimate(
            flops=4 * rows * rows * heads * heads * HEAD,
            bytes_accessed=8 * rows * heads * HEAD,
            transcendentals=rows * rows * heads * heads,
        ),
        name="self_attention",
    )(*moved)
    back = lax.all_to_all(own, "ctx", split_axis=0, concat_axis=0, tiled=True)
    return back, pair, (pair, moved[:4])


def shared_attention(q, k, v, ctx_size):
    rows, width = q.shape
    heads = width // HEAD
    parts = ctx_size // heads
    piece = rows // parts
    query = jnp.transpose(q.reshape(parts, piece, heads, HEAD), (2, 0, 1, 3)).reshape(
        ctx_size, piece, HEAD
    )
    key = jnp.repeat(jnp.transpose(k.reshape(rows, heads, HEAD), (1, 0, 2)), parts, axis=0)
    value = jnp.repeat(jnp.transpose(v.reshape(rows, heads, HEAD), (1, 0, 2)), parts, axis=0)
    packed = jnp.concatenate([query, key, value], axis=1)
    moved = lax.all_to_all(packed, "ctx", split_axis=0, concat_axis=0, tiled=True)
    query = moved[:, :piece].reshape(ctx_size * piece, HEAD)
    key = moved[:, piece : piece + rows].reshape(ctx_size * rows, HEAD)
    value = moved[:, piece + rows :].reshape(ctx_size * rows, HEAD)
    own = pl.pallas_call(
        attention_kernel,
        out_shape=jax.ShapeDtypeStruct((ctx_size * piece, HEAD), q.dtype),
        grid=(ctx_size * piece // rows,),
        in_specs=[
            pl.BlockSpec((rows, HEAD), lambda i: (i, 0)),
            pl.BlockSpec((ctx_size * rows, HEAD), lambda i: (0, 0)),
            pl.BlockSpec((ctx_size * rows, HEAD), lambda i: (0, 0)),
        ],
        out_specs=pl.BlockSpec((rows, HEAD), lambda i: (i, 0)),
        compiler_params=kernel_params(),
        name="self_attention",
    )(query, key, value)
    back = lax.all_to_all(
        own.reshape(ctx_size, piece, HEAD), "ctx", split_axis=0, concat_axis=0, tiled=True
    )
    return back.reshape(heads, rows, HEAD)


def body(view_count, ctx_size, q_self, k_self, v_self, q_cross, k_cross, v_cross):
    _, rows, width = q_self.shape
    heads = width // HEAD
    if ctx_size == heads == 8:
        o_self, pair, after = split_attention(
            q_self[0], k_self[0], v_self[0], k_cross[0], v_cross[0], ctx_size
        )
    else:
        o_self = shared_attention(q_self[0], k_self[0], v_self[0], ctx_size)
        pair = jnp.concatenate([k_cross[0], v_cross[0]], axis=0)
        after = [pair] * (view_count.bit_length() - 1)
    pairs = gather_views(pair, view_count, *after)
    vmem = pl.BlockSpec(memory_space=pltpu.VMEM)
    out = pl.pallas_call(
        functools.partial(cross_kernel, heads),
        out_shape=jax.ShapeDtypeStruct((rows, width), q_self.dtype),
        in_specs=[vmem] * (2 + view_count),
        out_specs=vmem,
        compiler_params=kernel_params(),
        name="cross_view",
    )(o_self, q_cross[0], *pairs)
    return out[None]


def solution(mesh):
    spec = P("view", "ctx", None)
    return jax.shard_map(
        functools.partial(body, mesh.shape["view"], mesh.shape["ctx"]),
        mesh=mesh,
        in_specs=(spec,) * 6,
        out_specs=spec,
        check_vma=False,
    )
```

```python
import functools
import math

import jax
import jax.numpy as jnp
from jax import lax
from jax.experimental import pallas as pl
from jax.experimental.pallas import tpu as pltpu
from jax.sharding import PartitionSpec as P

HEAD = 128
SCALE = 1.0 / math.sqrt(HEAD)
EXP2_SCALE = SCALE * math.log2(math.e)
MIB = 1024 * 1024


def pack_kernel(partners, q_ref, k_ref, v_ref, kc_ref, vc_ref, *refs):
    block_refs, pair_ref, sems = refs[: len(partners)], refs[-2], refs[-1]
    rows = q_ref.shape[0]
    me = lax.axis_index("ctx")
    copies = []

    def start(source, target):
        copy = pltpu.make_async_copy(source, target, sems.at[len(copies)])
        copy.start()
        copies.append(copy)

    for partner, block_ref in zip(partners, block_refs):
        lanes = pl.ds(pl.multiple_of((me ^ partner) * HEAD, HEAD), HEAD)
        for part, source in enumerate((q_ref, k_ref, v_ref)):
            start(source.at[:, lanes], block_ref.at[pl.ds(part * rows, rows)])
    for part, source in enumerate((kc_ref, vc_ref)):
        start(source, pair_ref.at[pl.ds(part * rows, rows)])
    for copy in copies:
        copy.wait()


def attend(query, keys, values):
    scores = lax.dot_general(
        query, keys, (((1,), (1,)), ((), ())), preferred_element_type=jnp.float32
    )
    row_max = jnp.max(scores, axis=-1, keepdims=True)
    weights_raw = jnp.exp2((scores - row_max) * EXP2_SCALE).astype(jnp.bfloat16)
    values_ones = jnp.concatenate([values, jnp.ones_like(values)], axis=1)
    mixed = jnp.dot(weights_raw, values_ones, preferred_element_type=jnp.float32)
    return (mixed[:, :HEAD] / mixed[:, HEAD:]).astype(jnp.bfloat16)


def packed_attention_kernel(partners, rows, group, *refs):
    *in_refs, out_ref = refs
    me = lax.axis_index("ctx")
    keys = jnp.concatenate([ref[rows : 2 * rows] for ref in in_refs], axis=0)
    values = jnp.concatenate([ref[2 * rows : 3 * rows] for ref in in_refs], axis=0)
    for first in range(0, len(in_refs), group):
        query = jnp.concatenate([ref[0:rows] for ref in in_refs[first : first + group]], axis=0)
        mixed = attend(query, keys, values)
        for i in range(group):
            out_ref[me ^ partners[first + i]] = mixed[i * rows : (i + 1) * rows]


def attention_kernel(q_ref, k_ref, v_ref, out_ref):
    out_ref[...] = attend(q_ref[...], k_ref[...], v_ref[...])


def cross_kernel(head_count, o_ref, q_ref, *refs):
    *pair_refs, out_ref = refs
    rows = q_ref.shape[0]
    lane = lax.broadcasted_iota(jnp.int32, (rows, HEAD), 1)
    scores = [jnp.zeros((rows, HEAD), jnp.float32) for _ in pair_refs]
    for head in range(head_count):
        lanes = slice(head * HEAD, (head + 1) * HEAD)
        o_self = o_ref[head].astype(jnp.float32)
        query = (q_ref[:, lanes].astype(jnp.float32) + o_self).astype(jnp.bfloat16).astype(jnp.float32)
        for view, ref in enumerate(pair_refs):
            products = query * ref[0:rows, lanes].astype(jnp.float32)
            summed = jnp.sum(products, axis=-1, keepdims=True)
            scores[view] = jnp.where(lane == head, summed, scores[view])
    top = functools.reduce(jnp.maximum, scores)
    weights = [jnp.exp2((score - top) * EXP2_SCALE) for score in scores]
    inverse = 1.0 / sum(weights[1:], weights[0])
    packed = jnp.concatenate([(weight * inverse).astype(jnp.bfloat16) for weight in weights], axis=0)
    source = lax.broadcasted_iota(jnp.int32, (HEAD, 2 * HEAD), 0)
    target = lax.broadcasted_iota(jnp.int32, (HEAD, 2 * HEAD), 1)
    second = jnp.where(target >= HEAD, 1, 0)
    for head in range(0, head_count, 2):
        lanes = slice(head * HEAD, (head + 2) * HEAD)
        spread = jnp.where(source == second + head, 1.0, 0.0).astype(jnp.bfloat16)
        rounded = jnp.dot(packed, spread, preferred_element_type=jnp.float32)
        mixed = None
        for view, ref in enumerate(pair_refs):
            term = rounded[view * rows : (view + 1) * rows] * ref[rows : 2 * rows, lanes].astype(jnp.float32)
            mixed = term if mixed is None else mixed + term
        o_cross = mixed.astype(jnp.bfloat16).astype(jnp.float32)
        o_self = jnp.concatenate([o_ref[head], o_ref[head + 1]], axis=1).astype(jnp.float32)
        out_ref[:, lanes] = (o_self + o_cross).astype(jnp.bfloat16)


def kernel_params(grant=32):
    return pltpu.CompilerParams(vmem_limit_bytes=grant * MIB)


def swap(array, axis_name, axis_size, partner):
    return lax.ppermute(array, axis_name, [(i, i ^ partner) for i in range(axis_size)])


def gather_views(array, view_count, *after):
    gathered = [array]
    step = view_count // 2
    for earlier in after:
        gathered, _ = lax.optimization_barrier((gathered, earlier))
        gathered += [swap(block, "view", view_count, step) for block in gathered]
        step //= 2
    return gathered


def split_attention(q, k, v, k_cross, v_cross, ctx_size):
    rows, width = q.shape
    heads = width // HEAD
    partners = (3, 7, 6, 2, 5, 4, 1, 0)
    vmem = pl.BlockSpec(memory_space=pltpu.VMEM)
    hbm = pl.BlockSpec(memory_space=pltpu.HBM)
    sources = [pltpu.with_memory_space_constraint(x, pltpu.HBM) for x in (q, k, v, k_cross, v_cross)]
    block = jax.ShapeDtypeStruct((3 * rows, HEAD), q.dtype)
    *blocks, pair = pl.pallas_call(
        functools.partial(pack_kernel, partners),
        out_shape=[block] * heads + [jax.ShapeDtypeStruct((2 * rows, width), q.dtype)],
        in_specs=[hbm] * 5,
        out_specs=[vmem] * (heads + 1),
        scratch_shapes=[pltpu.SemaphoreType.DMA((3 * heads + 2,))],
        compiler_params=kernel_params(),
        name="pack_qkv",
    )(*sources)
    moved = [
        swap(data, "ctx", ctx_size, partner) if partner else data
        for partner, data in zip(partners, blocks)
    ]
    own = pl.pallas_call(
        functools.partial(packed_attention_kernel, partners, rows, max(heads // 4, 1)),
        out_shape=jax.ShapeDtypeStruct((heads, rows, HEAD), q.dtype),
        in_specs=[vmem] * heads,
        out_specs=vmem,
        compiler_params=kernel_params(),
        cost_estimate=pl.CostEstimate(
            flops=4 * rows * rows * heads * heads * HEAD,
            bytes_accessed=8 * rows * heads * HEAD,
            transcendentals=rows * rows * heads * heads,
        ),
        name="self_attention",
    )(*moved)
    back = lax.all_to_all(own, "ctx", split_axis=0, concat_axis=0, tiled=True)
    return back, pair, (pair, moved[:4])


def shared_attention(q, k, v, ctx_size):
    rows, width = q.shape
    heads = width // HEAD
    parts = ctx_size // heads
    piece = rows // parts
    query = jnp.transpose(q.reshape(parts, piece, heads, HEAD), (2, 0, 1, 3)).reshape(
        ctx_size, piece, HEAD
    )
    key = jnp.repeat(jnp.transpose(k.reshape(rows, heads, HEAD), (1, 0, 2)), parts, axis=0)
    value = jnp.repeat(jnp.transpose(v.reshape(rows, heads, HEAD), (1, 0, 2)), parts, axis=0)
    packed = jnp.concatenate([query, key, value], axis=1)
    moved = lax.all_to_all(packed, "ctx", split_axis=0, concat_axis=0, tiled=True)
    query = moved[:, :piece].reshape(ctx_size * piece, HEAD)
    key = moved[:, piece : piece + rows].reshape(ctx_size * rows, HEAD)
    value = moved[:, piece + rows :].reshape(ctx_size * rows, HEAD)
    own = pl.pallas_call(
        attention_kernel,
        out_shape=jax.ShapeDtypeStruct((ctx_size * piece, HEAD), q.dtype),
        grid=(ctx_size * piece // rows,),
        in_specs=[
            pl.BlockSpec((rows, HEAD), lambda i: (i, 0)),
            pl.BlockSpec((ctx_size * rows, HEAD), lambda i: (0, 0)),
            pl.BlockSpec((ctx_size * rows, HEAD), lambda i: (0, 0)),
        ],
        out_specs=pl.BlockSpec((rows, HEAD), lambda i: (i, 0)),
        compiler_params=kernel_params(),
        name="self_attention",
    )(query, key, value)
    back = lax.all_to_all(
        own.reshape(ctx_size, piece, HEAD), "ctx", split_axis=0, concat_axis=0, tiled=True
    )
    return back.reshape(heads, rows, HEAD)


def body(view_count, ctx_size, q_self, k_self, v_self, q_cross, k_cross, v_cross):
    _, rows, width = q_self.shape
    heads = width // HEAD
    if ctx_size == heads == 8:
        o_self, pair, after = split_attention(
            q_self[0], k_self[0], v_self[0], k_cross[0], v_cross[0], ctx_size
        )
    else:
        o_self = shared_attention(q_self[0], k_self[0], v_self[0], ctx_size)
        pair = jnp.concatenate([k_cross[0], v_cross[0]], axis=0)
        after = [pair] * (view_count.bit_length() - 1)
    pairs = gather_views(pair, view_count, *after)
    vmem = pl.BlockSpec(memory_space=pltpu.VMEM)
    out = pl.pallas_call(
        functools.partial(cross_kernel, heads),
        out_shape=jax.ShapeDtypeStruct((rows, width), q_self.dtype),
        in_specs=[vmem] * (2 + view_count),
        out_specs=vmem,
        compiler_params=kernel_params(),
        name="cross_view",
    )(o_self, q_cross[0], *pairs)
    return out[None]


def solution(mesh):
    spec = P("view", "ctx", None)
    return jax.shard_map(
        functools.partial(body, mesh.shape["view"], mesh.shape["ctx"]),
        mesh=mesh,
        in_specs=(spec,) * 6,
        out_specs=spec,
        check_vma=False,
    )
```

```python
import functools
import math

import jax
import jax.numpy as jnp
from jax import lax
from jax.experimental import pallas as pl
from jax.experimental.pallas import tpu as pltpu
from jax.sharding import PartitionSpec as P

HEAD = 128
SCALE = 1.0 / math.sqrt(HEAD)
EXP2_SCALE = SCALE * math.log2(math.e)
MIB = 1024 * 1024


def pack_kernel(partners, q_ref, k_ref, v_ref, kc_ref, vc_ref, *refs):
    block_refs, pair_ref, sems = refs[: len(partners)], refs[-2], refs[-1]
    rows = q_ref.shape[0]
    me = lax.axis_index("ctx")
    copies = []

    def start(source, target):
        copy = pltpu.make_async_copy(source, target, sems.at[len(copies)])
        copy.start()
        copies.append(copy)

    for partner, block_ref in zip(partners, block_refs):
        lanes = pl.ds(pl.multiple_of((me ^ partner) * HEAD, HEAD), HEAD)
        for part, source in enumerate((q_ref, k_ref, v_ref)):
            start(source.at[:, lanes], block_ref.at[pl.ds(part * rows, rows)])
    for part, source in enumerate((kc_ref, vc_ref)):
        start(source, pair_ref.at[pl.ds(part * rows, rows)])
    for copy in copies:
        copy.wait()


def attend(query, keys, values):
    scores = lax.dot_general(
        query, keys, (((1,), (1,)), ((), ())), preferred_element_type=jnp.float32
    )
    row_max = jnp.max(scores, axis=-1, keepdims=True)
    weights_raw = jnp.exp2((scores - row_max) * EXP2_SCALE).astype(jnp.bfloat16)
    values_ones = jnp.concatenate([values, jnp.ones_like(values)], axis=1)
    mixed = jnp.dot(weights_raw, values_ones, preferred_element_type=jnp.float32)
    return (mixed[:, :HEAD] / mixed[:, HEAD:]).astype(jnp.bfloat16)


def packed_attention_kernel(partners, rows, group, *refs):
    *in_refs, out_ref = refs
    me = lax.axis_index("ctx")
    keys = jnp.concatenate([ref[rows : 2 * rows] for ref in in_refs], axis=0)
    values = jnp.concatenate([ref[2 * rows : 3 * rows] for ref in in_refs], axis=0)
    for first in range(0, len(in_refs), group):
        query = jnp.concatenate([ref[0:rows] for ref in in_refs[first : first + group]], axis=0)
        mixed = attend(query, keys, values)
        for i in range(group):
            out_ref[me ^ partners[first + i]] = mixed[i * rows : (i + 1) * rows]


def attention_kernel(q_ref, k_ref, v_ref, out_ref):
    out_ref[...] = attend(q_ref[...], k_ref[...], v_ref[...])


def cross_kernel(head_count, o_ref, q_ref, *refs):
    *pair_refs, out_ref = refs
    rows = q_ref.shape[0]

    @pl.loop(0, head_count)
    def _(head):
        lanes = pl.ds(pl.multiple_of(head * HEAD, HEAD), HEAD)
        o_self = o_ref[head].astype(jnp.float32)
        query = (q_ref[:, lanes].astype(jnp.float32) + o_self).astype(jnp.bfloat16).astype(jnp.float32)
        scores = [
            jnp.sum(query * ref[0:rows, lanes].astype(jnp.float32), axis=-1, keepdims=True)
            for ref in pair_refs
        ]
        top = functools.reduce(jnp.maximum, scores)
        weights = [jnp.exp2((score - top) * EXP2_SCALE) for score in scores]
        inverse = 1.0 / sum(weights[1:], weights[0])
        mixed = None
        for weight, ref in zip(weights, pair_refs):
            rounded = (weight * inverse).astype(jnp.bfloat16).astype(jnp.float32)
            term = rounded * ref[rows : 2 * rows, lanes].astype(jnp.float32)
            mixed = term if mixed is None else mixed + term
        o_cross = mixed.astype(jnp.bfloat16).astype(jnp.float32)
        out_ref[:, lanes] = (o_self + o_cross).astype(jnp.bfloat16)


def kernel_params(grant=32):
    return pltpu.CompilerParams(vmem_limit_bytes=grant * MIB)


def swap(array, axis_name, axis_size, partner):
    return lax.ppermute(array, axis_name, [(i, i ^ partner) for i in range(axis_size)])


def gather_views(array, view_count, *after):
    gathered = [array]
    step = view_count // 2
    for earlier in after:
        gathered, _ = lax.optimization_barrier((gathered, earlier))
        gathered += [swap(block, "view", view_count, step) for block in gathered]
        step //= 2
    return gathered


def split_attention(q, k, v, k_cross, v_cross, ctx_size):
    rows, width = q.shape
    heads = width // HEAD
    partners = (3, 7, 6, 2, 5, 4, 1, 0)
    vmem = pl.BlockSpec(memory_space=pltpu.VMEM)
    hbm = pl.BlockSpec(memory_space=pltpu.HBM)
    sources = [pltpu.with_memory_space_constraint(x, pltpu.HBM) for x in (q, k, v, k_cross, v_cross)]
    block = jax.ShapeDtypeStruct((3 * rows, HEAD), q.dtype)
    *blocks, pair = pl.pallas_call(
        functools.partial(pack_kernel, partners),
        out_shape=[block] * heads + [jax.ShapeDtypeStruct((2 * rows, width), q.dtype)],
        in_specs=[hbm] * 5,
        out_specs=[vmem] * (heads + 1),
        scratch_shapes=[pltpu.SemaphoreType.DMA((3 * heads + 2,))],
        compiler_params=kernel_params(),
        name="pack_qkv",
    )(*sources)
    moved = [
        swap(data, "ctx", ctx_size, partner) if partner else data
        for partner, data in zip(partners, blocks)
    ]
    own = pl.pallas_call(
        functools.partial(packed_attention_kernel, partners, rows, max(heads // 4, 1)),
        out_shape=jax.ShapeDtypeStruct((heads, rows, HEAD), q.dtype),
        in_specs=[vmem] * heads,
        out_specs=vmem,
        compiler_params=kernel_params(),
        cost_estimate=pl.CostEstimate(
            flops=4 * rows * rows * heads * heads * HEAD,
            bytes_accessed=8 * rows * heads * HEAD,
            transcendentals=rows * rows * heads * heads,
        ),
        name="self_attention",
    )(*moved)
    back = lax.all_to_all(own, "ctx", split_axis=0, concat_axis=0, tiled=True)
    return back, pair, (pair, moved[:4])


def shared_attention(q, k, v, ctx_size):
    rows, width = q.shape
    heads = width // HEAD
    parts = ctx_size // heads
    piece = rows // parts
    query = jnp.transpose(q.reshape(parts, piece, heads, HEAD), (2, 0, 1, 3)).reshape(
        ctx_size, piece, HEAD
    )
    key = jnp.repeat(jnp.transpose(k.reshape(rows, heads, HEAD), (1, 0, 2)), parts, axis=0)
    value = jnp.repeat(jnp.transpose(v.reshape(rows, heads, HEAD), (1, 0, 2)), parts, axis=0)
    packed = jnp.concatenate([query, key, value], axis=1)
    moved = lax.all_to_all(packed, "ctx", split_axis=0, concat_axis=0, tiled=True)
    query = moved[:, :piece].reshape(ctx_size * piece, HEAD)
    key = moved[:, piece : piece + rows].reshape(ctx_size * rows, HEAD)
    value = moved[:, piece + rows :].reshape(ctx_size * rows, HEAD)
    own = pl.pallas_call(
        attention_kernel,
        out_shape=jax.ShapeDtypeStruct((ctx_size * piece, HEAD), q.dtype),
        grid=(ctx_size * piece // rows,),
        in_specs=[
            pl.BlockSpec((rows, HEAD), lambda i: (i, 0)),
            pl.BlockSpec((ctx_size * rows, HEAD), lambda i: (0, 0)),
            pl.BlockSpec((ctx_size * rows, HEAD), lambda i: (0, 0)),
        ],
        out_specs=pl.BlockSpec((rows, HEAD), lambda i: (i, 0)),
        compiler_params=kernel_params(),
        name="self_attention",
    )(query, key, value)
    back = lax.all_to_all(
        own.reshape(ctx_size, piece, HEAD), "ctx", split_axis=0, concat_axis=0, tiled=True
    )
    return back.reshape(heads, rows, HEAD)


def body(view_count, ctx_size, q_self, k_self, v_self, q_cross, k_cross, v_cross):
    _, rows, width = q_self.shape
    heads = width // HEAD
    if ctx_size == heads == 8:
        o_self, pair, after = split_attention(
            q_self[0], k_self[0], v_self[0], k_cross[0], v_cross[0], ctx_size
        )
    else:
        o_self = shared_attention(q_self[0], k_self[0], v_self[0], ctx_size)
        pair = jnp.concatenate([k_cross[0], v_cross[0]], axis=0)
        after = [pair] * (view_count.bit_length() - 1)
    pairs = gather_views(pair, view_count, *after)
    vmem = pl.BlockSpec(memory_space=pltpu.VMEM)
    out = pl.pallas_call(
        functools.partial(cross_kernel, heads),
        out_shape=jax.ShapeDtypeStruct((rows, width), q_self.dtype),
        in_specs=[vmem] * (2 + view_count),
        out_specs=vmem,
        compiler_params=kernel_params(),
        name="cross_view",
    )(o_self, q_cross[0], *pairs)
    return out[None]


def solution(mesh):
    spec = P("view", "ctx", None)
    return jax.shard_map(
        functools.partial(body, mesh.shape["view"], mesh.shape["ctx"]),
        mesh=mesh,
        in_specs=(spec,) * 6,
        out_specs=spec,
        check_vma=False,
    )
```

```python
import functools
import math

import jax
import jax.numpy as jnp
from jax import lax
from jax.experimental import pallas as pl
from jax.experimental.pallas import tpu as pltpu
from jax.sharding import PartitionSpec as P

HEAD = 128
SCALE = 1.0 / math.sqrt(HEAD)
EXP2_SCALE = SCALE * math.log2(math.e)
MIB = 1024 * 1024
PARTNERS = tuple(zip((3, 7, 6, 2, 5, 4, 1, 0), (3, 2, 1, 7, 6, 5, 4, 0)))


def partner_of(orders):
    core = lax.rem(lax.axis_index("view"), 2)
    first, second = orders
    return lax.axis_index("ctx") ^ (first + core * (second - first))


def pack_kernel(partners, q_ref, k_ref, v_ref, kc_ref, vc_ref, *refs):
    block_refs, pair_ref, sems = refs[: len(partners)], refs[-2], refs[-1]
    rows = q_ref.shape[0]
    copies = []

    def start(source, target):
        copy = pltpu.make_async_copy(source, target, sems.at[len(copies)])
        copy.start()
        copies.append(copy)

    for partner, block_ref in zip(partners, block_refs):
        lanes = pl.ds(pl.multiple_of(partner_of(partner) * HEAD, HEAD), HEAD)
        for part, source in enumerate((q_ref, k_ref, v_ref)):
            start(source.at[:, lanes], block_ref.at[pl.ds(part * rows, rows)])
    for part, source in enumerate((kc_ref, vc_ref)):
        start(source, pair_ref.at[pl.ds(part * rows, rows)])
    for copy in copies:
        copy.wait()


def attend(query, keys, values):
    scores = lax.dot_general(
        query, keys, (((1,), (1,)), ((), ())), preferred_element_type=jnp.float32
    )
    row_max = jnp.max(scores, axis=-1, keepdims=True)
    weights_raw = jnp.exp2((scores - row_max) * EXP2_SCALE).astype(jnp.bfloat16)
    values_ones = jnp.concatenate([values, jnp.ones_like(values)], axis=1)
    mixed = jnp.dot(weights_raw, values_ones, preferred_element_type=jnp.float32)
    return (mixed[:, :HEAD] / mixed[:, HEAD:]).astype(jnp.bfloat16)


def packed_attention_kernel(partners, rows, group, *refs):
    *in_refs, out_ref = refs
    keys = jnp.concatenate([ref[rows : 2 * rows] for ref in in_refs], axis=0)
    values = jnp.concatenate([ref[2 * rows : 3 * rows] for ref in in_refs], axis=0)
    for first in range(0, len(in_refs), group):
        query = jnp.concatenate([ref[0:rows] for ref in in_refs[first : first + group]], axis=0)
        mixed = attend(query, keys, values)
        for i in range(group):
            out_ref[partner_of(partners[first + i])] = mixed[i * rows : (i + 1) * rows]


def attention_kernel(q_ref, k_ref, v_ref, out_ref):
    out_ref[...] = attend(q_ref[...], k_ref[...], v_ref[...])


def cross_kernel(head_count, o_ref, q_ref, *refs):
    *pair_refs, out_ref = refs
    rows = q_ref.shape[0]
    for head in range(head_count):
        lanes = slice(head * HEAD, (head + 1) * HEAD)
        o_self = o_ref[head].astype(jnp.float32)
        query = (q_ref[:, lanes].astype(jnp.float32) + o_self).astype(jnp.bfloat16).astype(jnp.float32)
        scores = [
            jnp.sum(query * ref[0:rows, lanes].astype(jnp.float32), axis=-1, keepdims=True)
            for ref in pair_refs
        ]
        top = functools.reduce(jnp.maximum, scores)
        weights = [jnp.exp2((score - top) * EXP2_SCALE) for score in scores]
        inverse = 1.0 / sum(weights[1:], weights[0])
        mixed = None
        for weight, ref in zip(weights, pair_refs):
            rounded = (weight * inverse).astype(jnp.bfloat16).astype(jnp.float32)
            term = rounded * ref[rows : 2 * rows, lanes].astype(jnp.float32)
            mixed = term if mixed is None else mixed + term
        o_cross = mixed.astype(jnp.bfloat16).astype(jnp.float32)
        out_ref[:, lanes] = (o_self + o_cross).astype(jnp.bfloat16)


def kernel_params(grant=32):
    return pltpu.CompilerParams(vmem_limit_bytes=grant * MIB)


def swap(array, axis_name, axis_size, partner):
    return lax.ppermute(array, axis_name, [(i, i ^ partner) for i in range(axis_size)])


def exchange(array, view_count, ctx_size, orders):
    pairs = [
        (view * ctx_size + i, view * ctx_size + (i ^ orders[view % 2]))
        for view in range(view_count)
        for i in range(ctx_size)
    ]
    return lax.ppermute(array, ("view", "ctx"), pairs)


def gather_views(array, view_count, *after):
    gathered = [array]
    step = view_count // 2
    for earlier in after:
        gathered, _ = lax.optimization_barrier((gathered, earlier))
        gathered += [swap(block, "view", view_count, step) for block in gathered]
        step //= 2
    return gathered


def split_attention(q, k, v, k_cross, v_cross, view_count, ctx_size):
    rows, width = q.shape
    heads = width // HEAD
    partners = PARTNERS
    vmem = pl.BlockSpec(memory_space=pltpu.VMEM)
    hbm = pl.BlockSpec(memory_space=pltpu.HBM)
    sources = [pltpu.with_memory_space_constraint(x, pltpu.HBM) for x in (q, k, v, k_cross, v_cross)]
    block = jax.ShapeDtypeStruct((3 * rows, HEAD), q.dtype)
    *blocks, pair = pl.pallas_call(
        functools.partial(pack_kernel, partners),
        out_shape=[block] * heads + [jax.ShapeDtypeStruct((2 * rows, width), q.dtype)],
        in_specs=[hbm] * 5,
        out_specs=[vmem] * (heads + 1),
        scratch_shapes=[pltpu.SemaphoreType.DMA((3 * heads + 2,))],
        compiler_params=kernel_params(),
        name="pack_qkv",
    )(*sources)
    moved = [
        exchange(data, view_count, ctx_size, partner) if any(partner) else data
        for partner, data in zip(partners, blocks)
    ]
    own = pl.pallas_call(
        functools.partial(packed_attention_kernel, partners, rows, max(heads // 4, 1)),
        out_shape=jax.ShapeDtypeStruct((heads, rows, HEAD), q.dtype),
        in_specs=[vmem] * heads,
        out_specs=vmem,
        compiler_params=kernel_params(),
        cost_estimate=pl.CostEstimate(
            flops=4 * rows * rows * heads * heads * HEAD,
            bytes_accessed=8 * rows * heads * HEAD,
            transcendentals=rows * rows * heads * heads,
        ),
        name="self_attention",
    )(*moved)
    back = lax.all_to_all(own, "ctx", split_axis=0, concat_axis=0, tiled=True)
    return back, pair, (pair, moved[:4])


def shared_attention(q, k, v, ctx_size):
    rows, width = q.shape
    heads = width // HEAD
    parts = ctx_size // heads
    piece = rows // parts
    query = jnp.transpose(q.reshape(parts, piece, heads, HEAD), (2, 0, 1, 3)).reshape(
        ctx_size, piece, HEAD
    )
    key = jnp.repeat(jnp.transpose(k.reshape(rows, heads, HEAD), (1, 0, 2)), parts, axis=0)
    value = jnp.repeat(jnp.transpose(v.reshape(rows, heads, HEAD), (1, 0, 2)), parts, axis=0)
    packed = jnp.concatenate([query, key, value], axis=1)
    moved = lax.all_to_all(packed, "ctx", split_axis=0, concat_axis=0, tiled=True)
    query = moved[:, :piece].reshape(ctx_size * piece, HEAD)
    key = moved[:, piece : piece + rows].reshape(ctx_size * rows, HEAD)
    value = moved[:, piece + rows :].reshape(ctx_size * rows, HEAD)
    own = pl.pallas_call(
        attention_kernel,
        out_shape=jax.ShapeDtypeStruct((ctx_size * piece, HEAD), q.dtype),
        grid=(ctx_size * piece // rows,),
        in_specs=[
            pl.BlockSpec((rows, HEAD), lambda i: (i, 0)),
            pl.BlockSpec((ctx_size * rows, HEAD), lambda i: (0, 0)),
            pl.BlockSpec((ctx_size * rows, HEAD), lambda i: (0, 0)),
        ],
        out_specs=pl.BlockSpec((rows, HEAD), lambda i: (i, 0)),
        compiler_params=kernel_params(),
        name="self_attention",
    )(query, key, value)
    back = lax.all_to_all(
        own.reshape(ctx_size, piece, HEAD), "ctx", split_axis=0, concat_axis=0, tiled=True
    )
    return back.reshape(heads, rows, HEAD)


def body(view_count, ctx_size, q_self, k_self, v_self, q_cross, k_cross, v_cross):
    _, rows, width = q_self.shape
    heads = width // HEAD
    if ctx_size == heads == 8:
        o_self, pair, after = split_attention(
            q_self[0], k_self[0], v_self[0], k_cross[0], v_cross[0], view_count, ctx_size
        )
    else:
        o_self = shared_attention(q_self[0], k_self[0], v_self[0], ctx_size)
        pair = jnp.concatenate([k_cross[0], v_cross[0]], axis=0)
        after = [pair] * (view_count.bit_length() - 1)
    pairs = gather_views(pair, view_count, *after)
    vmem = pl.BlockSpec(memory_space=pltpu.VMEM)
    out = pl.pallas_call(
        functools.partial(cross_kernel, heads),
        out_shape=jax.ShapeDtypeStruct((rows, width), q_self.dtype),
        in_specs=[vmem] * (2 + view_count),
        out_specs=vmem,
        compiler_params=kernel_params(),
        name="cross_view",
    )(o_self, q_cross[0], *pairs)
    return out[None]


def solution(mesh):
    spec = P("view", "ctx", None)
    return jax.shard_map(
        functools.partial(body, mesh.shape["view"], mesh.shape["ctx"]),
        mesh=mesh,
        in_specs=(spec,) * 6,
        out_specs=spec,
        check_vma=False,
    )
```

```python
import functools
import math

import jax
import jax.numpy as jnp
from jax import lax
from jax.experimental import pallas as pl
from jax.experimental.pallas import tpu as pltpu
from jax.sharding import PartitionSpec as P

HEAD = 128
SCALE = 1.0 / math.sqrt(HEAD)
EXP2_SCALE = SCALE * math.log2(math.e)
MIB = 1024 * 1024


def pack_kernel(partners, q_ref, k_ref, v_ref, kc_ref, vc_ref, *refs):
    block_refs, pair_ref, sems = refs[: len(partners)], refs[-2], refs[-1]
    rows = q_ref.shape[0]
    me = lax.axis_index("ctx")
    copies = []

    def start(source, target):
        copy = pltpu.make_async_copy(source, target, sems.at[len(copies)])
        copy.start()
        copies.append(copy)

    for partner, block_ref in zip(partners, block_refs):
        lanes = pl.ds(pl.multiple_of((me ^ partner) * HEAD, HEAD), HEAD)
        for part, source in enumerate((q_ref, k_ref, v_ref)):
            start(source.at[:, lanes], block_ref.at[pl.ds(part * rows, rows)])
    for part, source in enumerate((kc_ref, vc_ref)):
        start(source, pair_ref.at[pl.ds(part * rows, rows)])
    for copy in copies:
        copy.wait()


def attend(query, keys, values):
    scores = lax.dot_general(
        query, keys, (((1,), (1,)), ((), ())), preferred_element_type=jnp.float32
    )
    row_max = jnp.max(scores, axis=-1, keepdims=True)
    weights_raw = jnp.exp2((scores - row_max) * EXP2_SCALE).astype(jnp.bfloat16)
    values_ones = jnp.concatenate([values, jnp.ones_like(values)], axis=1)
    mixed = jnp.dot(weights_raw, values_ones, preferred_element_type=jnp.float32)
    return (mixed[:, :HEAD] / mixed[:, HEAD:]).astype(jnp.bfloat16)


def packed_attention_kernel(partners, rows, group, *refs):
    *in_refs, out_ref = refs
    me = lax.axis_index("ctx")
    keys = jnp.concatenate([ref[rows : 2 * rows] for ref in in_refs], axis=0)
    values = jnp.concatenate([ref[2 * rows : 3 * rows] for ref in in_refs], axis=0)
    for first in range(0, len(in_refs), group):
        query = jnp.concatenate([ref[0:rows] for ref in in_refs[first : first + group]], axis=0)
        mixed = attend(query, keys, values)
        for i in range(group):
            out_ref[me ^ partners[first + i]] = mixed[i * rows : (i + 1) * rows]


def attention_kernel(q_ref, k_ref, v_ref, out_ref):
    out_ref[...] = attend(q_ref[...], k_ref[...], v_ref[...])


def cross_kernel(head_count, o_ref, q_ref, *refs):
    *pair_refs, out_ref = refs
    rows = q_ref.shape[0]
    for head in range(head_count):
        lanes = slice(head * HEAD, (head + 1) * HEAD)
        o_self = o_ref[head].astype(jnp.float32)
        query = (q_ref[:, lanes].astype(jnp.float32) + o_self).astype(jnp.bfloat16).astype(jnp.float32)
        scores = [
            jnp.sum(query * ref[0:rows, lanes].astype(jnp.float32), axis=-1, keepdims=True)
            for ref in pair_refs
        ]
        top = functools.reduce(jnp.maximum, scores)
        weights = [jnp.exp2((score - top) * EXP2_SCALE) for score in scores]
        inverse = 1.0 / sum(weights[1:], weights[0])
        mixed = None
        for weight, ref in zip(weights, pair_refs):
            rounded = (weight * inverse).astype(jnp.bfloat16).astype(jnp.float32)
            term = rounded * ref[rows : 2 * rows, lanes].astype(jnp.float32)
            mixed = term if mixed is None else mixed + term
        o_cross = mixed.astype(jnp.bfloat16).astype(jnp.float32)
        out_ref[:, lanes] = (o_self + o_cross).astype(jnp.bfloat16)


def kernel_params(grant=32):
    return pltpu.CompilerParams(vmem_limit_bytes=grant * MIB)


def swap(array, axis_name, axis_size, partner):
    return lax.ppermute(array, axis_name, [(i, i ^ partner) for i in range(axis_size)])


def gather_views(array, view_count, *after):
    gathered = [array]
    step = view_count // 2
    for earlier in after:
        gathered, _ = lax.optimization_barrier((gathered, earlier))
        gathered += [swap(block, "view", view_count, step) for block in gathered]
        step //= 2
    return gathered


def split_attention(q, k, v, k_cross, v_cross, ctx_size):
    rows, width = q.shape
    heads = width // HEAD
    partners = (3, 5, 7, 2, 4, 6, 1, 0)
    vmem = pl.BlockSpec(memory_space=pltpu.VMEM)
    hbm = pl.BlockSpec(memory_space=pltpu.HBM)
    sources = [pltpu.with_memory_space_constraint(x, pltpu.HBM) for x in (q, k, v, k_cross, v_cross)]
    block = jax.ShapeDtypeStruct((3 * rows, HEAD), q.dtype)
    *blocks, pair = pl.pallas_call(
        functools.partial(pack_kernel, partners),
        out_shape=[block] * heads + [jax.ShapeDtypeStruct((2 * rows, width), q.dtype)],
        in_specs=[hbm] * 5,
        out_specs=[vmem] * (heads + 1),
        scratch_shapes=[pltpu.SemaphoreType.DMA((3 * heads + 2,))],
        compiler_params=kernel_params(),
        name="pack_qkv",
    )(*sources)
    moved = [
        swap(data, "ctx", ctx_size, partner) if partner else data
        for partner, data in zip(partners, blocks)
    ]
    own = pl.pallas_call(
        functools.partial(packed_attention_kernel, partners, rows, max(heads // 4, 1)),
        out_shape=jax.ShapeDtypeStruct((heads, rows, HEAD), q.dtype),
        in_specs=[vmem] * heads,
        out_specs=vmem,
        compiler_params=kernel_params(),
        cost_estimate=pl.CostEstimate(
            flops=4 * rows * rows * heads * heads * HEAD,
            bytes_accessed=8 * rows * heads * HEAD,
            transcendentals=rows * rows * heads * heads,
        ),
        name="self_attention",
    )(*moved)
    back = lax.all_to_all(own, "ctx", split_axis=0, concat_axis=0, tiled=True)
    return back, pair, (pair, moved[:4])


def shared_attention(q, k, v, ctx_size):
    rows, width = q.shape
    heads = width // HEAD
    parts = ctx_size // heads
    piece = rows // parts
    query = jnp.transpose(q.reshape(parts, piece, heads, HEAD), (2, 0, 1, 3)).reshape(
        ctx_size, piece, HEAD
    )
    key = jnp.repeat(jnp.transpose(k.reshape(rows, heads, HEAD), (1, 0, 2)), parts, axis=0)
    value = jnp.repeat(jnp.transpose(v.reshape(rows, heads, HEAD), (1, 0, 2)), parts, axis=0)
    packed = jnp.concatenate([query, key, value], axis=1)
    moved = lax.all_to_all(packed, "ctx", split_axis=0, concat_axis=0, tiled=True)
    query = moved[:, :piece].reshape(ctx_size * piece, HEAD)
    key = moved[:, piece : piece + rows].reshape(ctx_size * rows, HEAD)
    value = moved[:, piece + rows :].reshape(ctx_size * rows, HEAD)
    own = pl.pallas_call(
        attention_kernel,
        out_shape=jax.ShapeDtypeStruct((ctx_size * piece, HEAD), q.dtype),
        grid=(ctx_size * piece // rows,),
        in_specs=[
            pl.BlockSpec((rows, HEAD), lambda i: (i, 0)),
            pl.BlockSpec((ctx_size * rows, HEAD), lambda i: (0, 0)),
            pl.BlockSpec((ctx_size * rows, HEAD), lambda i: (0, 0)),
        ],
        out_specs=pl.BlockSpec((rows, HEAD), lambda i: (i, 0)),
        compiler_params=kernel_params(),
        name="self_attention",
    )(query, key, value)
    back = lax.all_to_all(
        own.reshape(ctx_size, piece, HEAD), "ctx", split_axis=0, concat_axis=0, tiled=True
    )
    return back.reshape(heads, rows, HEAD)


def body(view_count, ctx_size, q_self, k_self, v_self, q_cross, k_cross, v_cross):
    _, rows, width = q_self.shape
    heads = width // HEAD
    if ctx_size == heads == 8:
        o_self, pair, after = split_attention(
            q_self[0], k_self[0], v_self[0], k_cross[0], v_cross[0], ctx_size
        )
    else:
        o_self = shared_attention(q_self[0], k_self[0], v_self[0], ctx_size)
        pair = jnp.concatenate([k_cross[0], v_cross[0]], axis=0)
        after = [pair] * (view_count.bit_length() - 1)
    pairs = gather_views(pair, view_count, *after)
    vmem = pl.BlockSpec(memory_space=pltpu.VMEM)
    out = pl.pallas_call(
        functools.partial(cross_kernel, heads),
        out_shape=jax.ShapeDtypeStruct((rows, width), q_self.dtype),
        in_specs=[vmem] * (2 + view_count),
        out_specs=vmem,
        compiler_params=kernel_params(),
        name="cross_view",
    )(o_self, q_cross[0], *pairs)
    return out[None]


def solution(mesh):
    spec = P("view", "ctx", None)
    return jax.shard_map(
        functools.partial(body, mesh.shape["view"], mesh.shape["ctx"]),
        mesh=mesh,
        in_specs=(spec,) * 6,
        out_specs=spec,
        check_vma=False,
    )
```

```python
import functools
import math

import jax
import jax.numpy as jnp
from jax import lax
from jax.experimental import pallas as pl
from jax.experimental.pallas import tpu as pltpu
from jax.sharding import PartitionSpec as P

HEAD = 128
SCALE = 1.0 / math.sqrt(HEAD)
EXP2_SCALE = SCALE * math.log2(math.e)
MIB = 1024 * 1024


def pack_kernel(partners, q_ref, k_ref, v_ref, kc_ref, vc_ref, *refs):
    block_refs, pair_ref, sems = refs[: len(partners)], refs[-2], refs[-1]
    rows = q_ref.shape[0]
    me = lax.axis_index("ctx")
    copies = []

    def start(source, target):
        copy = pltpu.make_async_copy(source, target, sems.at[len(copies)])
        copy.start()
        copies.append(copy)

    for partner, block_ref in zip(partners, block_refs):
        lanes = pl.ds(pl.multiple_of((me ^ partner) * HEAD, HEAD), HEAD)
        for part, source in enumerate((q_ref, k_ref, v_ref)):
            start(source.at[:, lanes], block_ref.at[pl.ds(part * rows, rows)])
    for part, source in enumerate((kc_ref, vc_ref)):
        start(source, pair_ref.at[pl.ds(part * rows, rows)])
    for copy in copies:
        copy.wait()


def attend(query, keys, values):
    scores = lax.dot_general(
        query, keys, (((1,), (1,)), ((), ())), preferred_element_type=jnp.float32
    )
    row_max = jnp.max(scores, axis=-1, keepdims=True)
    weights_raw = jnp.exp2((scores - row_max) * EXP2_SCALE).astype(jnp.bfloat16)
    values_ones = jnp.concatenate([values, jnp.ones_like(values)], axis=1)
    mixed = jnp.dot(weights_raw, values_ones, preferred_element_type=jnp.float32)
    return (mixed[:, :HEAD] / mixed[:, HEAD:]).astype(jnp.bfloat16)


def packed_attention_kernel(partners, rows, group, *refs):
    *in_refs, out_ref = refs
    me = lax.axis_index("ctx")
    keys = jnp.concatenate([ref[rows : 2 * rows] for ref in in_refs], axis=0)
    values = jnp.concatenate([ref[2 * rows : 3 * rows] for ref in in_refs], axis=0)
    for first in range(0, len(in_refs), group):
        query = jnp.concatenate([ref[0:rows] for ref in in_refs[first : first + group]], axis=0)
        mixed = attend(query, keys, values)
        for i in range(group):
            out_ref[me ^ partners[first + i]] = mixed[i * rows : (i + 1) * rows]


def attention_kernel(q_ref, k_ref, v_ref, out_ref):
    out_ref[...] = attend(q_ref[...], k_ref[...], v_ref[...])


def cross_kernel(head_count, o_ref, q_ref, *refs):
    *pair_refs, out_ref = refs
    rows = q_ref.shape[0]
    for head in range(head_count):
        lanes = slice(head * HEAD, (head + 1) * HEAD)
        o_self = o_ref[head].astype(jnp.float32)
        query = (q_ref[:, lanes].astype(jnp.float32) + o_self).astype(jnp.bfloat16).astype(jnp.float32)
        scores = [
            jnp.sum(query * ref[0:rows, lanes].astype(jnp.float32), axis=-1, keepdims=True)
            for ref in pair_refs
        ]
        top = functools.reduce(jnp.maximum, scores)
        weights = [jnp.exp2((score - top) * EXP2_SCALE) for score in scores]
        inverse = 1.0 / sum(weights[1:], weights[0])
        mixed = None
        for weight, ref in zip(weights, pair_refs):
            rounded = (weight * inverse).astype(jnp.bfloat16).astype(jnp.float32)
            term = rounded * ref[rows : 2 * rows, lanes].astype(jnp.float32)
            mixed = term if mixed is None else mixed + term
        o_cross = mixed.astype(jnp.bfloat16).astype(jnp.float32)
        out_ref[:, lanes] = (o_self + o_cross).astype(jnp.bfloat16)


def kernel_params(grant=32):
    return pltpu.CompilerParams(vmem_limit_bytes=grant * MIB)


def swap(array, axis_name, axis_size, partner):
    return lax.ppermute(array, axis_name, [(i, i ^ partner) for i in range(axis_size)])


def gather_views(array, view_count, *after):
    gathered = [array]
    step = view_count // 2
    for earlier in after:
        gathered, _ = lax.optimization_barrier((gathered, earlier))
        gathered += [swap(block, "view", view_count, step) for block in gathered]
        step //= 2
    return gathered


def split_attention(q, k, v, k_cross, v_cross, ctx_size):
    rows, width = q.shape
    heads = width // HEAD
    partners = (3, 7, 6, 2, 5, 4, 1, 0)
    vmem = pl.BlockSpec(memory_space=pltpu.VMEM)
    hbm = pl.BlockSpec(memory_space=pltpu.HBM)
    sources = [pltpu.with_memory_space_constraint(x, pltpu.HBM) for x in (q, k, v, k_cross, v_cross)]
    block = jax.ShapeDtypeStruct((3 * rows, HEAD), q.dtype)
    *blocks, pair = pl.pallas_call(
        functools.partial(pack_kernel, partners),
        out_shape=[block] * heads + [jax.ShapeDtypeStruct((2 * rows, width), q.dtype)],
        in_specs=[hbm] * 5,
        out_specs=[vmem] * (heads + 1),
        scratch_shapes=[pltpu.SemaphoreType.DMA((3 * heads + 2,))],
        compiler_params=kernel_params(),
        name="pack_qkv",
    )(*sources)
    moved = [
        swap(data, "ctx", ctx_size, partner) if partner else data
        for partner, data in zip(partners, blocks)
    ]
    own = pl.pallas_call(
        functools.partial(packed_attention_kernel, partners, rows, max(heads // 2, 1)),
        out_shape=jax.ShapeDtypeStruct((heads, rows, HEAD), q.dtype),
        in_specs=[vmem] * heads,
        out_specs=vmem,
        compiler_params=kernel_params(),
        cost_estimate=pl.CostEstimate(
            flops=4 * rows * rows * heads * heads * HEAD,
            bytes_accessed=8 * rows * heads * HEAD,
            transcendentals=rows * rows * heads * heads,
        ),
        name="self_attention",
    )(*moved)
    back = lax.all_to_all(own, "ctx", split_axis=0, concat_axis=0, tiled=True)
    return back, pair, (pair, moved[:4])


def shared_attention(q, k, v, ctx_size):
    rows, width = q.shape
    heads = width // HEAD
    parts = ctx_size // heads
    piece = rows // parts
    query = jnp.transpose(q.reshape(parts, piece, heads, HEAD), (2, 0, 1, 3)).reshape(
        ctx_size, piece, HEAD
    )
    key = jnp.repeat(jnp.transpose(k.reshape(rows, heads, HEAD), (1, 0, 2)), parts, axis=0)
    value = jnp.repeat(jnp.transpose(v.reshape(rows, heads, HEAD), (1, 0, 2)), parts, axis=0)
    packed = jnp.concatenate([query, key, value], axis=1)
    moved = lax.all_to_all(packed, "ctx", split_axis=0, concat_axis=0, tiled=True)
    query = moved[:, :piece].reshape(ctx_size * piece, HEAD)
    key = moved[:, piece : piece + rows].reshape(ctx_size * rows, HEAD)
    value = moved[:, piece + rows :].reshape(ctx_size * rows, HEAD)
    own = pl.pallas_call(
        attention_kernel,
        out_shape=jax.ShapeDtypeStruct((ctx_size * piece, HEAD), q.dtype),
        grid=(ctx_size * piece // rows,),
        in_specs=[
            pl.BlockSpec((rows, HEAD), lambda i: (i, 0)),
            pl.BlockSpec((ctx_size * rows, HEAD), lambda i: (0, 0)),
            pl.BlockSpec((ctx_size * rows, HEAD), lambda i: (0, 0)),
        ],
        out_specs=pl.BlockSpec((rows, HEAD), lambda i: (i, 0)),
        compiler_params=kernel_params(),
        name="self_attention",
    )(query, key, value)
    back = lax.all_to_all(
        own.reshape(ctx_size, piece, HEAD), "ctx", split_axis=0, concat_axis=0, tiled=True
    )
    return back.reshape(heads, rows, HEAD)


def body(view_count, ctx_size, q_self, k_self, v_self, q_cross, k_cross, v_cross):
    _, rows, width = q_self.shape
    heads = width // HEAD
    if ctx_size == heads == 8:
        o_self, pair, after = split_attention(
            q_self[0], k_self[0], v_self[0], k_cross[0], v_cross[0], ctx_size
        )
    else:
        o_self = shared_attention(q_self[0], k_self[0], v_self[0], ctx_size)
        pair = jnp.concatenate([k_cross[0], v_cross[0]], axis=0)
        after = [pair] * (view_count.bit_length() - 1)
    pairs = gather_views(pair, view_count, *after)
    vmem = pl.BlockSpec(memory_space=pltpu.VMEM)
    out = pl.pallas_call(
        functools.partial(cross_kernel, heads),
        out_shape=jax.ShapeDtypeStruct((rows, width), q_self.dtype),
        in_specs=[vmem] * (2 + view_count),
        out_specs=vmem,
        compiler_params=kernel_params(),
        name="cross_view",
    )(o_self, q_cross[0], *pairs)
    return out[None]


def solution(mesh):
    spec = P("view", "ctx", None)
    return jax.shard_map(
        functools.partial(body, mesh.shape["view"], mesh.shape["ctx"]),
        mesh=mesh,
        in_specs=(spec,) * 6,
        out_specs=spec,
        check_vma=False,
    )
```

```python
import functools
import math

import jax
import jax.numpy as jnp
from jax import lax
from jax.experimental import pallas as pl
from jax.experimental.pallas import tpu as pltpu
from jax.sharding import PartitionSpec as P

HEAD = 128
SCALE = 1.0 / math.sqrt(HEAD)
EXP2_SCALE = SCALE * math.log2(math.e)
MIB = 1024 * 1024


def pack_kernel(partners, q_ref, k_ref, v_ref, kc_ref, vc_ref, *refs):
    block_refs, pair_ref, sems = refs[: len(partners)], refs[-2], refs[-1]
    rows = q_ref.shape[0]
    me = lax.axis_index("ctx")
    copies = []

    def start(source, target):
        copy = pltpu.make_async_copy(source, target, sems.at[len(copies)])
        copy.start()
        copies.append(copy)

    for partner, block_ref in zip(partners, block_refs):
        lanes = pl.ds(pl.multiple_of((me ^ partner) * HEAD, HEAD), HEAD)
        for part, source in enumerate((q_ref, k_ref, v_ref)):
            start(source.at[:, lanes], block_ref.at[pl.ds(part * rows, rows)])
    for part, source in enumerate((kc_ref, vc_ref)):
        start(source, pair_ref.at[pl.ds(part * rows, rows)])
    for copy in copies:
        copy.wait()


def attend(query, keys, values):
    scores = lax.dot_general(
        query, keys, (((1,), (1,)), ((), ())), preferred_element_type=jnp.float32
    )
    row_max = jnp.max(scores, axis=-1, keepdims=True)
    weights_raw = jnp.exp2((scores - row_max) * EXP2_SCALE).astype(jnp.bfloat16)
    values_ones = jnp.concatenate([values, jnp.ones_like(values)], axis=1)
    mixed = jnp.dot(weights_raw, values_ones, preferred_element_type=jnp.float32)
    return (mixed[:, :HEAD] / mixed[:, HEAD:]).astype(jnp.bfloat16)


def packed_attention_kernel(partners, rows, group, *refs):
    *in_refs, out_ref = refs
    me = lax.axis_index("ctx")
    keys = jnp.concatenate([ref[rows : 2 * rows] for ref in in_refs], axis=0)
    values = jnp.concatenate([ref[2 * rows : 3 * rows] for ref in in_refs], axis=0)
    for first in range(0, len(in_refs), group):
        query = jnp.concatenate([ref[0:rows] for ref in in_refs[first : first + group]], axis=0)
        mixed = attend(query, keys, values)
        for i in range(group):
            out_ref[me ^ partners[first + i]] = mixed[i * rows : (i + 1) * rows]


def attention_kernel(q_ref, k_ref, v_ref, out_ref):
    out_ref[...] = attend(q_ref[...], k_ref[...], v_ref[...])


def cross_kernel(head_count, o_ref, q_ref, *refs):
    *pair_refs, out_ref = refs
    rows = q_ref.shape[0]
    for head in range(head_count):
        lanes = slice(head * HEAD, (head + 1) * HEAD)
        o_self = o_ref[head].astype(jnp.float32)
        query = (q_ref[:, lanes].astype(jnp.float32) + o_self).astype(jnp.bfloat16).astype(jnp.float32)
        scores = [
            jnp.sum(query * ref[0:rows, lanes].astype(jnp.float32), axis=-1, keepdims=True)
            for ref in pair_refs
        ]
        top = functools.reduce(jnp.maximum, scores)
        weights = [jnp.exp2((score - top) * EXP2_SCALE) for score in scores]
        inverse = 1.0 / sum(weights[1:], weights[0])
        mixed = None
        for weight, ref in zip(weights, pair_refs):
            rounded = (weight * inverse).astype(jnp.bfloat16).astype(jnp.float32)
            term = rounded * ref[rows : 2 * rows, lanes].astype(jnp.float32)
            mixed = term if mixed is None else mixed + term
        o_cross = mixed.astype(jnp.bfloat16).astype(jnp.float32)
        out_ref[:, lanes] = (o_self + o_cross).astype(jnp.bfloat16)


def kernel_params(grant=32):
    return pltpu.CompilerParams(vmem_limit_bytes=grant * MIB)


def swap(array, axis_name, axis_size, partner):
    return lax.ppermute(array, axis_name, [(i, i ^ partner) for i in range(axis_size)])


def gather_views(array, view_count, *after):
    gathered = [array]
    step = view_count // 2
    for earlier in after:
        gathered, _ = lax.optimization_barrier((gathered, earlier))
        gathered += [swap(block, "view", view_count, step) for block in gathered]
        step //= 2
    return gathered


def split_attention(q, k, v, k_cross, v_cross, ctx_size):
    rows, width = q.shape
    heads = width // HEAD
    partners = (3, 7, 6, 2, 5, 4, 1, 0)
    vmem = pl.BlockSpec(memory_space=pltpu.VMEM)
    hbm = pl.BlockSpec(memory_space=pltpu.HBM)
    sources = [pltpu.with_memory_space_constraint(x, pltpu.HBM) for x in (q, k, v, k_cross, v_cross)]
    block = jax.ShapeDtypeStruct((3 * rows, HEAD), q.dtype)
    *blocks, pair = pl.pallas_call(
        functools.partial(pack_kernel, partners),
        out_shape=[block] * heads + [jax.ShapeDtypeStruct((2 * rows, width), q.dtype)],
        in_specs=[hbm] * 5,
        out_specs=[vmem] * (heads + 1),
        scratch_shapes=[pltpu.SemaphoreType.DMA((3 * heads + 2,))],
        compiler_params=kernel_params(),
        name="pack_qkv",
    )(*sources)
    moved = [
        swap(data, "ctx", ctx_size, partner) if partner else data
        for partner, data in zip(partners, blocks)
    ]
    own = pl.pallas_call(
        functools.partial(packed_attention_kernel, partners, rows, heads),
        out_shape=jax.ShapeDtypeStruct((heads, rows, HEAD), q.dtype),
        in_specs=[vmem] * heads,
        out_specs=vmem,
        compiler_params=kernel_params(),
        cost_estimate=pl.CostEstimate(
            flops=4 * rows * rows * heads * heads * HEAD,
            bytes_accessed=8 * rows * heads * HEAD,
            transcendentals=rows * rows * heads * heads,
        ),
        name="self_attention",
    )(*moved)
    back = lax.all_to_all(own, "ctx", split_axis=0, concat_axis=0, tiled=True)
    return back, pair, (pair, moved[:4])


def shared_attention(q, k, v, ctx_size):
    rows, width = q.shape
    heads = width // HEAD
    parts = ctx_size // heads
    piece = rows // parts
    query = jnp.transpose(q.reshape(parts, piece, heads, HEAD), (2, 0, 1, 3)).reshape(
        ctx_size, piece, HEAD
    )
    key = jnp.repeat(jnp.transpose(k.reshape(rows, heads, HEAD), (1, 0, 2)), parts, axis=0)
    value = jnp.repeat(jnp.transpose(v.reshape(rows, heads, HEAD), (1, 0, 2)), parts, axis=0)
    packed = jnp.concatenate([query, key, value], axis=1)
    moved = lax.all_to_all(packed, "ctx", split_axis=0, concat_axis=0, tiled=True)
    query = moved[:, :piece].reshape(ctx_size * piece, HEAD)
    key = moved[:, piece : piece + rows].reshape(ctx_size * rows, HEAD)
    value = moved[:, piece + rows :].reshape(ctx_size * rows, HEAD)
    own = pl.pallas_call(
        attention_kernel,
        out_shape=jax.ShapeDtypeStruct((ctx_size * piece, HEAD), q.dtype),
        grid=(ctx_size * piece // rows,),
        in_specs=[
            pl.BlockSpec((rows, HEAD), lambda i: (i, 0)),
            pl.BlockSpec((ctx_size * rows, HEAD), lambda i: (0, 0)),
            pl.BlockSpec((ctx_size * rows, HEAD), lambda i: (0, 0)),
        ],
        out_specs=pl.BlockSpec((rows, HEAD), lambda i: (i, 0)),
        compiler_params=kernel_params(),
        name="self_attention",
    )(query, key, value)
    back = lax.all_to_all(
        own.reshape(ctx_size, piece, HEAD), "ctx", split_axis=0, concat_axis=0, tiled=True
    )
    return back.reshape(heads, rows, HEAD)


def body(view_count, ctx_size, q_self, k_self, v_self, q_cross, k_cross, v_cross):
    _, rows, width = q_self.shape
    heads = width // HEAD
    if ctx_size == heads == 8:
        o_self, pair, after = split_attention(
            q_self[0], k_self[0], v_self[0], k_cross[0], v_cross[0], ctx_size
        )
    else:
        o_self = shared_attention(q_self[0], k_self[0], v_self[0], ctx_size)
        pair = jnp.concatenate([k_cross[0], v_cross[0]], axis=0)
        after = [pair] * (view_count.bit_length() - 1)
    pairs = gather_views(pair, view_count, *after)
    vmem = pl.BlockSpec(memory_space=pltpu.VMEM)
    out = pl.pallas_call(
        functools.partial(cross_kernel, heads),
        out_shape=jax.ShapeDtypeStruct((rows, width), q_self.dtype),
        in_specs=[vmem] * (2 + view_count),
        out_specs=vmem,
        compiler_params=kernel_params(),
        name="cross_view",
    )(o_self, q_cross[0], *pairs)
    return out[None]


def solution(mesh):
    spec = P("view", "ctx", None)
    return jax.shard_map(
        functools.partial(body, mesh.shape["view"], mesh.shape["ctx"]),
        mesh=mesh,
        in_specs=(spec,) * 6,
        out_specs=spec,
        check_vma=False,
    )
```

```python
import functools
import math

import jax
import jax.numpy as jnp
from jax import lax
from jax.experimental import pallas as pl
from jax.experimental.pallas import tpu as pltpu
from jax.sharding import PartitionSpec as P

HEAD = 128
SCALE = 1.0 / math.sqrt(HEAD)
EXP2_SCALE = SCALE * math.log2(math.e)
MIB = 1024 * 1024


def pack_kernel(partners, q_ref, k_ref, v_ref, kc_ref, vc_ref, *refs):
    block_refs, pair_ref, sems = refs[: len(partners)], refs[-2], refs[-1]
    rows = q_ref.shape[0]
    me = lax.axis_index("ctx")
    copies = []

    def start(source, target):
        copy = pltpu.make_async_copy(source, target, sems.at[len(copies)])
        copy.start()
        copies.append(copy)

    for partner, block_ref in zip(partners, block_refs):
        lanes = pl.ds(pl.multiple_of((me ^ partner) * HEAD, HEAD), HEAD)
        for part, source in enumerate((q_ref, k_ref, v_ref)):
            start(source.at[:, lanes], block_ref.at[pl.ds(part * rows, rows)])
    for part, source in enumerate((kc_ref, vc_ref)):
        start(source, pair_ref.at[pl.ds(part * rows, rows)])
    for copy in copies:
        copy.wait()


def attend(query, keys, values):
    scores = lax.dot_general(
        query, keys, (((1,), (1,)), ((), ())), preferred_element_type=jnp.float32
    )
    row_max = jnp.max(scores, axis=-1, keepdims=True)
    weights_raw = jnp.exp2((scores - row_max) * EXP2_SCALE).astype(jnp.bfloat16)
    values_ones = jnp.concatenate([values, jnp.ones_like(values)], axis=1)
    mixed = jnp.dot(weights_raw, values_ones, preferred_element_type=jnp.float32)
    return (mixed[:, :HEAD] / mixed[:, HEAD:]).astype(jnp.bfloat16)


def packed_attention_kernel(partners, rows, group, *refs):
    *in_refs, out_ref = refs
    me = lax.axis_index("ctx")
    keys = jnp.concatenate([ref[rows : 2 * rows] for ref in in_refs], axis=0)
    values = jnp.concatenate([ref[2 * rows : 3 * rows] for ref in in_refs], axis=0)
    for first in range(0, len(in_refs), group):
        query = jnp.concatenate([ref[0:rows] for ref in in_refs[first : first + group]], axis=0)
        mixed = attend(query, keys, values)
        for i in range(group):
            out_ref[me ^ partners[first + i]] = mixed[i * rows : (i + 1) * rows]


def attention_kernel(q_ref, k_ref, v_ref, out_ref):
    out_ref[...] = attend(q_ref[...], k_ref[...], v_ref[...])


def cross_kernel(head_count, o_ref, q_ref, *refs):
    *pair_refs, out_ref = refs
    rows = q_ref.shape[0]
    for head in range(head_count):
        lanes = slice(head * HEAD, (head + 1) * HEAD)
        o_self = o_ref[head].astype(jnp.float32)
        query = (q_ref[:, lanes].astype(jnp.float32) + o_self).astype(jnp.bfloat16).astype(jnp.float32)
        scores = [
            jnp.sum(query * ref[0:rows, lanes].astype(jnp.float32), axis=-1, keepdims=True)
            for ref in pair_refs
        ]
        top = functools.reduce(jnp.maximum, scores)
        weights = [jnp.exp2((score - top) * EXP2_SCALE) for score in scores]
        inverse = 1.0 / sum(weights[1:], weights[0])
        mixed = None
        for weight, ref in zip(weights, pair_refs):
            rounded = (weight * inverse).astype(jnp.bfloat16).astype(jnp.float32)
            term = rounded * ref[rows : 2 * rows, lanes].astype(jnp.float32)
            mixed = term if mixed is None else mixed + term
        o_cross = mixed.astype(jnp.bfloat16).astype(jnp.float32)
        out_ref[:, lanes] = (o_self + o_cross).astype(jnp.bfloat16)


def kernel_params(grant=32):
    return pltpu.CompilerParams(vmem_limit_bytes=grant * MIB)


def swap(array, axis_name, axis_size, partner):
    return lax.ppermute(array, axis_name, [(i, i ^ partner) for i in range(axis_size)])


def gather_views(array, view_count, *after):
    gathered = [array]
    step = view_count // 2
    for earlier in after:
        gathered, _ = lax.optimization_barrier((gathered, earlier))
        gathered += [swap(block, "view", view_count, step) for block in gathered]
        step //= 2
    return gathered


def split_attention(q, k, v, k_cross, v_cross, ctx_size):
    rows, width = q.shape
    heads = width // HEAD
    partners = (3, 7, 6, 2, 4, 5, 1, 0)
    vmem = pl.BlockSpec(memory_space=pltpu.VMEM)
    hbm = pl.BlockSpec(memory_space=pltpu.HBM)
    sources = [pltpu.with_memory_space_constraint(x, pltpu.HBM) for x in (q, k, v, k_cross, v_cross)]
    block = jax.ShapeDtypeStruct((3 * rows, HEAD), q.dtype)
    *blocks, pair = pl.pallas_call(
        functools.partial(pack_kernel, partners),
        out_shape=[block] * heads + [jax.ShapeDtypeStruct((2 * rows, width), q.dtype)],
        in_specs=[hbm] * 5,
        out_specs=[vmem] * (heads + 1),
        scratch_shapes=[pltpu.SemaphoreType.DMA((3 * heads + 2,))],
        compiler_params=kernel_params(),
        name="pack_qkv",
    )(*sources)
    moved = [
        swap(data, "ctx", ctx_size, partner) if partner else data
        for partner, data in zip(partners, blocks)
    ]
    own = pl.pallas_call(
        functools.partial(packed_attention_kernel, partners, rows, max(heads // 2, 1)),
        out_shape=jax.ShapeDtypeStruct((heads, rows, HEAD), q.dtype),
        in_specs=[vmem] * heads,
        out_specs=vmem,
        compiler_params=kernel_params(),
        cost_estimate=pl.CostEstimate(
            flops=4 * rows * rows * heads * heads * HEAD,
            bytes_accessed=8 * rows * heads * HEAD,
            transcendentals=rows * rows * heads * heads,
        ),
        name="self_attention",
    )(*moved)
    back = lax.all_to_all(own, "ctx", split_axis=0, concat_axis=0, tiled=True)
    return back, pair, (pair, moved[:4])


def shared_attention(q, k, v, ctx_size):
    rows, width = q.shape
    heads = width // HEAD
    parts = ctx_size // heads
    piece = rows // parts
    query = jnp.transpose(q.reshape(parts, piece, heads, HEAD), (2, 0, 1, 3)).reshape(
        ctx_size, piece, HEAD
    )
    key = jnp.repeat(jnp.transpose(k.reshape(rows, heads, HEAD), (1, 0, 2)), parts, axis=0)
    value = jnp.repeat(jnp.transpose(v.reshape(rows, heads, HEAD), (1, 0, 2)), parts, axis=0)
    packed = jnp.concatenate([query, key, value], axis=1)
    moved = lax.all_to_all(packed, "ctx", split_axis=0, concat_axis=0, tiled=True)
    query = moved[:, :piece].reshape(ctx_size * piece, HEAD)
    key = moved[:, piece : piece + rows].reshape(ctx_size * rows, HEAD)
    value = moved[:, piece + rows :].reshape(ctx_size * rows, HEAD)
    own = pl.pallas_call(
        attention_kernel,
        out_shape=jax.ShapeDtypeStruct((ctx_size * piece, HEAD), q.dtype),
        grid=(ctx_size * piece // rows,),
        in_specs=[
            pl.BlockSpec((rows, HEAD), lambda i: (i, 0)),
            pl.BlockSpec((ctx_size * rows, HEAD), lambda i: (0, 0)),
            pl.BlockSpec((ctx_size * rows, HEAD), lambda i: (0, 0)),
        ],
        out_specs=pl.BlockSpec((rows, HEAD), lambda i: (i, 0)),
        compiler_params=kernel_params(),
        name="self_attention",
    )(query, key, value)
    back = lax.all_to_all(
        own.reshape(ctx_size, piece, HEAD), "ctx", split_axis=0, concat_axis=0, tiled=True
    )
    return back.reshape(heads, rows, HEAD)


def body(view_count, ctx_size, q_self, k_self, v_self, q_cross, k_cross, v_cross):
    _, rows, width = q_self.shape
    heads = width // HEAD
    if ctx_size == heads == 8:
        o_self, pair, after = split_attention(
            q_self[0], k_self[0], v_self[0], k_cross[0], v_cross[0], ctx_size
        )
    else:
        o_self = shared_attention(q_self[0], k_self[0], v_self[0], ctx_size)
        pair = jnp.concatenate([k_cross[0], v_cross[0]], axis=0)
        after = [pair] * (view_count.bit_length() - 1)
    pairs = gather_views(pair, view_count, *after)
    vmem = pl.BlockSpec(memory_space=pltpu.VMEM)
    out = pl.pallas_call(
        functools.partial(cross_kernel, heads),
        out_shape=jax.ShapeDtypeStruct((rows, width), q_self.dtype),
        in_specs=[vmem] * (2 + view_count),
        out_specs=vmem,
        compiler_params=kernel_params(),
        name="cross_view",
    )(o_self, q_cross[0], *pairs)
    return out[None]


def solution(mesh):
    spec = P("view", "ctx", None)
    return jax.shard_map(
        functools.partial(body, mesh.shape["view"], mesh.shape["ctx"]),
        mesh=mesh,
        in_specs=(spec,) * 6,
        out_specs=spec,
        check_vma=False,
    )
```

```python
import functools
import math

import jax
import jax.numpy as jnp
from jax import lax
from jax.experimental import pallas as pl
from jax.experimental.pallas import tpu as pltpu
from jax.sharding import PartitionSpec as P

HEAD = 128
SCALE = 1.0 / math.sqrt(HEAD)
EXP2_SCALE = SCALE * math.log2(math.e)
MIB = 1024 * 1024


def pack_kernel(partners, q_ref, k_ref, v_ref, kc_ref, vc_ref, *refs):
    block_refs, pair_ref, sems = refs[: len(partners)], refs[-2], refs[-1]
    rows = q_ref.shape[0]
    me = lax.axis_index("ctx")
    copies = []

    def start(source, target):
        copy = pltpu.make_async_copy(source, target, sems.at[len(copies)])
        copy.start()
        copies.append(copy)

    for partner, block_ref in zip(partners, block_refs):
        lanes = pl.ds(pl.multiple_of((me ^ partner) * HEAD, HEAD), HEAD)
        for part, source in enumerate((q_ref, k_ref, v_ref)):
            start(source.at[:, lanes], block_ref.at[pl.ds(part * rows, rows)])
    for part, source in enumerate((kc_ref, vc_ref)):
        start(source, pair_ref.at[pl.ds(part * rows, rows)])
    for copy in copies:
        copy.wait()


def attend(query, keys, values):
    scores = lax.dot_general(
        query, keys, (((1,), (1,)), ((), ())), preferred_element_type=jnp.float32
    )
    row_max = jnp.max(scores, axis=-1, keepdims=True)
    weights_raw = jnp.exp2((scores - row_max) * EXP2_SCALE).astype(jnp.bfloat16)
    values_ones = jnp.concatenate([values, jnp.ones_like(values)], axis=1)
    mixed = jnp.dot(weights_raw, values_ones, preferred_element_type=jnp.float32)
    return (mixed[:, :HEAD] / mixed[:, HEAD:]).astype(jnp.bfloat16)


def packed_attention_kernel(partners, rows, group, *refs):
    *in_refs, out_ref = refs
    me = lax.axis_index("ctx")
    keys = jnp.concatenate([ref[rows : 2 * rows] for ref in in_refs], axis=0)
    values = jnp.concatenate([ref[2 * rows : 3 * rows] for ref in in_refs], axis=0)
    for first in range(0, len(in_refs), group):
        query = jnp.concatenate([ref[0:rows] for ref in in_refs[first : first + group]], axis=0)
        mixed = attend(query, keys, values)
        for i in range(group):
            out_ref[me ^ partners[first + i]] = mixed[i * rows : (i + 1) * rows]


def attention_kernel(q_ref, k_ref, v_ref, out_ref):
    out_ref[...] = attend(q_ref[...], k_ref[...], v_ref[...])


def cross_kernel(head_count, o_ref, q_ref, *refs):
    *pair_refs, out_ref = refs
    rows = q_ref.shape[0]
    for head in range(head_count):
        lanes = slice(head * HEAD, (head + 1) * HEAD)
        o_self = o_ref[head].astype(jnp.float32)
        query = (q_ref[:, lanes].astype(jnp.float32) + o_self).astype(jnp.bfloat16).astype(jnp.float32)
        scores = [
            jnp.sum(query * ref[0:rows, lanes].astype(jnp.float32), axis=-1, keepdims=True)
            for ref in pair_refs
        ]
        top = functools.reduce(jnp.maximum, scores)
        weights = [jnp.exp2((score - top) * EXP2_SCALE) for score in scores]
        inverse = 1.0 / sum(weights[1:], weights[0])
        mixed = None
        for weight, ref in zip(weights, pair_refs):
            rounded = (weight * inverse).astype(jnp.bfloat16).astype(jnp.float32)
            term = rounded * ref[rows : 2 * rows, lanes].astype(jnp.float32)
            mixed = term if mixed is None else mixed + term
        o_cross = mixed.astype(jnp.bfloat16).astype(jnp.float32)
        out_ref[:, lanes] = (o_self + o_cross).astype(jnp.bfloat16)


def kernel_params(grant=32):
    return pltpu.CompilerParams(vmem_limit_bytes=grant * MIB)


def swap(array, axis_name, axis_size, partner):
    return lax.ppermute(array, axis_name, [(i, i ^ partner) for i in range(axis_size)])


def gather_views(array, view_count, *after):
    gathered = [array]
    step = view_count // 2
    for earlier in after:
        gathered, _ = lax.optimization_barrier((gathered, earlier))
        gathered += [swap(block, "view", view_count, step) for block in gathered]
        step //= 2
    return gathered


def split_attention(q, k, v, k_cross, v_cross, ctx_size):
    rows, width = q.shape
    heads = width // HEAD
    partners = (3, 7, 6, 2, 5, 4, 1, 0)
    vmem = pl.BlockSpec(memory_space=pltpu.VMEM)
    hbm = pl.BlockSpec(memory_space=pltpu.HBM)
    sources = [pltpu.with_memory_space_constraint(x, pltpu.HBM) for x in (q, k, v, k_cross, v_cross)]
    block = jax.ShapeDtypeStruct((3 * rows, HEAD), q.dtype)
    *blocks, pair = pl.pallas_call(
        functools.partial(pack_kernel, partners),
        out_shape=[block] * heads + [jax.ShapeDtypeStruct((2 * rows, width), q.dtype)],
        in_specs=[hbm] * 5,
        out_specs=[vmem] * (heads + 1),
        scratch_shapes=[pltpu.SemaphoreType.DMA((3 * heads + 2,))],
        compiler_params=kernel_params(),
        name="pack_qkv",
    )(*sources)
    moved = [
        swap(data, "ctx", ctx_size, partner) if partner else data
        for partner, data in zip(partners, blocks)
    ]
    own = pl.pallas_call(
        functools.partial(packed_attention_kernel, partners, rows, max(heads // 2, 1)),
        out_shape=jax.ShapeDtypeStruct((heads, rows, HEAD), q.dtype),
        in_specs=[vmem] * heads,
        out_specs=vmem,
        compiler_params=kernel_params(),
        cost_estimate=pl.CostEstimate(
            flops=4 * rows * rows * heads * heads * HEAD,
            bytes_accessed=8 * rows * heads * HEAD,
            transcendentals=rows * rows * heads * heads,
        ),
        name="self_attention",
    )(*moved)
    back = lax.all_to_all(own, "ctx", split_axis=0, concat_axis=0, tiled=True)
    return back, pair, (pair, moved[:3])


def shared_attention(q, k, v, ctx_size):
    rows, width = q.shape
    heads = width // HEAD
    parts = ctx_size // heads
    piece = rows // parts
    query = jnp.transpose(q.reshape(parts, piece, heads, HEAD), (2, 0, 1, 3)).reshape(
        ctx_size, piece, HEAD
    )
    key = jnp.repeat(jnp.transpose(k.reshape(rows, heads, HEAD), (1, 0, 2)), parts, axis=0)
    value = jnp.repeat(jnp.transpose(v.reshape(rows, heads, HEAD), (1, 0, 2)), parts, axis=0)
    packed = jnp.concatenate([query, key, value], axis=1)
    moved = lax.all_to_all(packed, "ctx", split_axis=0, concat_axis=0, tiled=True)
    query = moved[:, :piece].reshape(ctx_size * piece, HEAD)
    key = moved[:, piece : piece + rows].reshape(ctx_size * rows, HEAD)
    value = moved[:, piece + rows :].reshape(ctx_size * rows, HEAD)
    own = pl.pallas_call(
        attention_kernel,
        out_shape=jax.ShapeDtypeStruct((ctx_size * piece, HEAD), q.dtype),
        grid=(ctx_size * piece // rows,),
        in_specs=[
            pl.BlockSpec((rows, HEAD), lambda i: (i, 0)),
            pl.BlockSpec((ctx_size * rows, HEAD), lambda i: (0, 0)),
            pl.BlockSpec((ctx_size * rows, HEAD), lambda i: (0, 0)),
        ],
        out_specs=pl.BlockSpec((rows, HEAD), lambda i: (i, 0)),
        compiler_params=kernel_params(),
        name="self_attention",
    )(query, key, value)
    back = lax.all_to_all(
        own.reshape(ctx_size, piece, HEAD), "ctx", split_axis=0, concat_axis=0, tiled=True
    )
    return back.reshape(heads, rows, HEAD)


def body(view_count, ctx_size, q_self, k_self, v_self, q_cross, k_cross, v_cross):
    _, rows, width = q_self.shape
    heads = width // HEAD
    if ctx_size == heads == 8:
        o_self, pair, after = split_attention(
            q_self[0], k_self[0], v_self[0], k_cross[0], v_cross[0], ctx_size
        )
    else:
        o_self = shared_attention(q_self[0], k_self[0], v_self[0], ctx_size)
        pair = jnp.concatenate([k_cross[0], v_cross[0]], axis=0)
        after = [pair] * (view_count.bit_length() - 1)
    pairs = gather_views(pair, view_count, *after)
    vmem = pl.BlockSpec(memory_space=pltpu.VMEM)
    out = pl.pallas_call(
        functools.partial(cross_kernel, heads),
        out_shape=jax.ShapeDtypeStruct((rows, width), q_self.dtype),
        in_specs=[vmem] * (2 + view_count),
        out_specs=vmem,
        compiler_params=kernel_params(),
        name="cross_view",
    )(o_self, q_cross[0], *pairs)
    return out[None]


def solution(mesh):
    spec = P("view", "ctx", None)
    return jax.shard_map(
        functools.partial(body, mesh.shape["view"], mesh.shape["ctx"]),
        mesh=mesh,
        in_specs=(spec,) * 6,
        out_specs=spec,
        check_vma=False,
    )
```

```python
import functools
import math

import jax
import jax.numpy as jnp
from jax import lax
from jax.experimental import pallas as pl
from jax.experimental.pallas import tpu as pltpu
from jax.sharding import PartitionSpec as P

HEAD = 128
SCALE = 1.0 / math.sqrt(HEAD)
EXP2_SCALE = SCALE * math.log2(math.e)
MIB = 1024 * 1024


def pack_kernel(partners, q_ref, k_ref, v_ref, kc_ref, vc_ref, *refs):
    block_refs, pair_ref, sems = refs[: len(partners)], refs[-2], refs[-1]
    rows = q_ref.shape[0]
    me = lax.axis_index("ctx")
    copies = []

    def start(source, target):
        copy = pltpu.make_async_copy(source, target, sems.at[len(copies)])
        copy.start()
        copies.append(copy)

    for partner, block_ref in zip(partners, block_refs):
        lanes = pl.ds(pl.multiple_of((me ^ partner) * HEAD, HEAD), HEAD)
        for part, source in enumerate((q_ref, k_ref, v_ref)):
            start(source.at[:, lanes], block_ref.at[pl.ds(part * rows, rows)])
    for part, source in enumerate((kc_ref, vc_ref)):
        start(source, pair_ref.at[pl.ds(part * rows, rows)])
    for copy in copies:
        copy.wait()


def attend(query, keys, values):
    scores = lax.dot_general(
        query, keys, (((1,), (1,)), ((), ())), preferred_element_type=jnp.float32
    )
    row_max = jnp.max(scores, axis=-1, keepdims=True)
    weights_raw = jnp.exp2((scores - row_max) * EXP2_SCALE).astype(jnp.bfloat16)
    values_ones = jnp.concatenate([values, jnp.ones_like(values)], axis=1)
    mixed = jnp.dot(weights_raw, values_ones, preferred_element_type=jnp.float32)
    return (mixed[:, :HEAD] / mixed[:, HEAD:]).astype(jnp.bfloat16)


def packed_attention_kernel(partners, rows, group, *refs):
    *in_refs, out_ref = refs
    me = lax.axis_index("ctx")
    keys = jnp.concatenate([ref[rows : 2 * rows] for ref in in_refs], axis=0)
    values = jnp.concatenate([ref[2 * rows : 3 * rows] for ref in in_refs], axis=0)
    for first in range(0, len(in_refs), group):
        query = jnp.concatenate([ref[0:rows] for ref in in_refs[first : first + group]], axis=0)
        mixed = attend(query, keys, values)
        for i in range(group):
            out_ref[me ^ partners[first + i]] = mixed[i * rows : (i + 1) * rows]


def attention_kernel(q_ref, k_ref, v_ref, out_ref):
    out_ref[...] = attend(q_ref[...], k_ref[...], v_ref[...])


def cross_kernel(head_count, o_ref, q_ref, *refs):
    *pair_refs, out_hbm_ref, out_ref, sems = refs
    copies = []
    rows = q_ref.shape[0]
    for head in range(head_count):
        lanes = slice(head * HEAD, (head + 1) * HEAD)
        o_self = o_ref[head].astype(jnp.float32)
        query = (q_ref[:, lanes].astype(jnp.float32) + o_self).astype(jnp.bfloat16).astype(jnp.float32)
        scores = [
            jnp.sum(query * ref[0:rows, lanes].astype(jnp.float32), axis=-1, keepdims=True)
            for ref in pair_refs
        ]
        top = functools.reduce(jnp.maximum, scores)
        weights = [jnp.exp2((score - top) * EXP2_SCALE) for score in scores]
        inverse = 1.0 / sum(weights[1:], weights[0])
        mixed = None
        for weight, ref in zip(weights, pair_refs):
            rounded = (weight * inverse).astype(jnp.bfloat16).astype(jnp.float32)
            term = rounded * ref[rows : 2 * rows, lanes].astype(jnp.float32)
            mixed = term if mixed is None else mixed + term
        o_cross = mixed.astype(jnp.bfloat16).astype(jnp.float32)
        out_ref[:, lanes] = (o_self + o_cross).astype(jnp.bfloat16)
        if head % 2:
            done = pl.ds((head - 1) * HEAD, 2 * HEAD)
            copies.append(
                pltpu.make_async_copy(out_ref.at[:, done], out_hbm_ref.at[:, done], sems.at[head // 2])
            )
            copies[-1].start()
    for copy in copies:
        copy.wait()


def kernel_params(grant=32):
    return pltpu.CompilerParams(vmem_limit_bytes=grant * MIB)


def swap(array, axis_name, axis_size, partner):
    return lax.ppermute(array, axis_name, [(i, i ^ partner) for i in range(axis_size)])


def gather_views(array, view_count, *after):
    gathered = [array]
    step = view_count // 2
    for earlier in after:
        gathered, _ = lax.optimization_barrier((gathered, earlier))
        gathered += [swap(block, "view", view_count, step) for block in gathered]
        step //= 2
    return gathered


def split_attention(q, k, v, k_cross, v_cross, ctx_size):
    rows, width = q.shape
    heads = width // HEAD
    partners = (3, 7, 6, 2, 5, 4, 1, 0)
    vmem = pl.BlockSpec(memory_space=pltpu.VMEM)
    hbm = pl.BlockSpec(memory_space=pltpu.HBM)
    sources = [pltpu.with_memory_space_constraint(x, pltpu.HBM) for x in (q, k, v, k_cross, v_cross)]
    block = jax.ShapeDtypeStruct((3 * rows, HEAD), q.dtype)
    *blocks, pair = pl.pallas_call(
        functools.partial(pack_kernel, partners),
        out_shape=[block] * heads + [jax.ShapeDtypeStruct((2 * rows, width), q.dtype)],
        in_specs=[hbm] * 5,
        out_specs=[vmem] * (heads + 1),
        scratch_shapes=[pltpu.SemaphoreType.DMA((3 * heads + 2,))],
        compiler_params=kernel_params(),
        name="pack_qkv",
    )(*sources)
    moved = [
        swap(data, "ctx", ctx_size, partner) if partner else data
        for partner, data in zip(partners, blocks)
    ]
    own = pl.pallas_call(
        functools.partial(packed_attention_kernel, partners, rows, max(heads // 2, 1)),
        out_shape=jax.ShapeDtypeStruct((heads, rows, HEAD), q.dtype),
        in_specs=[vmem] * heads,
        out_specs=vmem,
        compiler_params=kernel_params(),
        cost_estimate=pl.CostEstimate(
            flops=4 * rows * rows * heads * heads * HEAD,
            bytes_accessed=8 * rows * heads * HEAD,
            transcendentals=rows * rows * heads * heads,
        ),
        name="self_attention",
    )(*moved)
    back = lax.all_to_all(own, "ctx", split_axis=0, concat_axis=0, tiled=True)
    return back, pair, (pair, moved[:4])


def shared_attention(q, k, v, ctx_size):
    rows, width = q.shape
    heads = width // HEAD
    parts = ctx_size // heads
    piece = rows // parts
    query = jnp.transpose(q.reshape(parts, piece, heads, HEAD), (2, 0, 1, 3)).reshape(
        ctx_size, piece, HEAD
    )
    key = jnp.repeat(jnp.transpose(k.reshape(rows, heads, HEAD), (1, 0, 2)), parts, axis=0)
    value = jnp.repeat(jnp.transpose(v.reshape(rows, heads, HEAD), (1, 0, 2)), parts, axis=0)
    packed = jnp.concatenate([query, key, value], axis=1)
    moved = lax.all_to_all(packed, "ctx", split_axis=0, concat_axis=0, tiled=True)
    query = moved[:, :piece].reshape(ctx_size * piece, HEAD)
    key = moved[:, piece : piece + rows].reshape(ctx_size * rows, HEAD)
    value = moved[:, piece + rows :].reshape(ctx_size * rows, HEAD)
    own = pl.pallas_call(
        attention_kernel,
        out_shape=jax.ShapeDtypeStruct((ctx_size * piece, HEAD), q.dtype),
        grid=(ctx_size * piece // rows,),
        in_specs=[
            pl.BlockSpec((rows, HEAD), lambda i: (i, 0)),
            pl.BlockSpec((ctx_size * rows, HEAD), lambda i: (0, 0)),
            pl.BlockSpec((ctx_size * rows, HEAD), lambda i: (0, 0)),
        ],
        out_specs=pl.BlockSpec((rows, HEAD), lambda i: (i, 0)),
        compiler_params=kernel_params(),
        name="self_attention",
    )(query, key, value)
    back = lax.all_to_all(
        own.reshape(ctx_size, piece, HEAD), "ctx", split_axis=0, concat_axis=0, tiled=True
    )
    return back.reshape(heads, rows, HEAD)


def body(view_count, ctx_size, q_self, k_self, v_self, q_cross, k_cross, v_cross):
    _, rows, width = q_self.shape
    heads = width // HEAD
    if ctx_size == heads == 8:
        o_self, pair, after = split_attention(
            q_self[0], k_self[0], v_self[0], k_cross[0], v_cross[0], ctx_size
        )
    else:
        o_self = shared_attention(q_self[0], k_self[0], v_self[0], ctx_size)
        pair = jnp.concatenate([k_cross[0], v_cross[0]], axis=0)
        after = [pair] * (view_count.bit_length() - 1)
    pairs = gather_views(pair, view_count, *after)
    vmem = pl.BlockSpec(memory_space=pltpu.VMEM)
    out = pl.pallas_call(
        functools.partial(cross_kernel, heads),
        out_shape=jax.ShapeDtypeStruct((rows, width), q_self.dtype),
        in_specs=[vmem] * (2 + view_count),
        out_specs=pl.BlockSpec(memory_space=pl.ANY),
        scratch_shapes=[
            pltpu.VMEM((rows, width), q_self.dtype),
            pltpu.SemaphoreType.DMA((heads // 2,)),
        ],
        compiler_params=kernel_params(),
        name="cross_view",
    )(o_self, q_cross[0], *pairs)
    return out[None]


def solution(mesh):
    spec = P("view", "ctx", None)
    return jax.shard_map(
        functools.partial(body, mesh.shape["view"], mesh.shape["ctx"]),
        mesh=mesh,
        in_specs=(spec,) * 6,
        out_specs=spec,
        check_vma=False,
    )
```

```python
import functools
import math

import jax
import jax.numpy as jnp
from jax import lax
from jax.experimental import pallas as pl
from jax.experimental.pallas import tpu as pltpu
from jax.sharding import PartitionSpec as P

HEAD = 128
SCALE = 1.0 / math.sqrt(HEAD)
EXP2_SCALE = SCALE * math.log2(math.e)
MIB = 1024 * 1024


def pack_kernel(partners, q_ref, k_ref, v_ref, kc_ref, vc_ref, *refs):
    block_refs, pair_ref, sems = refs[: len(partners)], refs[-2], refs[-1]
    rows = q_ref.shape[0]
    me = lax.axis_index("ctx")
    copies = []

    def start(source, target):
        copy = pltpu.make_async_copy(source, target, sems.at[len(copies)])
        copy.start()
        copies.append(copy)

    for partner, block_ref in zip(partners, block_refs):
        lanes = pl.ds(pl.multiple_of((me ^ partner) * HEAD, HEAD), HEAD)
        for part, source in enumerate((q_ref, k_ref, v_ref)):
            start(source.at[:, lanes], block_ref.at[pl.ds(part * rows, rows)])
    for part, source in enumerate((kc_ref, vc_ref)):
        start(source, pair_ref.at[pl.ds(part * rows, rows)])
    for copy in copies:
        copy.wait()


def attend(query, keys, values):
    scores = lax.dot_general(
        query, keys, (((1,), (1,)), ((), ())), preferred_element_type=jnp.float32
    )
    row_max = jnp.max(scores, axis=-1, keepdims=True)
    weights_raw = jnp.exp2((scores - row_max) * EXP2_SCALE).astype(jnp.bfloat16)
    values_ones = jnp.concatenate([values, jnp.ones_like(values)], axis=1)
    mixed = jnp.dot(weights_raw, values_ones, preferred_element_type=jnp.float32)
    return (mixed[:, :HEAD] / mixed[:, HEAD:]).astype(jnp.bfloat16)


def packed_attention_kernel(partners, rows, group, *refs):
    *in_refs, out_ref = refs
    me = lax.axis_index("ctx")
    keys = jnp.concatenate([ref[rows : 2 * rows] for ref in in_refs], axis=0)
    values = jnp.concatenate([ref[2 * rows : 3 * rows] for ref in in_refs], axis=0)
    for first in range(0, len(in_refs), group):
        query = jnp.concatenate([ref[0:rows] for ref in in_refs[first : first + group]], axis=0)
        mixed = attend(query, keys, values)
        for i in range(min(group, len(in_refs) - first)):
            out_ref[me ^ partners[first + i]] = mixed[i * rows : (i + 1) * rows]


def attention_kernel(q_ref, k_ref, v_ref, out_ref):
    out_ref[...] = attend(q_ref[...], k_ref[...], v_ref[...])


def cross_kernel(head_count, o_ref, q_ref, *refs):
    *pair_refs, out_ref = refs
    rows = q_ref.shape[0]
    for head in range(head_count):
        lanes = slice(head * HEAD, (head + 1) * HEAD)
        o_self = o_ref[head].astype(jnp.float32)
        query = (q_ref[:, lanes].astype(jnp.float32) + o_self).astype(jnp.bfloat16).astype(jnp.float32)
        scores = [
            jnp.sum(query * ref[0:rows, lanes].astype(jnp.float32), axis=-1, keepdims=True)
            for ref in pair_refs
        ]
        top = functools.reduce(jnp.maximum, scores)
        weights = [jnp.exp2((score - top) * EXP2_SCALE) for score in scores]
        inverse = 1.0 / sum(weights[1:], weights[0])
        mixed = None
        for weight, ref in zip(weights, pair_refs):
            rounded = (weight * inverse).astype(jnp.bfloat16).astype(jnp.float32)
            term = rounded * ref[rows : 2 * rows, lanes].astype(jnp.float32)
            mixed = term if mixed is None else mixed + term
        o_cross = mixed.astype(jnp.bfloat16).astype(jnp.float32)
        out_ref[:, lanes] = (o_self + o_cross).astype(jnp.bfloat16)


def kernel_params(grant=32):
    return pltpu.CompilerParams(vmem_limit_bytes=grant * MIB)


def swap(array, axis_name, axis_size, partner):
    return lax.ppermute(array, axis_name, [(i, i ^ partner) for i in range(axis_size)])


def gather_views(array, view_count, *after):
    gathered = [array]
    step = view_count // 2
    for earlier in after:
        gathered, _ = lax.optimization_barrier((gathered, earlier))
        gathered += [swap(block, "view", view_count, step) for block in gathered]
        step //= 2
    return gathered


def split_attention(q, k, v, k_cross, v_cross, ctx_size):
    rows, width = q.shape
    heads = width // HEAD
    partners = (3, 7, 6, 2, 5, 4, 1, 0)
    vmem = pl.BlockSpec(memory_space=pltpu.VMEM)
    hbm = pl.BlockSpec(memory_space=pltpu.HBM)
    sources = [pltpu.with_memory_space_constraint(x, pltpu.HBM) for x in (q, k, v, k_cross, v_cross)]
    block = jax.ShapeDtypeStruct((3 * rows, HEAD), q.dtype)
    *blocks, pair = pl.pallas_call(
        functools.partial(pack_kernel, partners),
        out_shape=[block] * heads + [jax.ShapeDtypeStruct((2 * rows, width), q.dtype)],
        in_specs=[hbm] * 5,
        out_specs=[vmem] * (heads + 1),
        scratch_shapes=[pltpu.SemaphoreType.DMA((3 * heads + 2,))],
        compiler_params=kernel_params(),
        name="pack_qkv",
    )(*sources)
    moved = [
        swap(data, "ctx", ctx_size, partner) if partner else data
        for partner, data in zip(partners, blocks)
    ]
    own = pl.pallas_call(
        functools.partial(packed_attention_kernel, partners, rows, (heads + 2) // 3),
        out_shape=jax.ShapeDtypeStruct((heads, rows, HEAD), q.dtype),
        in_specs=[vmem] * heads,
        out_specs=vmem,
        compiler_params=kernel_params(),
        cost_estimate=pl.CostEstimate(
            flops=4 * rows * rows * heads * heads * HEAD,
            bytes_accessed=8 * rows * heads * HEAD,
            transcendentals=rows * rows * heads * heads,
        ),
        name="self_attention",
    )(*moved)
    back = lax.all_to_all(own, "ctx", split_axis=0, concat_axis=0, tiled=True)
    return back, pair, (pair, moved[:4])


def shared_attention(q, k, v, ctx_size):
    rows, width = q.shape
    heads = width // HEAD
    parts = ctx_size // heads
    piece = rows // parts
    query = jnp.transpose(q.reshape(parts, piece, heads, HEAD), (2, 0, 1, 3)).reshape(
        ctx_size, piece, HEAD
    )
    key = jnp.repeat(jnp.transpose(k.reshape(rows, heads, HEAD), (1, 0, 2)), parts, axis=0)
    value = jnp.repeat(jnp.transpose(v.reshape(rows, heads, HEAD), (1, 0, 2)), parts, axis=0)
    packed = jnp.concatenate([query, key, value], axis=1)
    moved = lax.all_to_all(packed, "ctx", split_axis=0, concat_axis=0, tiled=True)
    query = moved[:, :piece].reshape(ctx_size * piece, HEAD)
    key = moved[:, piece : piece + rows].reshape(ctx_size * rows, HEAD)
    value = moved[:, piece + rows :].reshape(ctx_size * rows, HEAD)
    own = pl.pallas_call(
        attention_kernel,
        out_shape=jax.ShapeDtypeStruct((ctx_size * piece, HEAD), q.dtype),
        grid=(ctx_size * piece // rows,),
        in_specs=[
            pl.BlockSpec((rows, HEAD), lambda i: (i, 0)),
            pl.BlockSpec((ctx_size * rows, HEAD), lambda i: (0, 0)),
            pl.BlockSpec((ctx_size * rows, HEAD), lambda i: (0, 0)),
        ],
        out_specs=pl.BlockSpec((rows, HEAD), lambda i: (i, 0)),
        compiler_params=kernel_params(),
        name="self_attention",
    )(query, key, value)
    back = lax.all_to_all(
        own.reshape(ctx_size, piece, HEAD), "ctx", split_axis=0, concat_axis=0, tiled=True
    )
    return back.reshape(heads, rows, HEAD)


def body(view_count, ctx_size, q_self, k_self, v_self, q_cross, k_cross, v_cross):
    _, rows, width = q_self.shape
    heads = width // HEAD
    if ctx_size == heads == 8:
        o_self, pair, after = split_attention(
            q_self[0], k_self[0], v_self[0], k_cross[0], v_cross[0], ctx_size
        )
    else:
        o_self = shared_attention(q_self[0], k_self[0], v_self[0], ctx_size)
        pair = jnp.concatenate([k_cross[0], v_cross[0]], axis=0)
        after = [pair] * (view_count.bit_length() - 1)
    pairs = gather_views(pair, view_count, *after)
    vmem = pl.BlockSpec(memory_space=pltpu.VMEM)
    out = pl.pallas_call(
        functools.partial(cross_kernel, heads),
        out_shape=jax.ShapeDtypeStruct((rows, width), q_self.dtype),
        in_specs=[vmem] * (2 + view_count),
        out_specs=vmem,
        compiler_params=kernel_params(),
        name="cross_view",
    )(o_self, q_cross[0], *pairs)
    return out[None]


def solution(mesh):
    spec = P("view", "ctx", None)
    return jax.shard_map(
        functools.partial(body, mesh.shape["view"], mesh.shape["ctx"]),
        mesh=mesh,
        in_specs=(spec,) * 6,
        out_specs=spec,
        check_vma=False,
    )
```
